32 devices in a mesh: clip: 8 (over z, core), seq: 4 (over y, x).
Axes of the slice: x: 2, y: 2, z: 4, core: 2. Of those that a mesh axis runs over, the one named last changes fastest.
Arguments:
- video_latents: bfloat16 [8, 16, 256, 1152], P('clip', 'seq'), may hold values from -6 to 6
- conditioning: float32 [8, 1152], P('clip'), may hold values from -6 to 6
- ada_weight: bfloat16 [2, 1152, 6912], P(None, None, ('clip', 'seq')), may hold values from -0.1875 to 0.1875
- ada_bias: float32 [2, 6912], P(None, ('clip', 'seq')), may hold values from -3 to 3
- qkv_weight: bfloat16 [2, 1152, 3456], P(None, 'clip', 'seq'), may hold values from -1 to 1
- out_weight: bfloat16 [2, 1152, 1152], P(None, 'clip', 'seq'), may hold values from -0.75 to 0.75
- up_weight: bfloat16 [2, 1152, 4608], P(None, 'clip', 'seq'), may hold values from -0.1875 to 0.1875
- down_weight: bfloat16 [2, 4608, 1152], P(None, 'clip', 'seq'), may hold values from -0.09375 to 0.09375
- attention_bias: float32 [2, 3, 1152], replicated, may hold values from -3 to 3
- up_bias: float32 [2, 4608], replicated, may hold values from -3 to 3
- down_bias: float32 [2, 1152], replicated, may hold values from -3 to 3
- cotangent: bfloat16 [8, 16, 256, 1152], P('clip', 'seq'), may hold values from -6 to 6
Outputs:
- output_latents: bfloat16 [8, 16, 256, 1152], P('clip', 'seq')
- latents_grad: float32 [8, 16, 256, 1152], P('clip', 'seq')
- conditioning_grad: float32 [8, 1152], P('clip')
- ada_weight_grad: float32 [2, 1152, 6912], P(None, None, ('clip', 'seq'))
- ada_bias_grad: float32 [2, 6912], P(None, ('clip', 'seq'))
- qkv_weight_grad: float32 [2, 1152, 3456], P(None, 'clip', 'seq')
- out_weight_grad: float32 [2, 1152, 1152], P(None, 'clip', 'seq')
- up_weight_grad: float32 [2, 1152, 4608], P(None, 'clip', 'seq')
- down_weight_grad: float32 [2, 4608, 1152], P(None, 'clip', 'seq')
- attention_bias_grad: float32 [2, 3, 1152], replicated
- up_bias_grad: float32 [2, 4608], replicated
- down_bias_grad: float32 [2, 1152], replicated
- clipped_qkv: float32 [2, 1152, 3456], P(None, 'clip', 'seq')
- logit_peak: float32 [2, 16], replicated
The draws below stay inside these ranges and needn't reach their ends.
All inputs are finite; a program needn't handle non-finite values.
Results may differ from the reference program's by a relative error of at most 0.023.
Values may be sent and summed in bfloat16 or wider, within the bound.
No kernel may reach another device: no remote copies, remote signals or barrier semaphores. Data moves between devices by JAX's collectives and lax.ppermute only.
A program may use at most 512 MiB of HBM per device.

```python
import math
import jax
import jax.numpy as jnp
from jax import lax

D = 1152
HEADS = 16
FF = 4608
FRAMES = 16
PLACES = 256
LAYERS = 2
CLIPS = 8


def draw_qkv_weight(key, part):
    key = jax.random.fold_in(key, 7)
    entry_key, gain_key = jax.random.split(key)
    entries = jax.random.normal(entry_key, (LAYERS, D, 3 * D), jnp.float32) * D ** (-0.5)
    log_gain = jax.random.uniform(gain_key, (LAYERS, 2, HEADS), jnp.float32, math.log(0.7), math.log(1.4))
    head_gain = jnp.repeat(jnp.exp(log_gain), D // HEADS, axis=2).reshape(LAYERS, 2 * D)
    column_gain = jnp.concatenate([head_gain, jnp.ones((LAYERS, D), jnp.float32)], axis=1)
    return jnp.clip(entries * column_gain[:, None, :], -1.0, 1.0).astype(jnp.bfloat16)


def steps_of(own_key, dims, cuts, smallest, largest):
    gain, own = 1.0, jax.random.fold_in(own_key, 6)
    for dim, shards_of in cuts:
        heights = jnp.exp(jax.random.uniform(jax.random.fold_in(own, dim), (shards_of,), jnp.float32, smallest / len(cuts), largest / len(cuts)))
        gain = gain * jnp.repeat(heights, dims[dim] // shards_of).reshape([-1 if axis == dim else 1 for axis in range(len(dims))])
    return gain


def gaussian(own_key, extent, deviation, limit, shards=(), held_as=jnp.bfloat16):
    factor_of = steps_of(own_key, extent, shards, -0.22, 0.18) if shards else 1.0
    array = jax.random.normal(own_key, extent, jnp.float32) * deviation * factor_of
    return jnp.minimum(jnp.maximum(array, -limit), limit).astype(held_as)


def setup_inputs(seed: int = 0) -> dict:
    splits = jax.random.split(jax.random.key(seed), 13)
    return {
        "video_latents": gaussian(splits[0], (CLIPS, FRAMES, PLACES, D), 1.0, 6.0, ((0, 8), (1, 4))),
        "conditioning": gaussian(splits[1], (CLIPS, D), 1.0, 6.0, ((0, 8),), jnp.float32),
        "ada_weight": gaussian(splits[2], (LAYERS, D, 6 * D), D ** -0.5, 0.1875, ((2, 32),)),
        "ada_bias": gaussian(splits[3], (LAYERS, 6 * D), 0.5, 3.0, ((1, 32),), jnp.float32),
        "qkv_weight": draw_qkv_weight(jax.random.fold_in(splits[12], 71), 0),
        "out_weight": gaussian(splits[5], (LAYERS, D, D), (D // 16) ** -0.5, 0.75, ((1, 8), (2, 4))),
        "up_weight": gaussian(splits[6], (LAYERS, D, FF), D ** -0.5, 0.1875, ((1, 8), (2, 4))),
        "down_weight": gaussian(splits[7], (LAYERS, FF, D), FF ** -0.5, 0.09375, ((1, 8), (2, 4))),
        "attention_bias": gaussian(splits[8], (LAYERS, 3, D), 0.5, 3.0, (), jnp.float32),
        "up_bias": gaussian(splits[9], (LAYERS, FF), 0.5, 3.0, (), jnp.float32),
        "down_bias": gaussian(splits[10], (LAYERS, D), 0.5, 3.0, (), jnp.float32),
        "cotangent": gaussian(splits[11], (CLIPS, FRAMES, PLACES, D), 1.0, 6.0, ((0, 8), (1, 4))),
    }


@jax.custom_vjp
def low(v):
    return lax.optimization_barrier(v.astype(jnp.bfloat16)).astype(jnp.float32)

@jax.custom_vjp
def low_back(v):
    return v

def low_keep(v):
    return (low(v), None)

def low_pass(kept, grad):
    return (grad,)

def back_keep(v):
    return (v, None)

def back_low(kept, grad):
    return (low(grad),)
low.defvjp(low_keep, low_pass)
low_back.defvjp(back_keep, back_low)
clip_limit = 8.0
spatial_forms = ('cabhe,cakhe->cahbk', 'cahbk,cakhe->cabhe', 'cahbk,cabhe->cakhe')
temporal_forms = ('cabhe,ckbhe->cbhak', 'cbhak,ckbhe->cabhe', 'cbhak,cabhe->ckbhe')
highest = lax.Precision.HIGHEST

def normalize(stream):
    centred = stream - lax.optimization_barrier(jnp.mean(stream, axis=-1, keepdims=True))
    return centred * lax.rsqrt(lax.optimization_barrier(jnp.mean(centred * centred, axis=-1, keepdims=True)) + 1e-06)

def ref_layer(stream, modulation, qkv_full, out_full, up_full, down_full, attention_b, up_b, down_b, forms):
    model_width = stream.shape[-1]
    token_shape = stream.shape[:-1]
    pieces = [modulation[:, None, None, slot * model_width:(slot + 1) * model_width] for slot in range(6)]
    hidden = low(normalize(stream) * (1.0 + pieces[1]) + pieces[0])
    qkv_bias = jnp.concatenate([attention_b[0], jnp.zeros_like(attention_b[0]), attention_b[1]])
    projected = jnp.einsum('cabd,de->cabe', hidden, qkv_full, precision=highest) + qkv_bias
    heads_shape = token_shape + (HEADS, model_width // HEADS)
    query_heads = low_back(low(projected[..., :model_width])).reshape(heads_shape)
    key_heads = low_back(low(projected[..., model_width:2 * model_width])).reshape(heads_shape)
    value_heads = low_back(low(projected[..., 2 * model_width:])).reshape(heads_shape)
    score_scale = (model_width // HEADS) ** (-0.5)
    scores = low_back(score_scale * jnp.einsum(forms[0], query_heads, key_heads, precision=highest))
    head_peak = lax.optimization_barrier(jnp.max(scores, axis=(0, 1, 3, 4)))
    row_top = lax.optimization_barrier(jnp.max(scores, axis=-1, keepdims=True))
    exponent = jnp.exp(scores - row_top)
    probs = exponent / lax.optimization_barrier(jnp.sum(exponent, axis=-1, keepdims=True))
    attended = jnp.einsum(forms[1], low(probs), value_heads, precision=highest)
    attended = low_back(low(attended.reshape(token_shape + (model_width,))))
    branch = low_back(jnp.einsum('cabd,de->cabe', attended, out_full, precision=highest) + attention_b[2])
    middle = stream + pieces[2] * branch
    hidden_two = low(normalize(middle) * (1.0 + pieces[4]) + pieces[3])
    inner_pre = low_back(jnp.einsum('cabd,df->cabf', hidden_two, up_full, precision=highest) + up_b)
    active = low(jax.nn.gelu(inner_pre, approximate=True))
    update = low_back(jnp.einsum('cabf,fd->cabd', active, down_full, precision=highest) + down_b)
    return (middle + pieces[5] * update, head_peak)

def forward(video_clip, condition_row, ada_w, ada_b, qkv_w, out_w, up_w, down_w, attention_b, up_b, down_b):
    squashed = low(jax.nn.silu(condition_row))[None, :]
    stream = video_clip[None]
    peaks = []
    for layer in range(LAYERS):
        modulation = low_back(jnp.dot(squashed, ada_w[layer], precision=highest)) + ada_b[layer][None, :]
        forms = spatial_forms if layer % 2 == 0 else temporal_forms
        stream, head_peak = ref_layer(stream, modulation, qkv_w[layer], out_w[layer], up_w[layer], down_w[layer], attention_b[layer], up_b[layer], down_b[layer], forms)
        if layer + 1 < LAYERS:
            stream = low_back(low(stream))
        peaks.append(head_peak)
    return (stream[0], jnp.stack(peaks))

def reference(video_latents, conditioning, ada_weight, ada_bias, qkv_weight, out_weight, up_weight, down_weight, attention_bias, up_bias, down_bias, cotangent):
    params = tuple((item.astype(jnp.float32) for item in (ada_weight, ada_bias, qkv_weight, out_weight, up_weight, down_weight, attention_bias, up_bias, down_bias)))

    def clip_step(totals, inputs):
        video_clip, condition_row, cotangent_clip = inputs
        result, pullback, head_peak = jax.vjp(forward, video_clip.astype(jnp.float32), condition_row, *params, has_aux=True)
        gradients = pullback(cotangent_clip.astype(jnp.float32))
        sums = tuple((total + grad for total, grad in zip(totals[0], gradients[2:])))
        return ((sums, jnp.maximum(totals[1], head_peak)), (result.astype(jnp.bfloat16), gradients[0], gradients[1]))
    start = (tuple((jnp.zeros_like(item) for item in params)), jnp.full((LAYERS, HEADS), -1e+30, jnp.float32))
    (sums, peaks), (output_latents, latents_grad, conditioning_grad) = lax.scan(clip_step, start, (video_latents, conditioning, cotangent))
    roots = jnp.sqrt(clip_limit / jnp.maximum(peaks, clip_limit))
    columns = jnp.arange(3 * D, dtype=jnp.int32)
    heads_of = columns % D // (D // HEADS)
    column_roots = jnp.where(columns[None, :] < 2 * D, roots[:, heads_of], 1.0)
    clipped_qkv = params[2] * column_roots[:, None, :]
    return (output_latents, latents_grad, conditioning_grad, sums[0], sums[1], sums[2], sums[3], sums[4], sums[5], sums[6], sums[7], sums[8], clipped_qkv, peaks)
```

```python
from functools import partial

import jax
import jax.numpy as jnp
from jax import lax
from jax.experimental import pallas as pl
from jax.experimental.pallas import tpu as pltpu
from jax.sharding import PartitionSpec as P

HEADS = 16
F32 = jnp.float32
BF16 = jnp.bfloat16
NN = (((1,), (0,)), ((), ()))
NT = (((1,), (1,)), ((), ()))
TN = (((0,), (0,)), ((), ()))
VMEM_BYTES = 56 * 1024 * 1024


def mm(a, b, dims=NN):
    return lax.dot_general(a, b, dims, preferred_element_type=F32)


def call(body, grid, in_specs, out_specs, out_shape, scratch=(), scalars=0, flops=0, nbytes=0):
    return pl.pallas_call(
        body,
        grid_spec=pltpu.PrefetchScalarGridSpec(
            num_scalar_prefetch=scalars,
            grid=grid,
            in_specs=in_specs,
            out_specs=out_specs,
            scratch_shapes=list(scratch),
        ),
        out_shape=out_shape,
        compiler_params=pltpu.CompilerParams(
            dimension_semantics=("arbitrary",) * len(grid), vmem_limit_bytes=VMEM_BYTES
        ),
        cost_estimate=pl.CostEstimate(flops=flops, bytes_accessed=nbytes, transcendentals=0),
    )


def whole(shape):
    return pl.BlockSpec(shape, lambda *_: (0,) * len(shape))


def sds(shape, dtype):
    return jax.ShapeDtypeStruct(shape, dtype)


def standard(x):
    centred = x - jnp.mean(x, axis=-1, keepdims=True)
    r = lax.rsqrt(jnp.mean(centred * centred, axis=-1, keepdims=True) + 1e-06)
    return centred * r, r


def fold(n, limit=512):
    return min(n, limit)


def qkv_forward(x, mods, w, bias):
    n, d = x.shape
    wide = w.shape[1]
    mt = fold(n)

    def body(x_ref, mod_ref, w_ref, b_ref, hid_ref, out_ref):
        m = pl.program_id(1)
        rows = pl.ds(pl.multiple_of(m * mt, mt), mt)

        @pl.when(pl.program_id(0) == 0)
        def _():
            v, _ = standard(x_ref[...].astype(F32))
            hid_ref[rows, :] = (v * (1.0 + mod_ref[1:2, :]) + mod_ref[0:1, :]).astype(BF16)

        out_ref[...] = (mm(hid_ref[rows, :], w_ref[...]) + b_ref[...]).astype(BF16)

    return call(
        body,
        (wide // d, n // mt),
        [
            pl.BlockSpec((mt, d), lambda j, m: (jnp.where(j == 0, m, n // mt - 1), 0)),
            whole((8, d)),
            pl.BlockSpec((d, d), lambda j, m: (0, j)),
            pl.BlockSpec((1, d), lambda j, m: (0, j)),
        ],
        [whole((n, d)), pl.BlockSpec((mt, d), lambda j, m: (m, j))],
        [sds((n, d), BF16), sds((n, wide), BF16)],
        flops=2 * n * d * wide,
        nbytes=2 * (d * wide + n * wide + 2 * n * d),
    )(x, mods, w, bias)


def window(h, size, d):
    lo = h * size
    start = lo // 128 * 128
    stop = min(-(-(lo + size) // 128) * 128, d)
    return start, stop, lo - start


def head_mask(start, stop, off, size, rows):
    lane = lax.broadcasted_iota(jnp.int32, (rows, stop - start), 1)
    return (lane >= off) & (lane < off + size)


def attention_forward(qkv, temporal):
    a, g, p, wide = qkv.shape
    d = wide // 3
    size = d // HEADS
    t = a * p
    scale = size ** (-0.5)

    def body(qkv_ref, att_ref, lse_ref, peak_ref, acc):
        acc[...] = jnp.zeros_like(acc)
        if temporal:
            qi = lax.broadcasted_iota(jnp.int32, (t, t), 0)
            ki = lax.broadcasted_iota(jnp.int32, (t, t), 1)
            same = lax.rem(qi, p) == lax.rem(ki, p)
        tops, totals = [], []
        for h in range(HEADS):
            lo, hi, off = window(h, size, d)
            keep = head_mask(lo, hi, off, size, t)
            q = qkv_ref[:, 0, :, lo:hi].reshape(t, hi - lo)
            k = qkv_ref[:, 0, :, d + lo : d + hi].reshape(t, hi - lo)
            v = qkv_ref[:, 0, :, 2 * d + lo : 2 * d + hi].reshape(t, hi - lo)
            zero = jnp.zeros_like(q)
            s = mm(jnp.where(keep, q, zero), k, NT) * scale
            if temporal:
                s = jnp.where(same, s, -1e30)
            top = jnp.max(s, axis=-1, keepdims=True)
            e = jnp.exp(s - top)
            total = jnp.sum(e, axis=-1, keepdims=True)
            probs = (e / total).astype(BF16)
            acc[:, lo:hi] += mm(probs, jnp.where(keep, v, zero))
            tops.append(top)
            totals.append(total)
        top = jnp.concatenate(tops, axis=1)
        lse_ref[0] = (top + jnp.log(jnp.concatenate(totals, axis=1))).T
        peak_ref[...] = jnp.max(top, axis=0, keepdims=True)[None]
        att_ref[...] = acc[...].astype(BF16).reshape(a, 1, p, d)

    return call(
        body,
        (g,),
        [pl.BlockSpec((a, 1, p, wide), lambda i: (0, i, 0, 0))],
        [
            pl.BlockSpec((a, 1, p, d), lambda i: (0, i, 0, 0)),
            pl.BlockSpec((1, HEADS, t), lambda i: (i, 0, 0)),
            pl.BlockSpec((1, 1, HEADS), lambda i: (i, 0, 0)),
        ],
        [sds((a, g, p, d), BF16), sds((g, HEADS, t), F32), sds((g, 1, HEADS), F32)],
        [pltpu.VMEM((t, d), F32)],
        flops=4 * g * HEADS * t * t * 256,
        nbytes=2 * a * g * p * (wide + d),
    )(qkv)


def out_forward(att, x, mods, w, bias):
    n, d = att.shape
    mt = fold(n, 256)

    def body(att_ref, x_ref, mod_ref, w_ref, b_ref, branch_ref, mid_ref, hid_ref):
        branch = mm(att_ref[...], w_ref[...]) + b_ref[...]
        branch_ref[...] = branch.astype(BF16)
        mid = x_ref[...].astype(F32) + mod_ref[2:3, :] * branch
        mid_ref[...] = mid
        v, _ = standard(mid)
        hid_ref[...] = (v * (1.0 + mod_ref[4:5, :]) + mod_ref[3:4, :]).astype(BF16)

    tile = pl.BlockSpec((mt, d), lambda m: (m, 0))
    return call(
        body,
        (n // mt,),
        [tile, tile, whole((8, d)), whole((d, d)), whole((1, d))],
        [tile, tile, tile],
        [sds((n, d), BF16), sds((n, d), F32), sds((n, d), BF16)],
        flops=2 * n * d * d,
        nbytes=2 * (d * d + 6 * n * d),
    )(att, x, mods, w, bias)


GELU_A = 0.7978845608028654
GELU_B = 0.044715


def up_forward(hid, w, bias):
    n, d = hid.shape
    ff = w.shape[1]
    mt = fold(n)
    ft = d
    cuts = 3

    def body(hid_ref, w_ref, b_ref, act_ref, slope_ref):
        for c in range(cuts):
            cols = slice(c * ft // cuts, (c + 1) * ft // cuts)
            u = mm(hid_ref[...], w_ref[:, cols]) + b_ref[:, cols]
            square = u * u
            tanh = jnp.tanh(u * (GELU_A + (GELU_A * GELU_B) * square))
            half = 0.5 + 0.5 * tanh
            act_ref[:, cols] = (u * half).astype(BF16)
            bend = GELU_A + (3.0 * GELU_A * GELU_B) * square
            slope_ref[:, cols] = (half + (u * half) * ((1.0 - tanh) * bend)).astype(BF16)

    tile = pl.BlockSpec((mt, ft), lambda f, m: (m, f))
    return call(
        body,
        (ff // ft, n // mt),
        [
            pl.BlockSpec((mt, d), lambda f, m: (m, 0)),
            pl.BlockSpec((d, ft), lambda f, m: (0, f)),
            pl.BlockSpec((1, ft), lambda f, m: (0, f)),
        ],
        [tile, tile],
        [sds((n, ff), BF16), sds((n, ff), BF16)],
        flops=2 * n * d * ff,
        nbytes=2 * (d * ff + 2 * n * ff + n * d),
    )(hid, w, bias)


def down_forward(act, mid, mods, w, bias):
    n, ff = act.shape
    d = w.shape[1]
    mt = fold(n)
    last = ff // d - 1

    def body(act_ref, mid_ref, mod_ref, w_ref, b_ref, upd_ref, out_ref, acc):
        k = pl.program_id(0)
        rows = pl.ds(pl.multiple_of(pl.program_id(1) * mt, mt), mt)
        part = mm(act_ref[...], w_ref[...])

        @pl.when(k == 0)
        def _():
            acc[rows, :] = part

        @pl.when((k > 0) & (k < last))
        def _():
            acc[rows, :] += part

        @pl.when(k == last)
        def _():
            upd = acc[rows, :] + part + b_ref[...]
            upd_ref[...] = upd.astype(BF16)
            out_ref[...] = (mid_ref[...] + mod_ref[5:6, :] * upd).astype(BF16)

    late = pl.BlockSpec((mt, d), lambda k, m: (jnp.where(k == last, m, 0), 0))
    return call(
        body,
        (ff // d, n // mt),
        [
            pl.BlockSpec((mt, d), lambda k, m: (m, k)),
            late,
            whole((8, d)),
            pl.BlockSpec((d, d), lambda k, m: (k, 0)),
            whole((1, d)),
        ],
        [late, late],
        [sds((n, d), BF16), sds((n, d), BF16)],
        [pltpu.VMEM((n, d), F32)],
        flops=2 * n * d * ff,
        nbytes=2 * (d * ff + n * ff + 4 * n * d),
    )(act, mid, mods, w, bias)


def column_sum(v):
    return jnp.sum(v, axis=0, keepdims=True)


def update_back(go, upd, mods):
    n, d = go.shape
    mt = fold(n, 256)

    def body(go_ref, upd_ref, mod_ref, gu_ref, sum_ref):
        @pl.when(pl.program_id(0) == 0)
        def _():
            sum_ref[...] = jnp.zeros_like(sum_ref)

        g = go_ref[...].astype(F32)
        low = (mod_ref[5:6, :] * g).astype(BF16)
        gu_ref[...] = low
        sum_ref[0:1, :] += column_sum(g * upd_ref[...].astype(F32))
        sum_ref[1:2, :] += column_sum(low.astype(F32))

    tile = pl.BlockSpec((mt, d), lambda m: (m, 0))
    return call(
        body,
        (n // mt,),
        [tile, tile, whole((8, d))],
        [tile, whole((8, d))],
        [sds((n, d), BF16), sds((8, d), F32)],
        flops=n * d,
        nbytes=6 * n * d,
    )(go, upd, mods)


def shed_specs(seq, zs, rows, d):
    return sds((seq, zs, rows, d), BF16)


def down_grad(place, act, gu, seq, zs):
    n, ff = act.shape
    d = gu.shape[1]
    rows, quarter = d // (2 * zs), d // seq
    parts = ff // (2 * zs) // rows

    def body(place_ref, act_ref, gu_ref, mine_ref, other_ref, full):
        core = place_ref[0]
        cuts = 3
        for c in range(cuts):
            span = slice(c * d // cuts, (c + 1) * d // cuts)
            full[span, :] = mm(act_ref[:, span], gu_ref[...], TN).astype(BF16)
        for c in range(2):
            for target, flag in ((mine_ref, core == c), (other_ref, core != c)):

                @pl.when(flag)
                def _(target=target, c=c):
                    for q in range(parts):
                        base = (c * parts + q) * rows
                        for s in range(seq):
                            target[s, 0, :, q * quarter : (q + 1) * quarter] = full[
                                base : base + rows, s * quarter : (s + 1) * quarter
                            ]

    piece = pl.BlockSpec((seq, 1, rows, d), lambda i, place_ref: (0, i, 0, 0))
    return call(
        body,
        (zs,),
        [
            pl.BlockSpec((n, ff // zs), lambda i, place_ref: (0, i ^ place_ref[1])),
            whole((n, d)),
        ],
        [piece, piece],
        [shed_specs(seq, zs, rows, d)] * 2,
        [pltpu.VMEM((ff // zs, d), BF16)],
        scalars=1,
        flops=2 * n * d * ff,
        nbytes=2 * (d * ff + n * ff + n * d),
    )(place, act, gu)


def spread(place_ref, full, mine_ref, other_ref, zs, rows, cols):
    core, z = place_ref[0], place_ref[1]
    for c in range(2):
        for target, flag in ((mine_ref, core == c), (other_ref, core != c)):

            @pl.when(flag)
            def _(target=target, c=c):
                for zz in range(zs):
                    base = (zz * 2 + c) * rows
                    target[0, zz ^ z, :, cols] = full[base : base + rows, cols]


def up_grad(place, hid, gi, seq, zs):
    n, d = hid.shape
    ff = gi.shape[1]
    rows, wide = d // (2 * zs), ff // seq

    def body(place_ref, hid_ref, gi_ref, mine_ref, other_ref, hid_t, full):
        cuts = 3

        @pl.when(pl.program_id(0) == 0)
        def _():
            for c in range(cuts):
                span = slice(c * d // cuts, (c + 1) * d // cuts)
                hid_t[span, :] = hid_ref[:, span].T

        for c in range(cuts):
            span = slice(c * d // cuts, (c + 1) * d // cuts)
            full[span, :] = mm(hid_t[span, :], gi_ref[...]).astype(BF16)
        spread(place_ref, full, mine_ref, other_ref, zs, rows, slice(0, wide))

    piece = pl.BlockSpec((1, zs, rows, wide), lambda i, place_ref: (i, 0, 0, 0))
    return call(
        body,
        (seq,),
        [whole((n, d)), pl.BlockSpec((n, wide), lambda i, place_ref: (0, i))],
        [piece, piece],
        [shed_specs(seq, zs, rows, wide)] * 2,
        [pltpu.VMEM((d, n), BF16), pltpu.VMEM((d, wide), BF16)],
        scalars=1,
        flops=2 * n * d * ff,
        nbytes=2 * (d * ff + n * ff + n * d),
    )(place, hid, gi)


def qkv_out_grad(place, hid, att, gqkv, gb, zs):
    n, d = hid.shape
    seq, _, wa = gqkv.shape
    wb = gb.shape[2]
    rows = d // (2 * zs)

    def body(place_ref, hid_ref, att_ref, gqkv_ref, gb_ref, mine_ref, other_ref, hid_t, att_t, full):
        cuts = 3

        @pl.when(pl.program_id(0) == 0)
        def _():
            for c in range(cuts):
                span = slice(c * d // cuts, (c + 1) * d // cuts)
                hid_t[span, :] = hid_ref[:, span].T
                att_t[span, :] = att_ref[:, span].T

        for c in range(cuts):
            span = slice(c * d // cuts, (c + 1) * d // cuts)
            full[span, :] = jnp.concatenate(
                [
                    mm(hid_t[span, :], gqkv_ref[0]).astype(BF16),
                    mm(att_t[span, :], gb_ref[0]).astype(BF16),
                ],
                axis=1,
            )
        spread(place_ref, full, mine_ref, other_ref, zs, rows, slice(0, wa + wb))

    piece = pl.BlockSpec((1, zs, rows, wa + wb), lambda i, place_ref: (i, 0, 0, 0))
    return call(
        body,
        (seq,),
        [
            whole((n, d)),
            whole((n, d)),
            pl.BlockSpec((1, n, wa), lambda i, place_ref: (i, 0, 0)),
            pl.BlockSpec((1, n, wb), lambda i, place_ref: (i, 0, 0)),
        ],
        [piece, piece],
        [shed_specs(seq, zs, rows, wa + wb)] * 2,
        [pltpu.VMEM((d, n), BF16), pltpu.VMEM((d, n), BF16), pltpu.VMEM((d, wa + wb), BF16)],
        scalars=1,
        flops=2 * n * d * seq * (wa + wb),
        nbytes=2 * seq * (d + n) * (wa + wb),
    )(place, hid, att, gqkv, gb)


def feed_back(gu, slope, w_down, w_up):
    n, d = gu.shape
    ff = slope.shape[1]
    mt = fold(n)
    last = ff // d - 1

    def body(gu_ref, slope_ref, wd_ref, wu_ref, gi_ref, bias_ref, out_ref, acc):
        f = pl.program_id(0)
        m = pl.program_id(1)
        rows = pl.ds(pl.multiple_of(m * mt, mt), mt)
        gi = (mm(gu_ref[...], wd_ref[...], NT) * slope_ref[...].astype(F32)).astype(BF16)
        gi_ref[...] = gi
        total = column_sum(gi.astype(F32))

        @pl.when(m == 0)
        def _():
            bias_ref[...] = total

        @pl.when(m > 0)
        def _():
            bias_ref[...] += total

        part = mm(gi, wu_ref[...], NT)

        @pl.when(f == 0)
        def _():
            acc[rows, :] = part

        @pl.when((f > 0) & (f < last))
        def _():
            acc[rows, :] += part

        @pl.when(f == last)
        def _():
            out_ref[...] = acc[rows, :] + part

    return call(
        body,
        (ff // d, n // mt),
        [
            pl.BlockSpec((mt, d), lambda f, m: (m, 0)),
            pl.BlockSpec((mt, d), lambda f, m: (m, f)),
            pl.BlockSpec((d, d), lambda f, m: (f, 0)),
            pl.BlockSpec((d, d), lambda f, m: (0, f)),
        ],
        [
            pl.BlockSpec((mt, d), lambda f, m: (m, f)),
            pl.BlockSpec((1, d), lambda f, m: (0, f)),
            pl.BlockSpec((mt, d), lambda f, m: (jnp.where(f == last, m, 0), 0)),
        ],
        [sds((n, ff), BF16), sds((1, ff), F32), sds((n, d), F32)],
        [pltpu.VMEM((n, d), F32)],
        flops=4 * n * d * ff,
        nbytes=2 * (2 * d * ff + 2 * n * ff + 3 * n * d),
    )(gu, slope, w_down, w_up)


def norm_back(grad, v, r, stretch):
    dn = grad * stretch
    return r * (
        dn - jnp.mean(dn, axis=-1, keepdims=True) - v * jnp.mean(dn * v, axis=-1, keepdims=True)
    )


def middle_back(gh, mid, branch, go, mods, w, seq):
    n, d = gh.shape
    mt = fold(n, 256)
    wide = d // seq

    def body(gh_ref, mid_ref, branch_ref, go_ref, mod_ref, w_ref, gmid_ref, gb_ref, cut_ref, ga_ref, sum_ref):
        @pl.when(pl.program_id(0) == 0)
        def _():
            sum_ref[...] = jnp.zeros_like(sum_ref)

        g = gh_ref[...]
        v, r = standard(mid_ref[...])
        sum_ref[0:1, :] += column_sum(g * v)
        sum_ref[1:2, :] += column_sum(g)
        gmid = go_ref[...].astype(F32) + norm_back(g, v, r, 1.0 + mod_ref[4:5, :])
        gmid_ref[...] = gmid
        sum_ref[2:3, :] += column_sum(gmid * branch_ref[...].astype(F32))
        low = (mod_ref[2:3, :] * gmid).astype(BF16)
        gb_ref[...] = low
        for s in range(seq):
            cut_ref[s] = low[:, s * wide : (s + 1) * wide]
        sum_ref[3:4, :] += column_sum(low.astype(F32))
        ga_ref[...] = mm(low, w_ref[...], NT).astype(BF16)

    tile = pl.BlockSpec((mt, d), lambda m: (m, 0))
    return call(
        body,
        (n // mt,),
        [tile, tile, tile, tile, whole((8, d)), whole((d, d))],
        [tile, tile, pl.BlockSpec((seq, mt, wide), lambda m: (0, m, 0)), tile, whole((8, d))],
        [
            sds((n, d), F32),
            sds((n, d), BF16),
            sds((seq, n, wide), BF16),
            sds((n, d), BF16),
            sds((8, d), F32),
        ],
        flops=2 * n * d * d,
        nbytes=2 * (d * d + 11 * n * d),
    )(gh, mid, branch, go, mods, w)


def attention_back(qkv, ga, lse, temporal, seq):
    a, g, p, wide = qkv.shape
    d = wide // 3
    size = d // HEADS
    t = a * p
    scale = size ** (-0.5)
    cut = wide // seq

    def body(qkv_ref, ga_ref, lse_ref, out_ref, cut_ref, sum_ref, acc):
        acc[...] = jnp.zeros_like(acc)
        if temporal:
            ki = lax.broadcasted_iota(jnp.int32, (t, t), 0)
            qi = lax.broadcasted_iota(jnp.int32, (t, t), 1)
            same = lax.rem(qi, p) == lax.rem(ki, p)
        for h in range(HEADS):
            lo, hi, off = window(h, size, d)
            keep = head_mask(lo, hi, off, size, t)
            q = qkv_ref[:, 0, :, lo:hi].reshape(t, hi - lo)
            k = qkv_ref[:, 0, :, d + lo : d + hi].reshape(t, hi - lo)
            v = qkv_ref[:, 0, :, 2 * d + lo : 2 * d + hi].reshape(t, hi - lo)
            o = ga_ref[:, 0, :, lo:hi].reshape(t, hi - lo)
            zero = jnp.zeros_like(q)
            q, o = jnp.where(keep, q, zero), jnp.where(keep, o, zero)
            s = mm(k, q, NT) * scale
            probs = jnp.exp(s - lse_ref[0, h : h + 1, :])
            if temporal:
                probs = jnp.where(same, probs, 0.0)
            dp = mm(v, o, NT)
            acc[:, 2 * d + lo : 2 * d + hi] += mm(probs.astype(BF16), o)
            ds = (probs * (dp - column_sum(probs * dp))).astype(BF16)
            acc[:, d + lo : d + hi] += mm(ds, q) * scale
            acc[:, lo:hi] += mm(ds, jnp.where(keep, k, zero), TN) * scale
        low = acc[...].astype(BF16)
        out_ref[...] = low.reshape(a, 1, p, wide)
        for s in range(seq):
            cut_ref[s] = low[:, s * cut : (s + 1) * cut].reshape(a, 1, p, cut)
        total = column_sum(low.astype(F32))

        @pl.when(pl.program_id(0) == 0)
        def _():
            sum_ref[...] = total

        @pl.when(pl.program_id(0) > 0)
        def _():
            sum_ref[...] += total

    return call(
        body,
        (g,),
        [
            pl.BlockSpec((a, 1, p, wide), lambda i: (0, i, 0, 0)),
            pl.BlockSpec((a, 1, p, d), lambda i: (0, i, 0, 0)),
            pl.BlockSpec((1, HEADS, t), lambda i: (i, 0, 0)),
        ],
        [
            pl.BlockSpec((a, 1, p, wide), lambda i: (0, i, 0, 0)),
            pl.BlockSpec((seq, a, 1, p, cut), lambda i: (0, 0, i, 0, 0)),
            whole((1, wide)),
        ],
        [sds((a, g, p, wide), BF16), sds((seq, a, g, p, cut), BF16), sds((1, wide), F32)],
        [pltpu.VMEM((t, wide), F32)],
        flops=12 * g * HEADS * t * t * 256,
        nbytes=2 * a * g * p * (3 * wide + d),
    )(qkv, ga, lse)


def stream_back(gqkv, w, x, gmid, mods, out_dtype):
    n, wide = gqkv.shape
    d = w.shape[0]
    mt = fold(n)
    last = wide // d - 1

    def body(g_ref, w_ref, x_ref, gmid_ref, mod_ref, out_ref, sum_ref, acc):
        k = pl.program_id(0)
        m = pl.program_id(1)
        rows = pl.ds(pl.multiple_of(m * mt, mt), mt)
        part = mm(g_ref[...], w_ref[...], NT)

        @pl.when(k == 0)
        def _():
            acc[rows, :] = part

        @pl.when((k > 0) & (k < last))
        def _():
            acc[rows, :] += part

        @pl.when((k == last) & (m == 0))
        def _():
            sum_ref[...] = jnp.zeros_like(sum_ref)

        @pl.when(k == last)
        def _():
            grad = acc[rows, :] + part
            v, r = standard(x_ref[...].astype(F32))
            sum_ref[0:1, :] += column_sum(grad * v)
            sum_ref[1:2, :] += column_sum(grad)
            out_ref[...] = (gmid_ref[...] + norm_back(grad, v, r, 1.0 + mod_ref[1:2, :])).astype(
                out_dtype
            )

    late = pl.BlockSpec((mt, d), lambda k, m: (jnp.where(k == last, m, 0), 0))
    return call(
        body,
        (wide // d, n // mt),
        [
            pl.BlockSpec((mt, d), lambda k, m: (m, k)),
            pl.BlockSpec((d, d), lambda k, m: (0, k)),
            late,
            late,
            whole((8, d)),
        ],
        [late, whole((8, d))],
        [sds((n, d), out_dtype), sds((8, d), F32)],
        [pltpu.VMEM((n, d), F32)],
        flops=2 * n * d * wide,
        nbytes=2 * (d * wide + n * wide + 5 * n * d),
    )(gqkv, w, x, gmid, mods)


def join_qkv_out(place, own, got):
    seq, zs, rows, d = own.shape
    wide = d * 3 // 4

    def body(place_ref, own_ref, got_ref, qkv_ref, out_ref):
        def put(c, src):
            span = slice(c * rows, (c + 1) * rows)
            qkv_ref[span, :] = jnp.concatenate([src[s, 0, :, :wide] for s in range(seq)], axis=1)
            out_ref[span, :] = jnp.concatenate([src[s, 0, :, wide:] for s in range(seq)], axis=1)

        for c in range(2):

            @pl.when(place_ref[0] == c)
            def _(c=c):
                put(c, own_ref)
                put(1 - c, got_ref)

    piece = pl.BlockSpec((seq, 1, rows, d), lambda i, place_ref: (0, i ^ place_ref[1], 0, 0))
    return call(
        body,
        (zs,),
        [piece, piece],
        [
            pl.BlockSpec((2 * rows, seq * wide), lambda i, place_ref: (i, 0)),
            pl.BlockSpec((2 * rows, d), lambda i, place_ref: (i, 0)),
        ],
        [sds((2 * rows * zs, seq * wide), BF16), sds((2 * rows * zs, d), BF16)],
        scalars=1,
        nbytes=8 * seq * zs * rows * d,
    )(place, own, got)


def join_up(place, own, got):
    seq, zs, rows, d = own.shape

    def body(place_ref, own_ref, got_ref, up_ref):
        for c in range(2):

            @pl.when(place_ref[0] == c)
            def _(c=c):
                for s in range(seq):
                    cols = slice(s * d, (s + 1) * d)
                    up_ref[c * rows : (c + 1) * rows, cols] = own_ref[s, 0]
                    up_ref[(1 - c) * rows : (2 - c) * rows, cols] = got_ref[s, 0]

    piece = pl.BlockSpec((seq, 1, rows, d), lambda i, place_ref: (0, i ^ place_ref[1], 0, 0))
    return call(
        body,
        (zs,),
        [piece, piece],
        pl.BlockSpec((2 * rows, seq * d), lambda i, place_ref: (i, 0)),
        sds((2 * rows * zs, seq * d), BF16),
        scalars=1,
        nbytes=8 * seq * zs * rows * d,
    )(place, own, got)


def join_down(place, own, got):
    seq, zs, rows, d = own.shape
    quarter = d // seq
    parts = d // quarter

    def body(place_ref, own_ref, got_ref, down_ref):
        def put(c, src):
            for q in range(parts):
                base = (c * parts + q) * rows
                cols = slice(q * quarter, (q + 1) * quarter)
                down_ref[base : base + rows, :] = jnp.concatenate(
                    [src[s, 0, :, cols] for s in range(seq)], axis=1
                )

        for c in range(2):

            @pl.when(place_ref[0] == c)
            def _(c=c):
                put(c, own_ref)
                put(1 - c, got_ref)

    piece = pl.BlockSpec((seq, 1, rows, d), lambda i, place_ref: (0, i ^ place_ref[1], 0, 0))
    return call(
        body,
        (zs,),
        [piece, piece],
        pl.BlockSpec((2 * parts * rows, d), lambda i, place_ref: (i, 0)),
        sds((2 * parts * rows * zs, d), BF16),
        scalars=1,
        nbytes=8 * seq * zs * rows * d,
    )(place, own, got)


clip_limit = 8.0


def hop(x, distance, count):
    return lax.ppermute(x, "clip", [(i, i ^ distance) for i in range(count)])


def on_device(
    video_latents,
    conditioning,
    ada_weight,
    ada_bias,
    qkv_weight,
    out_weight,
    up_weight,
    down_weight,
    attention_bias,
    up_bias,
    down_bias,
    cotangent,
    *,
    clips,
    seq,
):
    zs = clips // 2
    layers, rows, own_columns = qkv_weight.shape
    d = video_latents.shape[-1]
    frames, places = video_latents.shape[1:3]
    n = frames * places
    ff = up_bias.shape[1]
    clip_index = lax.axis_index("clip")
    place = jnp.stack([clip_index % 2, clip_index // 2]).astype(jnp.int32)
    packed = rows % 16 == 0 and down_weight.shape[1] % rows == 0 and d % seq == 0
    cuts = seq if packed else 1

    every_condition = lax.all_gather(conditioning, "clip", axis=0, tiled=True)
    squashed = jax.nn.silu(every_condition).astype(BF16)
    local_mods = (
        jnp.einsum("kd,ldc->klc", squashed, ada_weight, preferred_element_type=F32)
        + ada_bias[None, :, :]
    )
    own_mods = lax.all_to_all(local_mods, "clip", 0, 0, tiled=True)
    every_mod = lax.all_gather(own_mods, "seq", axis=0, tiled=False)
    modulation = every_mod.transpose(2, 1, 0, 3).reshape(layers, 6, d)
    modulation = jnp.pad(modulation, ((0, 0), (0, 2), (0, 0)))

    def spread_out(block):
        blocks = block[None]
        step = 1
        while step < zs:
            blocks = jnp.concatenate([blocks, hop(blocks, 2 * step, clips)], axis=0)
            step *= 2
        own = lax.all_gather(blocks, "seq", axis=0, tiled=False)
        return own, hop(own, 1, clips)

    def fetch(layer):
        if packed:
            tall = down_weight[layer].reshape(-1, rows, d // seq)
            qkv_full, out_full = join_qkv_out(
                place,
                *spread_out(jnp.concatenate([qkv_weight[layer], out_weight[layer]], axis=1)),
            )
            up_full = join_up(place, *spread_out(up_weight[layer]))
            down_full = join_down(
                place,
                *spread_out(tall.transpose(1, 0, 2).reshape(rows, d)),
            )
            return qkv_full, out_full, up_full, down_full
        return tuple(
            lax.all_gather(
                lax.all_gather(item[layer], "clip", axis=0, tiled=True), "seq", axis=1, tiled=True
            )
            for item in (qkv_weight, out_weight, up_weight, down_weight)
        )

    def gather_in(mine, other):
        half = mine + hop(other, 1, clips)
        flat = lax.psum_scatter(half.reshape(-1, d), "seq", scatter_dimension=0, tiled=True)
        part = flat.reshape(zs, rows, d)
        step = zs // 2
        while step >= 1:
            part = part[:step].astype(F32) + hop(part[step:], 2 * step, clips).astype(F32)
            if step > 1:
                part = part.astype(BF16)
            step //= 2
        return part[0]

    def shed_natural(left, right):
        full = mm(left, right, TN).astype(BF16)
        part = lax.psum_scatter(full, "seq", scatter_dimension=1, tiled=True)
        return lax.psum_scatter(part, "clip", scatter_dimension=0, tiled=True).astype(F32)

    def swap_tokens(x):
        block = x.reshape(seq, n // seq, d)
        return lax.all_to_all(block, "seq", 0, 0, tiled=True).reshape(n, d)

    def by_places(x):
        return x.reshape(frames, seq, places // seq, d).transpose(1, 0, 2, 3).reshape(n, d)

    def by_frames(x):
        return (
            x.reshape(seq, frames, places // seq, d)
            .transpose(1, 0, 2, 3)
            .reshape(1, frames, places, d)
        )

    shapes = (
        (seq, frames, places // seq),
        (seq * frames, places // seq // 16, 16),
    )

    def forward(layer, x, weights):
        qkv_full, out_full, up_full, down_full = weights
        temporal = layer == 1
        mods = modulation[layer]
        bias = attention_bias[layer]
        qkv_bias = jnp.concatenate([bias[0], jnp.zeros_like(bias[0]), bias[1]])[None]
        hidden, qkv = qkv_forward(x, mods, qkv_full, qkv_bias)
        qkv = qkv.reshape(shapes[layer] + (3 * d,))
        attended, lse, peak = attention_forward(qkv, temporal)
        attended = attended.reshape(n, d)
        branch, middle, hidden_two = out_forward(attended, x, mods, out_full, bias[2:3])
        active, slope = up_forward(hidden_two, up_full, up_bias[layer : layer + 1])
        update, result = down_forward(
            active, middle, mods, down_full, down_bias[layer : layer + 1]
        )
        kept = (x, hidden, qkv, lse, attended, branch, middle, hidden_two, active, slope, update)
        return result, kept, jnp.max(peak, axis=(0, 1))

    def backward(layer, grad_out, kept, weights):
        x, hidden, qkv, lse, attended, branch, middle, hidden_two, active, slope, update = kept
        qkv_full, out_full, up_full, down_full = weights
        temporal = layer == 1
        mods = modulation[layer]
        grad_update, update_sums = update_back(grad_out, update, mods)
        if packed:
            down_g = gather_in(*down_grad(place, active, grad_update, seq, zs))
            down_g = down_g.reshape(rows, -1, d // seq).transpose(1, 0, 2).reshape(-1, d // seq)
        else:
            down_g = shed_natural(active, grad_update)
        inner_grad, up_sums, hidden_grad = feed_back(grad_update, slope, down_full, up_full)
        if packed:
            up_g = gather_in(*up_grad(place, hidden_two, inner_grad, seq, zs))
        else:
            up_g = shed_natural(hidden_two, inner_grad)
        middle_grad, branch_grad, branch_cut, attended_grad, middle_sums = middle_back(
            hidden_grad, middle, branch, grad_out, mods, out_full, cuts
        )
        qkv_grad, qkv_cut, qkv_sums = attention_back(
            qkv, attended_grad.reshape(shapes[layer] + (d,)), lse, temporal, cuts
        )
        qkv_grad = qkv_grad.reshape(n, 3 * d)
        stream_grad, stream_sums = stream_back(
            qkv_grad, qkv_full, x, middle_grad, mods, BF16 if temporal else F32
        )
        if packed:
            both = gather_in(
                *qkv_out_grad(
                    place, hidden, attended, qkv_cut.reshape(seq, n, -1), branch_cut, zs
                )
            )
            qkv_g, out_g = both[:, :own_columns], both[:, own_columns:]
        else:
            qkv_g = shed_natural(hidden, qkv_grad)
            out_g = shed_natural(attended, branch_grad)
        mod_grad = jnp.concatenate(
            [
                stream_sums[1:2],
                stream_sums[0:1],
                middle_sums[2:3],
                middle_sums[1:2],
                middle_sums[0:1],
                update_sums[0:1],
            ],
            axis=0,
        )
        bias_grad = jnp.concatenate(
            [
                qkv_sums[:, :d],
                qkv_sums[:, 2 * d :],
                middle_sums[3:4],
                update_sums[1:2],
                up_sums.reshape(-1, d),
            ],
            axis=0,
        )
        return stream_grad, mod_grad, bias_grad, (qkv_g, out_g, up_g, down_g)

    first_weights = fetch(0)
    second_weights = fetch(1)
    first_in = by_places(video_latents)
    second_go = swap_tokens(by_places(cotangent))
    first_out, first_kept, first_peak = forward(0, first_in, first_weights)
    second_out, second_kept, second_peak = forward(1, swap_tokens(first_out), second_weights)
    output_latents = by_frames(swap_tokens(second_out))

    peaks = lax.all_gather(jnp.stack([first_peak, second_peak]), ("clip", "seq"), axis=0)
    logit_peak = jnp.max(peaks, axis=0)
    column_index = lax.axis_index("seq") * own_columns + jnp.arange(own_columns, dtype=jnp.int32)
    head_of = column_index % d // (d // HEADS)
    head_match = (head_of[:, None] == jnp.arange(HEADS, dtype=jnp.int32)[None, :]).astype(F32)
    roots = jnp.sqrt(clip_limit / jnp.maximum(logit_peak, clip_limit))
    column_roots = jnp.sum(roots[:, None, :] * head_match[None, :, :], axis=-1)
    column_scale = jnp.where(column_index[None, :] < 2 * d, column_roots, 1.0)
    clipped_qkv = qkv_weight.astype(F32) * column_scale[:, None, :]

    second_grad, second_mod, second_bias, second_shed = backward(
        1, second_go, second_kept, second_weights
    )
    latents_grad, first_mod, first_bias, first_shed = backward(
        0, swap_tokens(second_grad), first_kept, first_weights
    )

    mod_grads = jnp.stack([first_mod, second_mod]).reshape(layers, clips, seq, -1)
    of_columns = lax.psum_scatter(
        mod_grads.transpose(2, 1, 0, 3), "seq", scatter_dimension=0, tiled=False
    )
    own_mod_grad = lax.all_to_all(of_columns, "clip", 0, 0, tiled=True)
    ada_bias_grad = jnp.sum(own_mod_grad, axis=0)
    rounded_mod = own_mod_grad.astype(BF16)
    ada_weight_grad = jnp.einsum("kd,klc->ldc", squashed, rounded_mod, preferred_element_type=F32)
    squash_part = jnp.einsum("klc,ldc->kd", rounded_mod, ada_weight, preferred_element_type=F32)
    bias_rows = first_bias.shape[0]
    summed = lax.psum(
        jnp.concatenate([first_bias, second_bias, squash_part], axis=0), ("clip", "seq")
    )
    bias_sums = summed[: 2 * bias_rows].reshape(layers, bias_rows, d)
    own_squash = lax.dynamic_slice_in_dim(summed[2 * bias_rows :], clip_index, 1, axis=0)
    silu_value, silu_pull = jax.vjp(jax.nn.silu, conditioning)
    conditioning_grad = silu_pull(own_squash)[0]
    return (
        output_latents,
        latents_grad.reshape(seq, frames, places // seq, d)
        .transpose(1, 0, 2, 3)
        .reshape(1, frames, places, d),
        conditioning_grad,
        ada_weight_grad,
        ada_bias_grad,
        jnp.stack([first_shed[0], second_shed[0]]),
        jnp.stack([first_shed[1], second_shed[1]]),
        jnp.stack([first_shed[2], second_shed[2]]),
        jnp.stack([first_shed[3], second_shed[3]]),
        bias_sums[:, :3],
        bias_sums[:, 4:].reshape(layers, ff),
        bias_sums[:, 3],
        clipped_qkv,
        logit_peak,
    )


def solution(mesh):
    return jax.shard_map(
        partial(on_device, clips=mesh.shape["clip"], seq=mesh.shape["seq"]),
        mesh=mesh,
        in_specs=(
            P("clip", "seq", None, None),
            P("clip", None),
            P(None, None, ("clip", "seq")),
            P(None, ("clip", "seq")),
            P(None, "clip", "seq"),
            P(None, "clip", "seq"),
            P(None, "clip", "seq"),
            P(None, "clip", "seq"),
            P(),
            P(),
            P(),
            P("clip", "seq", None, None),
        ),
        out_specs=(
            P("clip", "seq", None, None),
            P("clip", "seq", None, None),
            P("clip", None),
            P(None, None, ("clip", "seq")),
            P(None, ("clip", "seq")),
            P(None, "clip", "seq"),
            P(None, "clip", "seq"),
            P(None, "clip", "seq"),
            P(None, "clip", "seq"),
            P(),
            P(),
            P(),
            P(None, "clip", "seq"),
            P(),
        ),
        check_vma=False,
    )
```

```python
from functools import partial

import jax
import jax.numpy as jnp
from jax import lax
from jax.experimental import pallas as pl
from jax.experimental.pallas import tpu as pltpu
from jax.sharding import PartitionSpec as P

HEADS = 16
F32 = jnp.float32
BF16 = jnp.bfloat16
NN = (((1,), (0,)), ((), ()))
NT = (((1,), (1,)), ((), ()))
TN = (((0,), (0,)), ((), ()))
VMEM_BYTES = 56 * 1024 * 1024
FEED_ROWS = 1024
UP_ROWS, UP_CUTS = 1024, 1
QKV_ROWS = 512


def mm(a, b, dims=NN):
    return lax.dot_general(a, b, dims, preferred_element_type=F32)


def call(
    body, grid, in_specs, out_specs, out_shape, scratch=(), scalars=0, flops=0, nbytes=0, deps=()
):
    first = scalars + len(in_specs)

    def run(*refs):
        body(*refs[:first], *refs[first + len(deps) :])

    kernel = pl.pallas_call(
        run,
        grid_spec=pltpu.PrefetchScalarGridSpec(
            num_scalar_prefetch=scalars,
            grid=grid,
            in_specs=[*in_specs, *[pl.BlockSpec(memory_space=pl.ANY)] * len(deps)],
            out_specs=out_specs,
            scratch_shapes=list(scratch),
        ),
        out_shape=out_shape,
        compiler_params=pltpu.CompilerParams(
            dimension_semantics=("arbitrary",) * len(grid), vmem_limit_bytes=VMEM_BYTES
        ),
        cost_estimate=pl.CostEstimate(flops=flops, bytes_accessed=nbytes, transcendentals=0),
    )
    return lambda *args: kernel(*args, *deps)


def gate(x, deps):
    def body(*refs):
        pass

    anywhere = pl.BlockSpec(memory_space=pl.ANY)
    return pl.pallas_call(
        body,
        in_specs=[anywhere] * (1 + len(deps)),
        out_specs=anywhere,
        out_shape=sds(x.shape, x.dtype),
        input_output_aliases={0: 0},
    )(x, *deps)


def joint(*arrays):
    def body(*refs):
        pass

    anywhere = pl.BlockSpec(memory_space=pl.ANY)
    return pl.pallas_call(
        body,
        in_specs=[anywhere] * len(arrays),
        out_specs=[anywhere] * len(arrays),
        out_shape=[sds(x.shape, x.dtype) for x in arrays],
        input_output_aliases={k: k for k in range(len(arrays))},
    )(*arrays)


def whole(shape):
    return pl.BlockSpec(shape, lambda *_: (0,) * len(shape))


def sds(shape, dtype):
    return jax.ShapeDtypeStruct(shape, dtype)


def standard(x):
    centred = x - jnp.mean(x, axis=-1, keepdims=True)
    r = lax.rsqrt(jnp.mean(centred * centred, axis=-1, keepdims=True) + 1e-06)
    return centred * r, r


def fold(n, limit=512):
    return min(n, limit)


def qkv_forward(x, mods, w, bias, deps=()):
    n, d = x.shape
    wide = w.shape[1]
    mt = fold(n, QKV_ROWS)

    def body(x_ref, mod_ref, w_ref, b_ref, hid_ref, out_ref):
        m = pl.program_id(1)
        rows = pl.ds(pl.multiple_of(m * mt, mt), mt)

        @pl.when(pl.program_id(0) == 0)
        def _():
            v, _ = standard(x_ref[...].astype(F32))
            hid_ref[rows, :] = (v * (1.0 + mod_ref[1:2, :]) + mod_ref[0:1, :]).astype(BF16)

        out_ref[...] = (mm(hid_ref[rows, :], w_ref[...]) + b_ref[...]).astype(BF16)

    return call(
        body,
        (wide // d, n // mt),
        [
            pl.BlockSpec((mt, d), lambda j, m: (jnp.where(j == 0, m, n // mt - 1), 0)),
            whole((8, d)),
            pl.BlockSpec((d, d), lambda j, m: (0, j)),
            pl.BlockSpec((1, d), lambda j, m: (0, j)),
        ],
        [whole((n, d)), pl.BlockSpec((mt, d), lambda j, m: (m, j))],
        [sds((n, d), BF16), sds((n, wide), BF16)],
        flops=2 * n * d * wide,
        nbytes=2 * (d * wide + n * wide + 2 * n * d),
        deps=deps,
    )(x, mods, w, bias)


def window(h, size, d):
    lo = h * size
    start = lo // 128 * 128
    stop = min(-(-(lo + size) // 128) * 128, d)
    return start, stop, lo - start


def head_mask(start, stop, off, size, rows):
    lane = lax.broadcasted_iota(jnp.int32, (rows, stop - start), 1)
    return (lane >= off) & (lane < off + size)


def attention_forward(qkv, temporal, deps=()):
    a, g, p, wide = qkv.shape
    d = wide // 3
    size = d // HEADS
    t = a * p
    scale = size ** (-0.5)

    def body(qkv_ref, att_ref, lse_ref, peak_ref, acc):
        acc[...] = jnp.zeros_like(acc)
        if temporal:
            qi = lax.broadcasted_iota(jnp.int32, (t, t), 0)
            ki = lax.broadcasted_iota(jnp.int32, (t, t), 1)
            same = lax.rem(qi, p) == lax.rem(ki, p)
        tops, totals = [], []
        for h in range(HEADS):
            lo, hi, off = window(h, size, d)
            keep = head_mask(lo, hi, off, size, t)
            q = qkv_ref[:, 0, :, lo:hi].reshape(t, hi - lo)
            k = qkv_ref[:, 0, :, d + lo : d + hi].reshape(t, hi - lo)
            v = qkv_ref[:, 0, :, 2 * d + lo : 2 * d + hi].reshape(t, hi - lo)
            zero = jnp.zeros_like(q)
            s = mm(jnp.where(keep, q, zero), k, NT) * scale
            if temporal:
                s = jnp.where(same, s, -1e30)
            top = jnp.max(s, axis=-1, keepdims=True)
            e = jnp.exp(s - top)
            total = jnp.sum(e, axis=-1, keepdims=True)
            probs = (e / total).astype(BF16)
            acc[:, lo:hi] += mm(probs, jnp.where(keep, v, zero))
            tops.append(top)
            totals.append(total)
        top = jnp.concatenate(tops, axis=1)
        lse_ref[0] = (top + jnp.log(jnp.concatenate(totals, axis=1))).T
        peak_ref[...] = jnp.max(top, axis=0, keepdims=True)[None]
        att_ref[...] = acc[...].astype(BF16).reshape(a, 1, p, d)

    return call(
        body,
        (g,),
        [pl.BlockSpec((a, 1, p, wide), lambda i: (0, i, 0, 0))],
        [
            pl.BlockSpec((a, 1, p, d), lambda i: (0, i, 0, 0)),
            pl.BlockSpec((1, HEADS, t), lambda i: (i, 0, 0)),
            pl.BlockSpec((1, 1, HEADS), lambda i: (i, 0, 0)),
        ],
        [sds((a, g, p, d), BF16), sds((g, HEADS, t), F32), sds((g, 1, HEADS), F32)],
        [pltpu.VMEM((t, d), F32)],
        flops=4 * g * HEADS * t * t * 256,
        nbytes=2 * a * g * p * (wide + d),
        deps=deps,
    )(qkv)


def out_forward(att, x, mods, w, bias, deps=()):
    n, d = att.shape
    mt = fold(n, 256)

    def body(att_ref, x_ref, mod_ref, w_ref, b_ref, branch_ref, mid_ref, hid_ref):
        branch = mm(att_ref[...], w_ref[...]) + b_ref[...]
        branch_ref[...] = branch.astype(BF16)
        mid = x_ref[...].astype(F32) + mod_ref[2:3, :] * branch
        mid_ref[...] = mid
        v, _ = standard(mid)
        hid_ref[...] = (v * (1.0 + mod_ref[4:5, :]) + mod_ref[3:4, :]).astype(BF16)

    tile = pl.BlockSpec((mt, d), lambda m: (m, 0))
    return call(
        body,
        (n // mt,),
        [tile, tile, whole((8, d)), whole((d, d)), whole((1, d))],
        [tile, tile, tile],
        [sds((n, d), BF16), sds((n, d), F32), sds((n, d), BF16)],
        flops=2 * n * d * d,
        nbytes=2 * (d * d + 6 * n * d),
        deps=deps,
    )(att, x, mods, w, bias)


GELU_A = 0.7978845608028654
GELU_B = 0.044715


def up_forward(hid, w, bias, deps=()):
    n, d = hid.shape
    ff = w.shape[1]
    mt = fold(n, UP_ROWS)
    ft = d
    cuts = UP_CUTS

    def body(hid_ref, w_ref, b_ref, act_ref, slope_ref):
        for c in range(cuts):
            cols = slice(c * ft // cuts, (c + 1) * ft // cuts)
            u = mm(hid_ref[...], w_ref[:, cols]) + b_ref[:, cols]
            square = u * u
            tanh = jnp.tanh(u * (GELU_A + (GELU_A * GELU_B) * square))
            half = 0.5 + 0.5 * tanh
            act_ref[:, cols] = (u * half).astype(BF16)
            bend = GELU_A + (3.0 * GELU_A * GELU_B) * square
            slope_ref[:, cols] = (half + (u * half) * ((1.0 - tanh) * bend)).astype(BF16)

    tile = pl.BlockSpec((mt, ft), lambda f, m: (m, f))
    return call(
        body,
        (ff // ft, n // mt),
        [
            pl.BlockSpec((mt, d), lambda f, m: (m, 0)),
            pl.BlockSpec((d, ft), lambda f, m: (0, f)),
            pl.BlockSpec((1, ft), lambda f, m: (0, f)),
        ],
        [tile, tile],
        [sds((n, ff), BF16), sds((n, ff), BF16)],
        flops=2 * n * d * ff,
        nbytes=2 * (d * ff + 2 * n * ff + n * d),
        deps=deps,
    )(hid, w, bias)


def down_forward(act, mid, mods, w, bias, deps=()):
    n, ff = act.shape
    d = w.shape[1]
    mt = fold(n, 256)

    def body(act_ref, mid_ref, mod_ref, w_ref, b_ref, upd_ref, out_ref):
        upd = mm(act_ref[...], w_ref[...]) + b_ref[...]
        upd_ref[...] = upd.astype(BF16)
        out_ref[...] = (mid_ref[...] + mod_ref[5:6, :] * upd).astype(BF16)

    tile = pl.BlockSpec((mt, d), lambda m: (m, 0))
    return call(
        body,
        (n // mt,),
        [
            pl.BlockSpec((mt, ff), lambda m: (m, 0)),
            tile,
            whole((8, d)),
            whole((ff, d)),
            whole((1, d)),
        ],
        [tile, tile],
        [sds((n, d), BF16), sds((n, d), BF16)],
        flops=2 * n * d * ff,
        nbytes=2 * (d * ff + n * ff + 4 * n * d),
        deps=deps,
    )(act, mid, mods, w, bias)


def column_sum(v):
    return jnp.sum(v, axis=0, keepdims=True)


def update_back(go, mods, deps=()):
    n, d = go.shape
    mt = fold(n, 256)

    def body(go_ref, mod_ref, gu_ref, sum_ref):
        @pl.when(pl.program_id(0) == 0)
        def _():
            sum_ref[...] = jnp.zeros_like(sum_ref)

        low = (mod_ref[5:6, :] * go_ref[...].astype(F32)).astype(BF16)
        gu_ref[...] = low
        sum_ref[0:1, :] += column_sum(low.astype(F32))

    tile = pl.BlockSpec((mt, d), lambda m: (m, 0))
    return call(
        body,
        (n // mt,),
        [tile, whole((8, d))],
        [tile, whole((8, d))],
        [sds((n, d), BF16), sds((8, d), F32)],
        flops=n * d,
        nbytes=4 * n * d,
        deps=deps,
    )(go, mods)


def shed_specs(seq, zs, rows, d):
    return sds((seq, zs, rows, d), BF16)


def shares(start, stop, rows):
    found = []
    while start < stop:
        block = start // rows
        end = min(stop, (block + 1) * rows)
        found.append((block, start - block * rows, start, end))
        start = end
    return found


def down_grad(place, act, gu, seq, zs, deps=()):
    n, ff = act.shape
    d = gu.shape[1]
    rows, quarter = d // (2 * zs), d // seq
    parts = ff // (2 * zs) // rows
    cuts = 3

    def body(place_ref, act_ref, gu_ref, mine_ref, other_ref):
        def fill(targets):
            for c in range(cuts):
                first, stop = c * (ff // zs) // cuts, (c + 1) * (ff // zs) // cuts
                full = mm(act_ref[:, first:stop], gu_ref[...], TN).astype(BF16)
                for block, at, lo, hi in shares(first, stop, rows):
                    target, q = targets[block // parts], block % parts
                    for s in range(seq):
                        target[s, 0, at : at + hi - lo, q * quarter : (q + 1) * quarter] = full[
                            lo - first : hi - first, s * quarter : (s + 1) * quarter
                        ]

        @pl.when(place_ref[0] == 0)
        def _():
            fill((mine_ref, other_ref))

        @pl.when(place_ref[0] == 1)
        def _():
            fill((other_ref, mine_ref))

    piece = pl.BlockSpec((seq, 1, rows, d), lambda i, place_ref: (0, i, 0, 0))
    return call(
        body,
        (zs,),
        [
            pl.BlockSpec((n, ff // zs), lambda i, place_ref: (0, i ^ place_ref[1])),
            whole((n, d)),
        ],
        [piece, piece],
        [shed_specs(seq, zs, rows, d)] * 2,
        scalars=1,
        flops=2 * n * d * ff,
        nbytes=2 * (d * ff + n * ff + n * d),
        deps=deps,
    )(place, act, gu)


def up_grad(place, hid, gi, seq, zs, deps=()):
    n, d = hid.shape
    ff = gi.shape[1]
    rows, wide = d // (2 * zs), ff // seq
    cuts = 3

    def body(place_ref, hid_ref, gi_ref, mine_ref, other_ref):
        z = place_ref[1]

        def fill(targets):
            for c in range(cuts):
                first, stop = c * d // cuts, (c + 1) * d // cuts
                full = mm(hid_ref[:, first:stop], gi_ref[...], TN).astype(BF16)
                for block, at, lo, hi in shares(first, stop, rows):
                    targets[block % 2][0, (block // 2) ^ z, at : at + hi - lo, :] = full[
                        lo - first : hi - first
                    ]

        @pl.when(place_ref[0] == 0)
        def _():
            fill((mine_ref, other_ref))

        @pl.when(place_ref[0] == 1)
        def _():
            fill((other_ref, mine_ref))

    piece = pl.BlockSpec((1, zs, rows, wide), lambda i, place_ref: (i, 0, 0, 0))
    return call(
        body,
        (seq,),
        [whole((n, d)), pl.BlockSpec((n, wide), lambda i, place_ref: (0, i))],
        [piece, piece],
        [shed_specs(seq, zs, rows, wide)] * 2,
        scalars=1,
        flops=2 * n * d * ff,
        nbytes=2 * (d * ff + n * ff + n * d),
        deps=deps,
    )(place, hid, gi)


def qkv_out_grad(place, hid, att, gqkv, gb, zs, deps=()):
    n, d = hid.shape
    seq, _, wa = gqkv.shape
    wb = gb.shape[2]
    rows = d // (2 * zs)
    cuts = 3

    def body(place_ref, hid_ref, att_ref, gqkv_ref, gb_ref, mine_ref, other_ref):
        z = place_ref[1]

        def fill(targets):
            for c in range(cuts):
                first, stop = c * d // cuts, (c + 1) * d // cuts
                left = mm(hid_ref[:, first:stop], gqkv_ref[0], TN).astype(BF16)
                right = mm(att_ref[:, first:stop], gb_ref[0], TN).astype(BF16)
                full = jnp.concatenate([left, right], axis=1)
                for block, at, lo, hi in shares(first, stop, rows):
                    targets[block % 2][0, (block // 2) ^ z, at : at + hi - lo, :] = full[
                        lo - first : hi - first
                    ]

        @pl.when(place_ref[0] == 0)
        def _():
            fill((mine_ref, other_ref))

        @pl.when(place_ref[0] == 1)
        def _():
            fill((other_ref, mine_ref))

    piece = pl.BlockSpec((1, zs, rows, wa + wb), lambda i, place_ref: (i, 0, 0, 0))
    return call(
        body,
        (seq,),
        [
            whole((n, d)),
            whole((n, d)),
            pl.BlockSpec((1, n, wa), lambda i, place_ref: (i, 0, 0)),
            pl.BlockSpec((1, n, wb), lambda i, place_ref: (i, 0, 0)),
        ],
        [piece, piece],
        [shed_specs(seq, zs, rows, wa + wb)] * 2,
        scalars=1,
        flops=2 * n * d * seq * (wa + wb),
        nbytes=2 * seq * (d + n) * (wa + wb),
        deps=deps,
    )(place, hid, att, gqkv, gb)


def feed_back(gu, slope, w_down, w_up, deps=()):
    n, d = gu.shape
    ff = slope.shape[1]
    mt = fold(n, FEED_ROWS)
    last = ff // d - 1

    def body(gu_ref, slope_ref, wd_ref, wu_ref, gi_ref, bias_ref, out_ref, acc):
        f = pl.program_id(0)
        m = pl.program_id(1)
        rows = pl.ds(pl.multiple_of(m * mt, mt), mt)
        gi = (mm(gu_ref[...], wd_ref[...], NT) * slope_ref[...].astype(F32)).astype(BF16)
        gi_ref[...] = gi
        total = column_sum(gi.astype(F32))

        @pl.when(m == 0)
        def _():
            bias_ref[...] = total

        @pl.when(m > 0)
        def _():
            bias_ref[...] += total

        part = mm(gi, wu_ref[...], NT)

        @pl.when(f == 0)
        def _():
            acc[rows, :] = part

        @pl.when((f > 0) & (f < last))
        def _():
            acc[rows, :] += part

        @pl.when(f == last)
        def _():
            out_ref[...] = acc[rows, :] + part

    return call(
        body,
        (ff // d, n // mt),
        [
            pl.BlockSpec((mt, d), lambda f, m: (m, 0)),
            pl.BlockSpec((mt, d), lambda f, m: (m, f)),
            pl.BlockSpec((d, d), lambda f, m: (f, 0)),
            pl.BlockSpec((d, d), lambda f, m: (0, f)),
        ],
        [
            pl.BlockSpec((mt, d), lambda f, m: (m, f)),
            pl.BlockSpec((1, d), lambda f, m: (0, f)),
            pl.BlockSpec((mt, d), lambda f, m: (jnp.where(f == last, m, 0), 0)),
        ],
        [sds((n, ff), BF16), sds((1, ff), F32), sds((n, d), F32)],
        [pltpu.VMEM((n, d), F32)],
        flops=4 * n * d * ff,
        nbytes=2 * (2 * d * ff + 2 * n * ff + 3 * n * d),
        deps=deps,
    )(gu, slope, w_down, w_up)


def norm_back(grad, v, r, stretch):
    dn = grad * stretch
    return r * (
        dn - jnp.mean(dn, axis=-1, keepdims=True) - v * jnp.mean(dn * v, axis=-1, keepdims=True)
    )


def middle_back(gh, mid, branch, go, upd, mods, w, seq, deps=()):
    n, d = gh.shape
    mt = fold(n, 256)
    wide = d // seq

    def body(
        gh_ref, mid_ref, branch_ref, go_ref, upd_ref, mod_ref, w_ref,
        gmid_ref, gb_ref, cut_ref, ga_ref, sum_ref,
    ):
        @pl.when(pl.program_id(0) == 0)
        def _():
            sum_ref[...] = jnp.zeros_like(sum_ref)

        g = gh_ref[...]
        v, r = standard(mid_ref[...])
        sum_ref[0:1, :] += column_sum(g * v)
        sum_ref[1:2, :] += column_sum(g)
        go = go_ref[...].astype(F32)
        sum_ref[4:5, :] += column_sum(go * upd_ref[...].astype(F32))
        gmid = go + norm_back(g, v, r, 1.0 + mod_ref[4:5, :])
        gmid_ref[...] = gmid
        sum_ref[2:3, :] += column_sum(gmid * branch_ref[...].astype(F32))
        low = (mod_ref[2:3, :] * gmid).astype(BF16)
        gb_ref[...] = low
        for s in range(seq):
            cut_ref[s] = low[:, s * wide : (s + 1) * wide]
        sum_ref[3:4, :] += column_sum(low.astype(F32))
        ga_ref[...] = mm(low, w_ref[...], NT).astype(BF16)

    tile = pl.BlockSpec((mt, d), lambda m: (m, 0))
    return call(
        body,
        (n // mt,),
        [tile, tile, tile, tile, tile, whole((8, d)), whole((d, d))],
        [tile, tile, pl.BlockSpec((seq, mt, wide), lambda m: (0, m, 0)), tile, whole((8, d))],
        [
            sds((n, d), F32),
            sds((n, d), BF16),
            sds((seq, n, wide), BF16),
            sds((n, d), BF16),
            sds((8, d), F32),
        ],
        flops=2 * n * d * d,
        nbytes=2 * (d * d + 11 * n * d),
        deps=deps,
    )(gh, mid, branch, go, upd, mods, w)


def attention_back(qkv, ga, lse, temporal, seq, deps=()):
    a, g, p, wide = qkv.shape
    d = wide // 3
    size = d // HEADS
    t = a * p
    scale = size ** (-0.5)
    cut = wide // seq

    def body(qkv_ref, ga_ref, lse_ref, out_ref, cut_ref, sum_ref, acc):
        acc[...] = jnp.zeros_like(acc)
        if temporal:
            ki = lax.broadcasted_iota(jnp.int32, (t, t), 0)
            qi = lax.broadcasted_iota(jnp.int32, (t, t), 1)
            same = lax.rem(qi, p) == lax.rem(ki, p)
        for h in range(HEADS):
            lo, hi, off = window(h, size, d)
            keep = head_mask(lo, hi, off, size, t)
            q = qkv_ref[:, 0, :, lo:hi].reshape(t, hi - lo)
            k = qkv_ref[:, 0, :, d + lo : d + hi].reshape(t, hi - lo)
            v = qkv_ref[:, 0, :, 2 * d + lo : 2 * d + hi].reshape(t, hi - lo)
            o = ga_ref[:, 0, :, lo:hi].reshape(t, hi - lo)
            zero = jnp.zeros_like(q)
            q, o = jnp.where(keep, q, zero), jnp.where(keep, o, zero)
            s = mm(k, q, NT) * scale
            probs = jnp.exp(s - lse_ref[0, h : h + 1, :])
            if temporal:
                probs = jnp.where(same, probs, 0.0)
            dp = mm(v, o, NT)
            acc[:, 2 * d + lo : 2 * d + hi] += mm(probs.astype(BF16), o)
            ds = (probs * (dp - column_sum(probs * dp))).astype(BF16)
            acc[:, d + lo : d + hi] += mm(ds, q) * scale
            acc[:, lo:hi] += mm(ds, jnp.where(keep, k, zero), TN) * scale
        low = acc[...].astype(BF16)
        out_ref[...] = low.reshape(a, 1, p, wide)
        for s in range(seq):
            cut_ref[s] = low[:, s * cut : (s + 1) * cut].reshape(a, 1, p, cut)
        total = column_sum(low.astype(F32))

        @pl.when(pl.program_id(0) == 0)
        def _():
            sum_ref[...] = total

        @pl.when(pl.program_id(0) > 0)
        def _():
            sum_ref[...] += total

    return call(
        body,
        (g,),
        [
            pl.BlockSpec((a, 1, p, wide), lambda i: (0, i, 0, 0)),
            pl.BlockSpec((a, 1, p, d), lambda i: (0, i, 0, 0)),
            pl.BlockSpec((1, HEADS, t), lambda i: (i, 0, 0)),
        ],
        [
            pl.BlockSpec((a, 1, p, wide), lambda i: (0, i, 0, 0)),
            pl.BlockSpec((seq, a, 1, p, cut), lambda i: (0, 0, i, 0, 0)),
            whole((1, wide)),
        ],
        [sds((a, g, p, wide), BF16), sds((seq, a, g, p, cut), BF16), sds((1, wide), F32)],
        [pltpu.VMEM((t, wide), F32)],
        flops=12 * g * HEADS * t * t * 256,
        nbytes=2 * a * g * p * (3 * wide + d),
        deps=deps,
    )(qkv, ga, lse)


def stream_back(gqkv, w, x, gmid, mods, out_dtype, deps=()):
    n, wide = gqkv.shape
    d = w.shape[0]
    mt = fold(n, 256)

    def body(g_ref, w_ref, x_ref, gmid_ref, mod_ref, out_ref, sum_ref):
        @pl.when(pl.program_id(0) == 0)
        def _():
            sum_ref[...] = jnp.zeros_like(sum_ref)

        grad = mm(g_ref[...], w_ref[...], NT)
        v, r = standard(x_ref[...].astype(F32))
        sum_ref[0:1, :] += column_sum(grad * v)
        sum_ref[1:2, :] += column_sum(grad)
        out_ref[...] = (gmid_ref[...] + norm_back(grad, v, r, 1.0 + mod_ref[1:2, :])).astype(
            out_dtype
        )

    tile = pl.BlockSpec((mt, d), lambda m: (m, 0))
    return call(
        body,
        (n // mt,),
        [
            pl.BlockSpec((mt, wide), lambda m: (m, 0)),
            whole((d, wide)),
            tile,
            tile,
            whole((8, d)),
        ],
        [tile, whole((8, d))],
        [sds((n, d), out_dtype), sds((8, d), F32)],
        flops=2 * n * d * wide,
        nbytes=2 * (d * wide + n * wide + 5 * n * d),
        deps=deps,
    )(gqkv, w, x, gmid, mods)


def add_pieces(left, right, deps=()):
    seq, zs, rows, d = left.shape

    def body(left_ref, right_ref, out_ref):
        out_ref[...] = (left_ref[...].astype(F32) + right_ref[...].astype(F32)).astype(BF16)

    piece = pl.BlockSpec((1, zs, rows, d), lambda i: (i, 0, 0, 0))
    return call(
        body,
        (seq,),
        [piece, piece],
        piece,
        sds(left.shape, BF16),
        nbytes=6 * seq * zs * rows * d,
        deps=deps,
    )(left, right)


def join_qkv_out(place, own, got, deps=()):
    seq, zs, rows, d = own.shape
    wide = d * 3 // 4

    def body(place_ref, own_ref, got_ref, qkv_ref, out_ref):
        def put(c, src):
            span = slice(c * rows, (c + 1) * rows)
            qkv_ref[span, :] = jnp.concatenate([src[s, 0, :, :wide] for s in range(seq)], axis=1)
            out_ref[span, :] = jnp.concatenate([src[s, 0, :, wide:] for s in range(seq)], axis=1)

        for c in range(2):

            @pl.when(place_ref[0] == c)
            def _(c=c):
                put(c, own_ref)
                put(1 - c, got_ref)

    piece = pl.BlockSpec((seq, 1, rows, d), lambda i, place_ref: (0, i ^ place_ref[1], 0, 0))
    return call(
        body,
        (zs,),
        [piece, piece],
        [
            pl.BlockSpec((2 * rows, seq * wide), lambda i, place_ref: (i, 0)),
            pl.BlockSpec((2 * rows, d), lambda i, place_ref: (i, 0)),
        ],
        [sds((2 * rows * zs, seq * wide), BF16), sds((2 * rows * zs, d), BF16)],
        scalars=1,
        nbytes=8 * seq * zs * rows * d,
        deps=deps,
    )(place, own, got)


def join_up(place, own, got, deps=()):
    seq, zs, rows, d = own.shape

    def body(place_ref, own_ref, got_ref, up_ref):
        for c in range(2):

            @pl.when(place_ref[0] == c)
            def _(c=c):
                for s in range(seq):
                    cols = slice(s * d, (s + 1) * d)
                    up_ref[c * rows : (c + 1) * rows, cols] = own_ref[s, 0]
                    up_ref[(1 - c) * rows : (2 - c) * rows, cols] = got_ref[s, 0]

    piece = pl.BlockSpec((seq, 1, rows, d), lambda i, place_ref: (0, i ^ place_ref[1], 0, 0))
    return call(
        body,
        (zs,),
        [piece, piece],
        pl.BlockSpec((2 * rows, seq * d), lambda i, place_ref: (i, 0)),
        sds((2 * rows * zs, seq * d), BF16),
        scalars=1,
        nbytes=8 * seq * zs * rows * d,
        deps=deps,
    )(place, own, got)


def join_down(place, own, got, deps=()):
    seq, zs, rows, d = own.shape
    quarter = d // seq
    parts = d // quarter

    def body(place_ref, own_ref, got_ref, down_ref):
        def put(c, src):
            for q in range(parts):
                base = (c * parts + q) * rows
                cols = slice(q * quarter, (q + 1) * quarter)
                down_ref[base : base + rows, :] = jnp.concatenate(
                    [src[s, 0, :, cols] for s in range(seq)], axis=1
                )

        for c in range(2):

            @pl.when(place_ref[0] == c)
            def _(c=c):
                put(c, own_ref)
                put(1 - c, got_ref)

    piece = pl.BlockSpec((seq, 1, rows, d), lambda i, place_ref: (0, i ^ place_ref[1], 0, 0))
    return call(
        body,
        (zs,),
        [piece, piece],
        pl.BlockSpec((2 * parts * rows, d), lambda i, place_ref: (i, 0)),
        sds((2 * parts * rows * zs, d), BF16),
        scalars=1,
        nbytes=8 * seq * zs * rows * d,
        deps=deps,
    )(place, own, got)


clip_limit = 8.0
CLIP = ("z", "core")


def hop(x, distance, count):
    return lax.ppermute(x, CLIP, [(i, i ^ distance) for i in range(count)])


def on_device(
    video_latents,
    conditioning,
    ada_weight,
    ada_bias,
    qkv_weight,
    out_weight,
    up_weight,
    down_weight,
    attention_bias,
    up_bias,
    down_bias,
    cotangent,
    *,
    clips,
    seq,
):
    zs = clips // 2
    layers, rows, own_columns = qkv_weight.shape
    d = video_latents.shape[-1]
    frames, places = video_latents.shape[1:3]
    n = frames * places
    ff = up_bias.shape[1]
    clip_index = lax.axis_index(CLIP)
    place = jnp.stack([clip_index % 2, clip_index // 2]).astype(jnp.int32)
    packed = zs == 4 and rows % 16 == 0 and down_weight.shape[1] % rows == 0 and d % seq == 0
    cuts = seq if packed else 1

    every_condition = lax.all_gather(conditioning, CLIP, axis=0, tiled=True)
    squashed = jax.nn.silu(every_condition).astype(BF16)
    local_mods = (
        jnp.einsum("kd,ldc->klc", squashed, ada_weight, preferred_element_type=F32)
        + ada_bias[None, :, :]
    )
    own_mods = lax.all_to_all(local_mods, CLIP, 0, 0, tiled=True)
    every_mod = lax.all_gather(own_mods, "seq", axis=0, tiled=False)
    modulation = every_mod.transpose(2, 1, 0, 3).reshape(layers, 6, d)
    modulation = jnp.pad(modulation, ((0, 0), (0, 2), (0, 0)))

    def pair_of(block, got):
        return jnp.concatenate([block[None], got[None]], axis=0)

    def line_of(pair, got):
        return jnp.concatenate([pair, got], axis=0)

    def pack_rows(layer):
        tall = down_weight[layer].reshape(-1, rows, d // seq)
        return (
            jnp.concatenate([qkv_weight[layer], out_weight[layer]], axis=1),
            up_weight[layer],
            tall.transpose(1, 0, 2).reshape(rows, d),
        )

    def along_seq(blocks):
        return lax.all_gather(blocks, "seq", axis=0, tiled=False)

    def both_cores(own, deps):
        own = gate(own, deps)
        return own, hop(own, 1, clips)

    def fetch_natural(layer):
        return tuple(
            lax.all_gather(
                lax.all_gather(item[layer], CLIP, axis=0, tiled=True), "seq", axis=1, tiled=True
            )
            for item in (qkv_weight, out_weight, up_weight, down_weight)
        )

    def reduce_seq(half):
        flat = lax.psum_scatter(half.reshape(-1, d), "seq", scatter_dimension=0, tiled=True)
        return flat.reshape(zs, rows, d)

    def far_half(part):
        return hop(part[2:], 4, clips)

    def add_far(part, got):
        return (part[:2].astype(F32) + got.astype(F32)).astype(BF16)

    def near_half(part):
        return hop(part[1], 2, clips)

    def add_near(part, got):
        return part[0].astype(F32) + got.astype(F32)

    def shed_natural(left, right):
        full = mm(left, right, TN).astype(BF16)
        part = lax.psum_scatter(full, "seq", scatter_dimension=1, tiled=True)
        return lax.psum_scatter(part, CLIP, scatter_dimension=0, tiled=True).astype(F32)

    def swap_tokens(x):
        block = x.reshape(seq, n // seq, d)
        return lax.all_to_all(block, "seq", 0, 0, tiled=True).reshape(n, d)

    def by_places(x):
        return x.reshape(frames, seq, places // seq, d).transpose(1, 0, 2, 3).reshape(n, d)

    def by_frames(x):
        return (
            x.reshape(seq, frames, places // seq, d)
            .transpose(1, 0, 2, 3)
            .reshape(1, frames, places, d)
        )

    shapes = (
        (seq, frames, places // seq),
        (seq * frames, places // seq // 16, 16),
    )

    def qkv_bias_of(layer):
        bias = attention_bias[layer]
        return jnp.concatenate([bias[0], jnp.zeros_like(bias[0]), bias[1]])[None]

    def forward_natural(layer, x):
        mods = modulation[layer]
        qkv_full, out_full, up_full, down_full = fetch_natural(layer)
        hidden, qkv = qkv_forward(x, mods, qkv_full, qkv_bias_of(layer))
        qkv = qkv.reshape(shapes[layer] + (3 * d,))
        attended, lse, peak = attention_forward(qkv, layer == 1)
        attended = attended.reshape(n, d)
        out_bias = attention_bias[layer, 2:3]
        branch, middle, hidden_two = out_forward(attended, x, mods, out_full, out_bias)
        active, slope = up_forward(hidden_two, up_full, up_bias[layer : layer + 1])
        update, result = down_forward(
            active, middle, mods, down_full, down_bias[layer : layer + 1]
        )
        kept = (x, hidden, qkv, lse, attended, branch, middle, hidden_two, active, slope, update)
        weights = (qkv_full, out_full, up_full, down_full)
        return result, kept, weights, jnp.max(peak, axis=(0, 1))

    def backward_natural(layer, grad_out, kept, weights):
        x, hidden, qkv, lse, attended, branch, middle, hidden_two, active, slope, update = kept
        qkv_full, out_full, up_full, down_full = weights
        mods = modulation[layer]
        grad_update, update_sums = update_back(grad_out, mods)
        inner_grad, up_sums, hidden_grad = feed_back(grad_update, slope, down_full, up_full)
        middle_grad, branch_grad, _, attended_grad, middle_sums = middle_back(
            hidden_grad, middle, branch, grad_out, update, mods, out_full, 1
        )
        qkv_grad, _, qkv_sums = attention_back(
            qkv, attended_grad.reshape(shapes[layer] + (d,)), lse, layer == 1, 1
        )
        qkv_grad = qkv_grad.reshape(n, 3 * d)
        stream_grad, stream_sums = stream_back(
            qkv_grad, qkv_full, x, middle_grad, mods, BF16 if layer == 1 else F32
        )
        parts = (
            shed_natural(hidden, qkv_grad),
            shed_natural(attended, branch_grad),
            shed_natural(hidden_two, inner_grad),
            shed_natural(active, grad_update),
        )
        return stream_grad, (stream_sums, middle_sums, update_sums, qkv_sums, up_sums), parts

    def mod_rows(sums):
        stream_sums, middle_sums, _, _, _ = sums
        return jnp.concatenate(
            [
                stream_sums[1:2],
                stream_sums[0:1],
                middle_sums[2:3],
                middle_sums[1:2],
                middle_sums[0:1],
                middle_sums[4:5],
            ],
            axis=0,
        )

    def bias_rows_of(sums):
        _, middle_sums, update_sums, qkv_sums, up_sums = sums
        return jnp.concatenate(
            [
                qkv_sums[:, :d],
                qkv_sums[:, 2 * d :],
                middle_sums[3:4],
                update_sums[0:1],
                up_sums.reshape(-1, d),
            ],
            axis=0,
        )

    def unpack(parts):
        down_g, up_g, both = parts
        down_g = down_g.reshape(rows, -1, d // seq).transpose(1, 0, 2).reshape(-1, d // seq)
        return both[:, :own_columns], both[:, own_columns:], up_g, down_g

    def run_natural():
        first_in = by_places(video_latents)
        second_go = swap_tokens(by_places(cotangent))
        first_out, first_kept, first_weights, first_peak = forward_natural(0, first_in)
        second_in = swap_tokens(first_out)
        second_out, second_kept, second_weights, second_peak = forward_natural(1, second_in)
        second_grad, second_sums, second_parts = backward_natural(
            1, second_go, second_kept, second_weights
        )
        first_grad, first_sums, first_parts = backward_natural(
            0, swap_tokens(second_grad), first_kept, first_weights
        )
        peaks = (first_peak, second_peak)
        sums = (first_sums, second_sums)
        second_out = swap_tokens(second_out)
        return second_out, first_grad, peaks, sums, first_parts, second_parts

    def run_packed():
        first_pack, second_pack = pack_rows(0), pack_rows(1)
        first_in = by_places(video_latents)
        second_go = swap_tokens(by_places(cotangent))

        pair = pair_of(first_pack[0], hop(first_pack[0], 2, clips))
        line_q0 = line_of(pair, gate(hop(pair, 4, clips), (second_go,)))
        block = gate(first_pack[1], (line_q0,))
        pair = pair_of(block, hop(block, 2, clips))
        line_u0 = line_of(pair, gate(hop(pair, 4, clips), (modulation,)))
        block = gate(first_pack[2], (line_u0,))
        pair_d0 = pair_of(block, hop(block, 2, clips))
        whole_q0, whole_u0 = along_seq(line_q0), along_seq(line_u0)

        def attention_part(layer, x, qkv, out_full):
            qkv = qkv.reshape(shapes[layer] + (3 * d,))
            attended, lse, peak = attention_forward(qkv, layer == 1)
            return qkv, attended.reshape(n, d), lse, jnp.max(peak, axis=(0, 1))

        mods = modulation[0]
        qkv_full, out_full = join_qkv_out(place, *both_cores(whole_q0, (pair_d0,)))
        hidden, qkv = qkv_forward(first_in, mods, qkv_full, qkv_bias_of(0))
        hidden, qkv, got = joint(hidden, qkv, hop(pair_d0, 4, clips))
        line_d0 = line_of(pair_d0, got)
        block_q1 = gate(second_pack[0], (hidden,))
        qkv, attended, lse, peak0 = attention_part(0, first_in, qkv, out_full)
        attended, lse, got = joint(attended, lse, hop(block_q1, 2, clips))
        pair_q1 = pair_of(block_q1, got)
        block_u1, block_d1 = gate(second_pack[1], (attended,)), gate(second_pack[2], (attended,))
        branch, middle, hidden_two = out_forward(
            attended, first_in, mods, out_full, attention_bias[0, 2:3]
        )
        branch, middle, hidden_two, got, got2 = joint(
            branch, middle, hidden_two, hop(block_u1, 2, clips), hop(block_d1, 2, clips)
        )
        pair_u1, pair_d1 = pair_of(block_u1, got), pair_of(block_d1, got2)
        whole_d0 = along_seq(line_d0)
        up_full = join_up(
            place, *both_cores(whole_u0, (branch,)), deps=(pair_q1, pair_u1, pair_d1, line_d0)
        )
        active, slope = up_forward(hidden_two, up_full, up_bias[:1])
        active, slope, got = joint(active, slope, hop(pair_q1, 4, clips))
        line_q1 = line_of(pair_q1, got)
        whole_q1 = along_seq(line_q1)
        down_full = join_down(place, *both_cores(whole_d0, (active,)), deps=(line_q1,))
        update, result = down_forward(active, middle, mods, down_full, down_bias[:1])
        update, result, got = joint(update, result, hop(pair_u1, 4, clips))
        line_u1 = line_of(pair_u1, got)
        whole_u1 = along_seq(line_u1)
        kept0 = (
            first_in, hidden, qkv, lse, attended, branch, middle, hidden_two, active, slope, update
        )
        weights0 = (qkv_full, out_full, up_full, down_full)
        second_in, got = joint(swap_tokens(result), hop(gate(pair_d1, (line_u1,)), 4, clips))
        line_d1 = line_of(pair_d1, got)
        whole_d1 = along_seq(line_d1)

        mods = modulation[1]
        qkv_full, out_full = join_qkv_out(
            place, *both_cores(whole_q1, (result, line_u1))
        )
        hidden, qkv = qkv_forward(second_in, mods, qkv_full, qkv_bias_of(1))
        qkv, attended, lse, peak1 = attention_part(1, second_in, qkv, out_full)
        branch, middle, hidden_two = out_forward(
            attended, second_in, mods, out_full, attention_bias[1, 2:3]
        )
        up_full = join_up(place, *both_cores(whole_u1, (branch,)))
        active, slope = up_forward(hidden_two, up_full, up_bias[1:2])
        grad_update, update_sums1 = update_back(second_go, mods, deps=(active,))
        own, got = both_cores(whole_d1, (grad_update,))
        down_m, down_o = down_grad(place, active, grad_update, seq, zs, deps=(own,))
        down_m, down_o, got = joint(down_m, down_o, got)
        down_full = join_down(place, own, got)
        half_d1 = add_pieces(down_m, hop(down_o, 1, clips), deps=(down_full,))
        part_d1 = reduce_seq(half_d1)
        update, result = down_forward(
            active, middle, mods, down_full, down_bias[1:2], deps=(half_d1,)
        )
        kept1 = (
            second_in, hidden, qkv, lse, attended, branch, middle, hidden_two, active, slope, update
        )
        weights1 = (qkv_full, out_full, up_full, down_full)
        kept, weights = (kept0, kept1), (weights0, weights1)

        def up_stage(layer, hidden_grad, inner_grad, grad_out, deps):
            _, _, _, _, _, branch, middle, hidden_two, _, _, update = kept[layer]
            up_m, up_o = up_grad(place, hidden_two, inner_grad, seq, zs, deps=deps)
            middle_grad, _, branch_cut, attended_grad, middle_sums = middle_back(
                hidden_grad, middle, branch, grad_out, update, modulation[layer],
                weights[layer][1], cuts, deps=(up_m,),
            )
            half_u = add_pieces(up_m, hop(up_o, 1, clips), deps=(middle_grad,))
            return half_u, reduce_seq(half_u), middle_grad, branch_cut, attended_grad, middle_sums

        def attention_stage(layer, attended_grad, deps):
            _, _, qkv, lse = kept[layer][:4]
            grad = attended_grad.reshape(shapes[layer] + (d,))
            qkv_grad, qkv_cut, qkv_sums = attention_back(
                qkv, grad, lse, layer == 1, cuts, deps=deps
            )
            return qkv_grad.reshape(n, 3 * d), qkv_cut.reshape(seq, n, -1), qkv_sums

        def last_grad(layer, qkv_cut, branch_cut, deps):
            hidden, attended = kept[layer][1], kept[layer][4]
            return qkv_out_grad(place, hidden, attended, qkv_cut, branch_cut, zs, deps=deps)

        inner_grad, up_sums, hidden_grad = feed_back(
            grad_update, kept1[9], weights1[3], weights1[2], deps=(result,)
        )
        inner_grad, hidden_grad, second_out = joint(inner_grad, hidden_grad, swap_tokens(result))
        half_u, part_u1, middle_grad, branch_cut, attended_grad, middle_sums = up_stage(
            1, hidden_grad, inner_grad, second_go, ()
        )
        qkv_grad, qkv_cut, qkv_sums = attention_stage(1, attended_grad, (half_u, part_d1))
        qkv_grad, qkv_cut, got = joint(qkv_grad, qkv_cut, far_half(part_d1))
        sum_d1 = add_far(part_d1, got)
        stream_grad, stream_sums = stream_back(
            qkv_grad, weights1[0], kept1[0], middle_grad, modulation[1], BF16
        )
        stream_grad, stream_sums, got = joint(stream_grad, stream_sums, near_half(sum_d1))
        down_g1 = add_near(sum_d1, got)
        second_sums = (stream_sums, middle_sums, update_sums1, qkv_sums, up_sums)
        last_m, last_o = last_grad(1, qkv_cut, branch_cut, (stream_grad,))
        last_m, last_o, first_go = joint(last_m, last_o, swap_tokens(stream_grad))

        grad_update, update_sums = update_back(first_go, modulation[0])
        half_q1 = add_pieces(last_m, hop(last_o, 1, clips), deps=(grad_update,))
        part_q1 = reduce_seq(half_q1)
        down_m, down_o = down_grad(place, kept0[8], grad_update, seq, zs, deps=(half_q1,))
        inner_grad, up_sums, hidden_grad = feed_back(
            grad_update, kept0[9], weights0[3], weights0[2], deps=(down_m, part_u1)
        )
        inner_grad, hidden_grad, got = joint(inner_grad, hidden_grad, far_half(part_u1))
        sum_u1 = add_far(part_u1, got)
        half_d0 = add_pieces(down_m, hop(down_o, 1, clips), deps=(hidden_grad, part_q1))
        part_d0 = reduce_seq(half_d0)
        half_u, part_u0, middle_grad, branch_cut, attended_grad, middle_sums = up_stage(
            0, hidden_grad, inner_grad, first_go, (half_d0, sum_u1)
        )
        qkv_grad, qkv_cut, qkv_sums = attention_stage(0, attended_grad, (half_u,))
        qkv_grad, qkv_cut, got, got2 = joint(
            qkv_grad, qkv_cut, far_half(part_q1), near_half(sum_u1)
        )
        sum_q1 = add_far(part_q1, got)
        up_g1 = add_near(sum_u1, got2)
        last_m, last_o = last_grad(0, qkv_cut, branch_cut, (part_d0, sum_q1))
        last_m, last_o, got, got2 = joint(last_m, last_o, far_half(part_d0), near_half(sum_q1))
        sum_d0 = add_far(part_d0, got)
        both_g1 = add_near(sum_q1, got2)
        first_grad, stream_sums = stream_back(
            qkv_grad, weights0[0], kept0[0], middle_grad, modulation[0], F32, deps=(last_m, sum_d0)
        )
        first_grad, stream_sums, got, got2 = joint(
            first_grad, stream_sums, near_half(sum_d0), far_half(part_u0)
        )
        down_g0 = add_near(sum_d0, got)
        sum_u0 = add_far(part_u0, got2)
        first_sums = (stream_sums, middle_sums, update_sums, qkv_sums, up_sums)
        half = add_pieces(last_m, hop(last_o, 1, clips), deps=(first_grad,))
        part_q0 = reduce_seq(half)
        up_g0 = add_near(sum_u0, near_half(sum_u0))
        part_q0 = gate(part_q0, (up_g0,))
        sum_q0 = add_far(part_q0, far_half(part_q0))
        both_g0 = add_near(sum_q0, near_half(sum_q0))
        sums = (first_sums, second_sums)
        first_parts = unpack((down_g0, up_g0, both_g0))
        second_parts = unpack((down_g1, up_g1, both_g1))
        return second_out, first_grad, (peak0, peak1), sums, first_parts, second_parts

    run = run_packed if packed else run_natural
    second_out, latents_grad, peaks, sums, first_shed, second_shed = run()
    output_latents = by_frames(second_out)

    def total(v, *axes):
        for axis, count in axes:
            step = 1
            while step < count:
                v = v + lax.ppermute(v, axis, [(i, i ^ step) for i in range(count)])
                step *= 2
        return v

    mod_grads = total(jnp.stack([mod_rows(sums[0]), mod_rows(sums[1])]), ("seq", seq))
    mod_grads = mod_grads.reshape(layers, clips, seq, -1)
    of_columns = lax.dynamic_index_in_dim(mod_grads, lax.axis_index("seq"), 2, keepdims=False)
    own_mod_grad = lax.all_to_all(of_columns.transpose(1, 0, 2), CLIP, 0, 0, tiled=True)
    ada_bias_grad = jnp.sum(own_mod_grad, axis=0)
    rounded_mod = own_mod_grad.astype(BF16)
    ada_weight_grad = jnp.einsum("kd,klc->ldc", squashed, rounded_mod, preferred_element_type=F32)
    squash_part = jnp.einsum("klc,ldc->kd", rounded_mod, ada_weight, preferred_element_type=F32)
    bias_sums = [bias_rows_of(sums[0]), bias_rows_of(sums[1])]
    bias_rows = bias_sums[0].shape[0]
    devices = clips * seq
    device = clip_index * seq + lax.axis_index("seq")
    peak_rows = -(-devices * layers * HEADS // d)
    own_peaks = jnp.concatenate(peaks)[None]
    placed = lax.dynamic_update_slice(
        jnp.zeros((devices, layers * HEADS), F32), own_peaks, (device, 0)
    ).reshape(-1)
    placed = jnp.pad(placed, (0, peak_rows * d - placed.shape[0])).reshape(peak_rows, d)
    summed = total(
        jnp.concatenate([*bias_sums, squash_part, placed], axis=0), (CLIP, clips), ("seq", seq)
    )
    bias_sums = summed[: 2 * bias_rows].reshape(layers, bias_rows, d)
    own_squash = lax.dynamic_slice_in_dim(summed, 2 * bias_rows + clip_index, 1, axis=0)
    peaks = summed[2 * bias_rows + clips :].reshape(-1)[: devices * layers * HEADS]
    logit_peak = jnp.max(peaks.reshape(devices, layers, HEADS), axis=0)
    column_index = lax.axis_index("seq") * own_columns + jnp.arange(own_columns, dtype=jnp.int32)
    head_of = column_index % d // (d // HEADS)
    head_match = (head_of[:, None] == jnp.arange(HEADS, dtype=jnp.int32)[None, :]).astype(F32)
    roots = jnp.sqrt(clip_limit / jnp.maximum(logit_peak, clip_limit))
    column_roots = jnp.sum(roots[:, None, :] * head_match[None, :, :], axis=-1)
    column_scale = jnp.where(column_index[None, :] < 2 * d, column_roots, 1.0)
    clipped_qkv = qkv_weight.astype(F32) * column_scale[:, None, :]
    silu_value, silu_pull = jax.vjp(jax.nn.silu, conditioning)
    conditioning_grad = silu_pull(own_squash)[0]
    return (
        output_latents,
        latents_grad.reshape(seq, frames, places // seq, d)
        .transpose(1, 0, 2, 3)
        .reshape(1, frames, places, d),
        conditioning_grad,
        ada_weight_grad,
        ada_bias_grad,
        jnp.stack([first_shed[0], second_shed[0]]),
        jnp.stack([first_shed[1], second_shed[1]]),
        jnp.stack([first_shed[2], second_shed[2]]),
        jnp.stack([first_shed[3], second_shed[3]]),
        bias_sums[:, :3],
        bias_sums[:, 4:].reshape(layers, ff),
        bias_sums[:, 3],
        clipped_qkv,
        logit_peak,
    )


def solution(mesh):
    clips, seq = mesh.shape["clip"], mesh.shape["seq"]
    finer = jax.sharding.Mesh(
        mesh.devices.reshape(clips // 2, 2, seq), ("z", "core", "seq")
    )
    every = (*CLIP, "seq")
    tokens = P(CLIP, "seq", None, None)
    matrix = P(None, CLIP, "seq")
    return jax.shard_map(
        partial(on_device, clips=clips, seq=seq),
        mesh=finer,
        in_specs=(
            tokens,
            P(CLIP, None),
            P(None, None, every),
            P(None, every),
            matrix,
            matrix,
            matrix,
            matrix,
            P(),
            P(),
            P(),
            tokens,
        ),
        out_specs=(
            tokens,
            tokens,
            P(CLIP, None),
            P(None, None, every),
            P(None, every),
            matrix,
            matrix,
            matrix,
            matrix,
            P(),
            P(),
            P(),
            matrix,
            P(),
        ),
        check_vma=False,
    )
```

```python
from functools import partial

import jax
import jax.numpy as jnp
from jax import lax
from jax.experimental import pallas as pl
from jax.experimental.pallas import tpu as pltpu
from jax.sharding import PartitionSpec as P

HEADS = 16
F32 = jnp.float32
BF16 = jnp.bfloat16
NN = (((1,), (0,)), ((), ()))
NT = (((1,), (1,)), ((), ()))
TN = (((0,), (0,)), ((), ()))
VMEM_BYTES = 56 * 1024 * 1024
FEED_ROWS = 1024
UP_ROWS, UP_CUTS = 1024, 1
QKV_ROWS = 512


def mm(a, b, dims=NN):
    return lax.dot_general(a, b, dims, preferred_element_type=F32)


def call(
    body, grid, in_specs, out_specs, out_shape, scratch=(), scalars=0, flops=0, nbytes=0, deps=()
):
    first = scalars + len(in_specs)

    def run(*refs):
        body(*refs[:first], *refs[first + len(deps) :])

    kernel = pl.pallas_call(
        run,
        grid_spec=pltpu.PrefetchScalarGridSpec(
            num_scalar_prefetch=scalars,
            grid=grid,
            in_specs=[*in_specs, *[pl.BlockSpec(memory_space=pl.ANY)] * len(deps)],
            out_specs=out_specs,
            scratch_shapes=list(scratch),
        ),
        out_shape=out_shape,
        compiler_params=pltpu.CompilerParams(
            dimension_semantics=("arbitrary",) * len(grid), vmem_limit_bytes=VMEM_BYTES
        ),
        cost_estimate=pl.CostEstimate(flops=flops, bytes_accessed=nbytes, transcendentals=0),
    )
    return lambda *args: kernel(*args, *deps)


def gate(x, deps):
    def body(*refs):
        pass

    anywhere = pl.BlockSpec(memory_space=pl.ANY)
    return pl.pallas_call(
        body,
        in_specs=[anywhere] * (1 + len(deps)),
        out_specs=anywhere,
        out_shape=sds(x.shape, x.dtype),
        input_output_aliases={0: 0},
    )(x, *deps)


def joint(*arrays):
    def body(*refs):
        pass

    anywhere = pl.BlockSpec(memory_space=pl.ANY)
    return pl.pallas_call(
        body,
        in_specs=[anywhere] * len(arrays),
        out_specs=[anywhere] * len(arrays),
        out_shape=[sds(x.shape, x.dtype) for x in arrays],
        input_output_aliases={k: k for k in range(len(arrays))},
    )(*arrays)


def whole(shape):
    return pl.BlockSpec(shape, lambda *_: (0,) * len(shape))


def sds(shape, dtype):
    return jax.ShapeDtypeStruct(shape, dtype)


def standard(x):
    centred = x - jnp.mean(x, axis=-1, keepdims=True)
    r = lax.rsqrt(jnp.mean(centred * centred, axis=-1, keepdims=True) + 1e-06)
    return centred * r, r


def fold(n, limit=512):
    return min(n, limit)


def qkv_forward(x, mods, w, bias, deps=()):
    n, d = x.shape
    wide = w.shape[1]
    mt = fold(n, QKV_ROWS)

    def body(x_ref, mod_ref, w_ref, b_ref, hid_ref, out_ref):
        m = pl.program_id(1)
        rows = pl.ds(pl.multiple_of(m * mt, mt), mt)

        @pl.when(pl.program_id(0) == 0)
        def _():
            v, _ = standard(x_ref[...].astype(F32))
            hid_ref[rows, :] = (v * (1.0 + mod_ref[1:2, :]) + mod_ref[0:1, :]).astype(BF16)

        out_ref[...] = (mm(hid_ref[rows, :], w_ref[...]) + b_ref[...]).astype(BF16)

    return call(
        body,
        (wide // d, n // mt),
        [
            pl.BlockSpec((mt, d), lambda j, m: (jnp.where(j == 0, m, n // mt - 1), 0)),
            whole((8, d)),
            pl.BlockSpec((d, d), lambda j, m: (0, j)),
            pl.BlockSpec((1, d), lambda j, m: (0, j)),
        ],
        [whole((n, d)), pl.BlockSpec((mt, d), lambda j, m: (m, j))],
        [sds((n, d), BF16), sds((n, wide), BF16)],
        flops=2 * n * d * wide,
        nbytes=2 * (d * wide + n * wide + 2 * n * d),
        deps=deps,
    )(x, mods, w, bias)


def window(h, size, d):
    lo = h * size
    start = lo // 128 * 128
    stop = min(-(-(lo + size) // 128) * 128, d)
    return start, stop, lo - start


def head_mask(start, stop, off, size, rows):
    lane = lax.broadcasted_iota(jnp.int32, (rows, stop - start), 1)
    return (lane >= off) & (lane < off + size)


def attention_forward(qkv, temporal, deps=()):
    a, g, p, wide = qkv.shape
    d = wide // 3
    size = d // HEADS
    t = a * p
    scale = size ** (-0.5)

    def body(qkv_ref, att_ref, lse_ref, peak_ref, acc):
        acc[...] = jnp.zeros_like(acc)
        if temporal:
            qi = lax.broadcasted_iota(jnp.int32, (t, t), 0)
            ki = lax.broadcasted_iota(jnp.int32, (t, t), 1)
            same = lax.rem(qi, p) == lax.rem(ki, p)
        tops, totals = [], []
        for h in range(HEADS):
            lo, hi, off = window(h, size, d)
            keep = head_mask(lo, hi, off, size, t)
            q = qkv_ref[:, 0, :, lo:hi].reshape(t, hi - lo)
            k = qkv_ref[:, 0, :, d + lo : d + hi].reshape(t, hi - lo)
            v = qkv_ref[:, 0, :, 2 * d + lo : 2 * d + hi].reshape(t, hi - lo)
            zero = jnp.zeros_like(q)
            s = mm(jnp.where(keep, q, zero), k, NT) * scale
            if temporal:
                s = jnp.where(same, s, -1e30)
            top = jnp.max(s, axis=-1, keepdims=True)
            e = jnp.exp(s - top)
            total = jnp.sum(e, axis=-1, keepdims=True)
            probs = (e / total).astype(BF16)
            acc[:, lo:hi] += mm(probs, jnp.where(keep, v, zero))
            tops.append(top)
            totals.append(total)
        top = jnp.concatenate(tops, axis=1)
        lse_ref[0] = (top + jnp.log(jnp.concatenate(totals, axis=1))).T
        peak_ref[...] = jnp.max(top, axis=0, keepdims=True)[None]
        att_ref[...] = acc[...].astype(BF16).reshape(a, 1, p, d)

    return call(
        body,
        (g,),
        [pl.BlockSpec((a, 1, p, wide), lambda i: (0, i, 0, 0))],
        [
            pl.BlockSpec((a, 1, p, d), lambda i: (0, i, 0, 0)),
            pl.BlockSpec((1, HEADS, t), lambda i: (i, 0, 0)),
            pl.BlockSpec((1, 1, HEADS), lambda i: (i, 0, 0)),
        ],
        [sds((a, g, p, d), BF16), sds((g, HEADS, t), F32), sds((g, 1, HEADS), F32)],
        [pltpu.VMEM((t, d), F32)],
        flops=4 * g * HEADS * t * t * 256,
        nbytes=2 * a * g * p * (wide + d),
        deps=deps,
    )(qkv)


def out_forward(att, x, mods, w, bias, deps=()):
    n, d = att.shape
    mt = fold(n, 256)

    def body(att_ref, x_ref, mod_ref, w_ref, b_ref, branch_ref, mid_ref, hid_ref):
        branch = mm(att_ref[...], w_ref[...]) + b_ref[...]
        branch_ref[...] = branch.astype(BF16)
        mid = x_ref[...].astype(F32) + mod_ref[2:3, :] * branch
        mid_ref[...] = mid
        v, _ = standard(mid)
        hid_ref[...] = (v * (1.0 + mod_ref[4:5, :]) + mod_ref[3:4, :]).astype(BF16)

    tile = pl.BlockSpec((mt, d), lambda m: (m, 0))
    return call(
        body,
        (n // mt,),
        [tile, tile, whole((8, d)), whole((d, d)), whole((1, d))],
        [tile, tile, tile],
        [sds((n, d), BF16), sds((n, d), F32), sds((n, d), BF16)],
        flops=2 * n * d * d,
        nbytes=2 * (d * d + 6 * n * d),
        deps=deps,
    )(att, x, mods, w, bias)


GELU_A = 0.7978845608028654
GELU_B = 0.044715


def up_forward(hid, w, bias, deps=()):
    n, d = hid.shape
    ff = w.shape[1]
    mt = fold(n, UP_ROWS)
    ft = d
    cuts = UP_CUTS

    def body(hid_ref, w_ref, b_ref, act_ref, slope_ref):
        for c in range(cuts):
            cols = slice(c * ft // cuts, (c + 1) * ft // cuts)
            u = mm(hid_ref[...], w_ref[:, cols]) + b_ref[:, cols]
            square = u * u
            tanh = jnp.tanh(u * (GELU_A + (GELU_A * GELU_B) * square))
            half = 0.5 + 0.5 * tanh
            act_ref[:, cols] = (u * half).astype(BF16)
            bend = GELU_A + (3.0 * GELU_A * GELU_B) * square
            slope_ref[:, cols] = (half + (u * half) * ((1.0 - tanh) * bend)).astype(BF16)

    tile = pl.BlockSpec((mt, ft), lambda f, m: (m, f))
    return call(
        body,
        (ff // ft, n // mt),
        [
            pl.BlockSpec((mt, d), lambda f, m: (m, 0)),
            pl.BlockSpec((d, ft), lambda f, m: (0, f)),
            pl.BlockSpec((1, ft), lambda f, m: (0, f)),
        ],
        [tile, tile],
        [sds((n, ff), BF16), sds((n, ff), BF16)],
        flops=2 * n * d * ff,
        nbytes=2 * (d * ff + 2 * n * ff + n * d),
        deps=deps,
    )(hid, w, bias)


def down_forward(act, mid, mods, w, bias, deps=()):
    n, ff = act.shape
    d = w.shape[1]
    mt = fold(n, 256)

    def body(act_ref, mid_ref, mod_ref, w_ref, b_ref, upd_ref, out_ref):
        upd = mm(act_ref[...], w_ref[...]) + b_ref[...]
        upd_ref[...] = upd.astype(BF16)
        out_ref[...] = (mid_ref[...] + mod_ref[5:6, :] * upd).astype(BF16)

    tile = pl.BlockSpec((mt, d), lambda m: (m, 0))
    return call(
        body,
        (n // mt,),
        [
            pl.BlockSpec((mt, ff), lambda m: (m, 0)),
            tile,
            whole((8, d)),
            whole((ff, d)),
            whole((1, d)),
        ],
        [tile, tile],
        [sds((n, d), BF16), sds((n, d), BF16)],
        flops=2 * n * d * ff,
        nbytes=2 * (d * ff + n * ff + 4 * n * d),
        deps=deps,
    )(act, mid, mods, w, bias)


def column_sum(v):
    return jnp.sum(v, axis=0, keepdims=True)


def update_back(go, mods, deps=()):
    n, d = go.shape
    mt = fold(n, 256)

    def body(go_ref, mod_ref, gu_ref, sum_ref):
        @pl.when(pl.program_id(0) == 0)
        def _():
            sum_ref[...] = jnp.zeros_like(sum_ref)

        low = (mod_ref[5:6, :] * go_ref[...].astype(F32)).astype(BF16)
        gu_ref[...] = low
        sum_ref[0:1, :] += column_sum(low.astype(F32))

    tile = pl.BlockSpec((mt, d), lambda m: (m, 0))
    return call(
        body,
        (n // mt,),
        [tile, whole((8, d))],
        [tile, whole((8, d))],
        [sds((n, d), BF16), sds((8, d), F32)],
        flops=n * d,
        nbytes=4 * n * d,
        deps=deps,
    )(go, mods)


def slot(k):
    return k % 2 * 2 + k // 2


def shed_specs(seq, zs, rows, d):
    return sds((seq, zs, rows, d), BF16)


def shares(start, stop, rows):
    found = []
    while start < stop:
        block = start // rows
        end = min(stop, (block + 1) * rows)
        found.append((block, start - block * rows, start, end))
        start = end
    return found


def down_grad(place, act, gu, seq, zs, deps=()):
    n, ff = act.shape
    d = gu.shape[1]
    rows, quarter = d // (2 * zs), d // seq
    parts = ff // (2 * zs) // rows
    cuts = 3

    def body(place_ref, act_ref, gu_ref, mine_ref, other_ref):
        def fill(targets):
            for c in range(cuts):
                first, stop = c * (ff // zs) // cuts, (c + 1) * (ff // zs) // cuts
                full = mm(act_ref[:, first:stop], gu_ref[...], TN).astype(BF16)
                for block, at, lo, hi in shares(first, stop, rows):
                    target, q = targets[block // parts], block % parts
                    for s in range(seq):
                        target[s, 0, at : at + hi - lo, q * quarter : (q + 1) * quarter] = full[
                            lo - first : hi - first, s * quarter : (s + 1) * quarter
                        ]

        @pl.when(place_ref[0] == 0)
        def _():
            fill((mine_ref, other_ref))

        @pl.when(place_ref[0] == 1)
        def _():
            fill((other_ref, mine_ref))

    piece = pl.BlockSpec((seq, 1, rows, d), lambda i, place_ref: (0, i, 0, 0))
    return call(
        body,
        (zs,),
        [
            pl.BlockSpec((n, ff // zs), lambda i, place_ref: (0, slot(i) ^ place_ref[1])),
            whole((n, d)),
        ],
        [piece, piece],
        [shed_specs(seq, zs, rows, d)] * 2,
        scalars=1,
        flops=2 * n * d * ff,
        nbytes=2 * (d * ff + n * ff + n * d),
        deps=deps,
    )(place, act, gu)


def up_grad(place, hid, gi, seq, zs, deps=()):
    n, d = hid.shape
    ff = gi.shape[1]
    rows, wide = d // (2 * zs), ff // seq
    cuts = 3

    def body(place_ref, hid_ref, gi_ref, mine_ref, other_ref):
        z = place_ref[1]

        def fill(targets):
            for c in range(cuts):
                first, stop = c * d // cuts, (c + 1) * d // cuts
                full = mm(hid_ref[:, first:stop], gi_ref[...], TN).astype(BF16)
                for block, at, lo, hi in shares(first, stop, rows):
                    targets[block % 2][0, slot((block // 2) ^ z), at : at + hi - lo, :] = full[
                        lo - first : hi - first
                    ]

        @pl.when(place_ref[0] == 0)
        def _():
            fill((mine_ref, other_ref))

        @pl.when(place_ref[0] == 1)
        def _():
            fill((other_ref, mine_ref))

    piece = pl.BlockSpec((1, zs, rows, wide), lambda i, place_ref: (i, 0, 0, 0))
    return call(
        body,
        (seq,),
        [whole((n, d)), pl.BlockSpec((n, wide), lambda i, place_ref: (0, i))],
        [piece, piece],
        [shed_specs(seq, zs, rows, wide)] * 2,
        scalars=1,
        flops=2 * n * d * ff,
        nbytes=2 * (d * ff + n * ff + n * d),
        deps=deps,
    )(place, hid, gi)


def qkv_out_grad(place, hid, att, gqkv, gb, zs, deps=()):
    n, d = hid.shape
    seq, _, wa = gqkv.shape
    wb = gb.shape[2]
    rows = d // (2 * zs)
    cuts = 3

    def body(place_ref, hid_ref, att_ref, gqkv_ref, gb_ref, mine_ref, other_ref):
        z = place_ref[1]

        def fill(targets):
            for c in range(cuts):
                first, stop = c * d // cuts, (c + 1) * d // cuts
                left = mm(hid_ref[:, first:stop], gqkv_ref[0], TN).astype(BF16)
                right = mm(att_ref[:, first:stop], gb_ref[0], TN).astype(BF16)
                full = jnp.concatenate([left, right], axis=1)
                for block, at, lo, hi in shares(first, stop, rows):
                    targets[block % 2][0, slot((block // 2) ^ z), at : at + hi - lo, :] = full[
                        lo - first : hi - first
                    ]

        @pl.when(place_ref[0] == 0)
        def _():
            fill((mine_ref, other_ref))

        @pl.when(place_ref[0] == 1)
        def _():
            fill((other_ref, mine_ref))

    piece = pl.BlockSpec((1, zs, rows, wa + wb), lambda i, place_ref: (i, 0, 0, 0))
    return call(
        body,
        (seq,),
        [
            whole((n, d)),
            whole((n, d)),
            pl.BlockSpec((1, n, wa), lambda i, place_ref: (i, 0, 0)),
            pl.BlockSpec((1, n, wb), lambda i, place_ref: (i, 0, 0)),
        ],
        [piece, piece],
        [shed_specs(seq, zs, rows, wa + wb)] * 2,
        scalars=1,
        flops=2 * n * d * seq * (wa + wb),
        nbytes=2 * seq * (d + n) * (wa + wb),
        deps=deps,
    )(place, hid, att, gqkv, gb)


def feed_back(gu, slope, w_down, w_up, deps=()):
    n, d = gu.shape
    ff = slope.shape[1]
    mt = fold(n, FEED_ROWS)
    last = ff // d - 1

    def body(gu_ref, slope_ref, wd_ref, wu_ref, gi_ref, bias_ref, out_ref, acc):
        f = pl.program_id(0)
        m = pl.program_id(1)
        rows = pl.ds(pl.multiple_of(m * mt, mt), mt)
        gi = (mm(gu_ref[...], wd_ref[...], NT) * slope_ref[...].astype(F32)).astype(BF16)
        gi_ref[...] = gi
        total = column_sum(gi.astype(F32))

        @pl.when(m == 0)
        def _():
            bias_ref[...] = total

        @pl.when(m > 0)
        def _():
            bias_ref[...] += total

        part = mm(gi, wu_ref[...], NT)

        @pl.when(f == 0)
        def _():
            acc[rows, :] = part

        @pl.when((f > 0) & (f < last))
        def _():
            acc[rows, :] += part

        @pl.when(f == last)
        def _():
            out_ref[...] = acc[rows, :] + part

    return call(
        body,
        (ff // d, n // mt),
        [
            pl.BlockSpec((mt, d), lambda f, m: (m, 0)),
            pl.BlockSpec((mt, d), lambda f, m: (m, f)),
            pl.BlockSpec((d, d), lambda f, m: (f, 0)),
            pl.BlockSpec((d, d), lambda f, m: (0, f)),
        ],
        [
            pl.BlockSpec((mt, d), lambda f, m: (m, f)),
            pl.BlockSpec((1, d), lambda f, m: (0, f)),
            pl.BlockSpec((mt, d), lambda f, m: (jnp.where(f == last, m, 0), 0)),
        ],
        [sds((n, ff), BF16), sds((1, ff), F32), sds((n, d), F32)],
        [pltpu.VMEM((n, d), F32)],
        flops=4 * n * d * ff,
        nbytes=2 * (2 * d * ff + 2 * n * ff + 3 * n * d),
        deps=deps,
    )(gu, slope, w_down, w_up)


def norm_back(grad, v, r, stretch):
    dn = grad * stretch
    return r * (
        dn - jnp.mean(dn, axis=-1, keepdims=True) - v * jnp.mean(dn * v, axis=-1, keepdims=True)
    )


def middle_back(gh, mid, branch, go, upd, mods, w, seq, deps=()):
    n, d = gh.shape
    mt = fold(n, 256)
    wide = d // seq

    def body(
        gh_ref, mid_ref, branch_ref, go_ref, upd_ref, mod_ref, w_ref,
        gmid_ref, gb_ref, cut_ref, ga_ref, sum_ref,
    ):
        @pl.when(pl.program_id(0) == 0)
        def _():
            sum_ref[...] = jnp.zeros_like(sum_ref)

        g = gh_ref[...]
        v, r = standard(mid_ref[...])
        sum_ref[0:1, :] += column_sum(g * v)
        sum_ref[1:2, :] += column_sum(g)
        go = go_ref[...].astype(F32)
        sum_ref[4:5, :] += column_sum(go * upd_ref[...].astype(F32))
        gmid = go + norm_back(g, v, r, 1.0 + mod_ref[4:5, :])
        gmid_ref[...] = gmid
        sum_ref[2:3, :] += column_sum(gmid * branch_ref[...].astype(F32))
        low = (mod_ref[2:3, :] * gmid).astype(BF16)
        gb_ref[...] = low
        for s in range(seq):
            cut_ref[s] = low[:, s * wide : (s + 1) * wide]
        sum_ref[3:4, :] += column_sum(low.astype(F32))
        ga_ref[...] = mm(low, w_ref[...], NT).astype(BF16)

    tile = pl.BlockSpec((mt, d), lambda m: (m, 0))
    return call(
        body,
        (n // mt,),
        [tile, tile, tile, tile, tile, whole((8, d)), whole((d, d))],
        [tile, tile, pl.BlockSpec((seq, mt, wide), lambda m: (0, m, 0)), tile, whole((8, d))],
        [
            sds((n, d), F32),
            sds((n, d), BF16),
            sds((seq, n, wide), BF16),
            sds((n, d), BF16),
            sds((8, d), F32),
        ],
        flops=2 * n * d * d,
        nbytes=2 * (d * d + 11 * n * d),
        deps=deps,
    )(gh, mid, branch, go, upd, mods, w)


def attention_back(qkv, ga, lse, temporal, seq, deps=()):
    a, g, p, wide = qkv.shape
    d = wide // 3
    size = d // HEADS
    t = a * p
    scale = size ** (-0.5)
    cut = wide // seq

    def body(qkv_ref, ga_ref, lse_ref, out_ref, cut_ref, sum_ref, acc):
        acc[...] = jnp.zeros_like(acc)
        if temporal:
            ki = lax.broadcasted_iota(jnp.int32, (t, t), 0)
            qi = lax.broadcasted_iota(jnp.int32, (t, t), 1)
            same = lax.rem(qi, p) == lax.rem(ki, p)
        for h in range(HEADS):
            lo, hi, off = window(h, size, d)
            keep = head_mask(lo, hi, off, size, t)
            q = qkv_ref[:, 0, :, lo:hi].reshape(t, hi - lo)
            k = qkv_ref[:, 0, :, d + lo : d + hi].reshape(t, hi - lo)
            v = qkv_ref[:, 0, :, 2 * d + lo : 2 * d + hi].reshape(t, hi - lo)
            o = ga_ref[:, 0, :, lo:hi].reshape(t, hi - lo)
            zero = jnp.zeros_like(q)
            q, o = jnp.where(keep, q, zero), jnp.where(keep, o, zero)
            s = mm(k, q, NT) * scale
            probs = jnp.exp(s - lse_ref[0, h : h + 1, :])
            if temporal:
                probs = jnp.where(same, probs, 0.0)
            dp = mm(v, o, NT)
            acc[:, 2 * d + lo : 2 * d + hi] += mm(probs.astype(BF16), o)
            ds = (probs * (dp - column_sum(probs * dp))).astype(BF16)
            acc[:, d + lo : d + hi] += mm(ds, q) * scale
            acc[:, lo:hi] += mm(ds, jnp.where(keep, k, zero), TN) * scale
        low = acc[...].astype(BF16)
        out_ref[...] = low.reshape(a, 1, p, wide)
        for s in range(seq):
            cut_ref[s] = low[:, s * cut : (s + 1) * cut].reshape(a, 1, p, cut)
        total = column_sum(low.astype(F32))

        @pl.when(pl.program_id(0) == 0)
        def _():
            sum_ref[...] = total

        @pl.when(pl.program_id(0) > 0)
        def _():
            sum_ref[...] += total

    return call(
        body,
        (g,),
        [
            pl.BlockSpec((a, 1, p, wide), lambda i: (0, i, 0, 0)),
            pl.BlockSpec((a, 1, p, d), lambda i: (0, i, 0, 0)),
            pl.BlockSpec((1, HEADS, t), lambda i: (i, 0, 0)),
        ],
        [
            pl.BlockSpec((a, 1, p, wide), lambda i: (0, i, 0, 0)),
            pl.BlockSpec((seq, a, 1, p, cut), lambda i: (0, 0, i, 0, 0)),
            whole((1, wide)),
        ],
        [sds((a, g, p, wide), BF16), sds((seq, a, g, p, cut), BF16), sds((1, wide), F32)],
        [pltpu.VMEM((t, wide), F32)],
        flops=12 * g * HEADS * t * t * 256,
        nbytes=2 * a * g * p * (3 * wide + d),
        deps=deps,
    )(qkv, ga, lse)


def stream_back(gqkv, w, x, gmid, mods, out_dtype, shape=None, deps=()):
    n, wide = gqkv.shape
    d = w.shape[0]
    mt = fold(n, 256) if shape is None else n // shape[0]

    def body(g_ref, w_ref, x_ref, gmid_ref, mod_ref, out_ref, sum_ref):
        @pl.when(pl.program_id(0) == 0)
        def _():
            sum_ref[...] = jnp.zeros_like(sum_ref)

        grad = mm(g_ref[...], w_ref[...], NT)
        v, r = standard(x_ref[...].astype(F32))
        sum_ref[0:1, :] += column_sum(grad * v)
        sum_ref[1:2, :] += column_sum(grad)
        out = gmid_ref[...] + norm_back(grad, v, r, 1.0 + mod_ref[1:2, :])
        out_ref[...] = out.astype(out_dtype).reshape(out_ref.shape)

    tile = pl.BlockSpec((mt, d), lambda m: (m, 0))
    result, block = sds((n, d), out_dtype), tile
    if shape is not None:
        parts, frames, places = shape
        result = sds((frames, parts, places, d), out_dtype)
        block = pl.BlockSpec((frames, 1, places, d), lambda m: (0, m, 0, 0))
    return call(
        body,
        (n // mt,),
        [
            pl.BlockSpec((mt, wide), lambda m: (m, 0)),
            whole((d, wide)),
            tile,
            tile,
            whole((8, d)),
        ],
        [block, whole((8, d))],
        [result, sds((8, d), F32)],
        flops=2 * n * d * wide,
        nbytes=2 * (d * wide + n * wide + 5 * n * d),
        deps=deps,
    )(gqkv, w, x, gmid, mods)


def collect(sums, deps=()):
    flat = [item for layer in sums for item in layer]
    d = flat[0].shape[1]
    ups = flat[4].shape[1] // d
    each = 4 + ups

    def body(*refs):
        mod_ref, bias_ref = refs[len(flat) :]
        for k in range(len(sums)):
            stream, middle, update, qkv, up = refs[5 * k : 5 * k + 5]
            rows = (
                (stream, 1), (stream, 0), (middle, 2), (middle, 1), (middle, 0), (middle, 4)
            )
            for r, (ref, at) in enumerate(rows):
                mod_ref[6 * k + r : 6 * k + r + 1, :] = ref[at : at + 1, :]
            base = each * k
            bias_ref[base : base + 1, :] = qkv[:, :d]
            bias_ref[base + 1 : base + 2, :] = qkv[:, 2 * d :]
            bias_ref[base + 2 : base + 3, :] = middle[3:4, :]
            bias_ref[base + 3 : base + 4, :] = update[0:1, :]
            for u in range(ups):
                bias_ref[base + 4 + u : base + 5 + u, :] = up[:, u * d : (u + 1) * d]

    shapes = [(6 * len(sums), d), (each * len(sums), d)]
    return call(
        body,
        (1,),
        [whole(item.shape) for item in flat],
        [whole(shape) for shape in shapes],
        [sds(shape, F32) for shape in shapes],
        deps=deps,
    )(*flat)


def add_pieces(left, right, deps=()):
    seq, zs, rows, d = left.shape

    def body(left_ref, right_ref, out_ref):
        out_ref[...] = (left_ref[...].astype(F32) + right_ref[...].astype(F32)).astype(BF16)

    piece = pl.BlockSpec((1, zs, rows, d), lambda i: (i, 0, 0, 0))
    return call(
        body,
        (seq,),
        [piece, piece],
        piece,
        sds(left.shape, BF16),
        nbytes=6 * seq * zs * rows * d,
        deps=deps,
    )(left, right)


def join_qkv_out(place, own, got, which, deps=()):
    seq, _, zs, rows, d = own.shape
    wide = d * 3 // 4

    def body(place_ref, own_ref, got_ref, qkv_ref, out_ref):
        def put(c, src):
            span = slice(c * rows, (c + 1) * rows)
            qkv_ref[span, :] = jnp.concatenate([src[s ^ place_ref[2], 0, 0, :, :wide] for s in range(seq)], axis=1)
            out_ref[span, :] = jnp.concatenate([src[s ^ place_ref[2], 0, 0, :, wide:] for s in range(seq)], axis=1)

        for c in range(2):

            @pl.when(place_ref[0] == c)
            def _(c=c):
                put(c, own_ref)
                put(1 - c, got_ref)

    piece = pl.BlockSpec(
        (seq, 1, 1, rows, d), lambda i, place_ref: (0, which, slot(i ^ place_ref[1]), 0, 0)
    )
    return call(
        body,
        (zs,),
        [piece, piece],
        [
            pl.BlockSpec((2 * rows, seq * wide), lambda i, place_ref: (i, 0)),
            pl.BlockSpec((2 * rows, d), lambda i, place_ref: (i, 0)),
        ],
        [sds((2 * rows * zs, seq * wide), BF16), sds((2 * rows * zs, d), BF16)],
        scalars=1,
        nbytes=8 * seq * zs * rows * d,
        deps=deps,
    )(place, own, got)


def join_up(place, own, got, which, deps=()):
    seq, _, zs, rows, d = own.shape

    def body(place_ref, own_ref, got_ref, up_ref):
        for c in range(2):

            @pl.when(place_ref[0] == c)
            def _(c=c):
                for s in range(seq):
                    cols = slice(s * d, (s + 1) * d)
                    up_ref[c * rows : (c + 1) * rows, cols] = own_ref[s ^ place_ref[2], 0, 0]
                    up_ref[(1 - c) * rows : (2 - c) * rows, cols] = got_ref[s ^ place_ref[2], 0, 0]

    piece = pl.BlockSpec(
        (seq, 1, 1, rows, d), lambda i, place_ref: (0, which, slot(i ^ place_ref[1]), 0, 0)
    )
    return call(
        body,
        (zs,),
        [piece, piece],
        pl.BlockSpec((2 * rows, seq * d), lambda i, place_ref: (i, 0)),
        sds((2 * rows * zs, seq * d), BF16),
        scalars=1,
        nbytes=8 * seq * zs * rows * d,
        deps=deps,
    )(place, own, got)


def join_down(place, own, got, which, deps=()):
    seq, _, zs, rows, d = own.shape
    quarter = d // seq
    parts = d // quarter

    def body(place_ref, own_ref, got_ref, down_ref):
        def put(c, src):
            for q in range(parts):
                base = (c * parts + q) * rows
                cols = slice(q * quarter, (q + 1) * quarter)
                down_ref[base : base + rows, :] = jnp.concatenate(
                    [src[s ^ place_ref[2], 0, 0, :, cols] for s in range(seq)], axis=1
                )

        for c in range(2):

            @pl.when(place_ref[0] == c)
            def _(c=c):
                put(c, own_ref)
                put(1 - c, got_ref)

    piece = pl.BlockSpec(
        (seq, 1, 1, rows, d), lambda i, place_ref: (0, which, slot(i ^ place_ref[1]), 0, 0)
    )
    return call(
        body,
        (zs,),
        [piece, piece],
        pl.BlockSpec((2 * parts * rows, d), lambda i, place_ref: (i, 0)),
        sds((2 * parts * rows * zs, d), BF16),
        scalars=1,
        nbytes=8 * seq * zs * rows * d,
        deps=deps,
    )(place, own, got)


clip_limit = 8.0
CLIP = ("z", "core")


def hop(x, distance, count):
    return lax.ppermute(x, CLIP, [(i, i ^ distance) for i in range(count)])


def on_device(
    video_latents,
    conditioning,
    ada_weight,
    ada_bias,
    qkv_weight,
    out_weight,
    up_weight,
    down_weight,
    attention_bias,
    up_bias,
    down_bias,
    cotangent,
    *,
    clips,
    seq,
):
    zs = clips // 2
    layers, rows, own_columns = qkv_weight.shape
    d = video_latents.shape[-1]
    frames, places = video_latents.shape[1:3]
    n = frames * places
    ff = up_bias.shape[1]
    clip_index = lax.axis_index(CLIP)
    seq_index = lax.axis_index("seq")
    place = jnp.stack([clip_index % 2, clip_index // 2, 0 * seq_index]).astype(jnp.int32)
    turned = jnp.stack([clip_index % 2, clip_index // 2, seq_index]).astype(jnp.int32)
    packed = zs == 4 and seq == 4 and rows % 16 == 0 and down_weight.shape[1] % rows == 0 and d % seq == 0
    cuts = seq if packed else 1

    def total(v, *axes):
        for axis, count in axes:
            step = 1
            while step < count:
                v = v + lax.ppermute(v, axis, [(i, i ^ step) for i in range(count)])
                step *= 2
        return v

    every_condition = total(
        lax.dynamic_update_slice(
            jnp.zeros((clips, d), F32), conditioning, (clip_index, jnp.zeros_like(clip_index))
        ),
        (CLIP, clips),
    )
    squashed = jax.nn.silu(every_condition).astype(BF16)
    local_mods = (
        jnp.einsum("kd,ldc->klc", squashed, ada_weight, preferred_element_type=F32)
        + ada_bias[None, :, :]
    )
    own_mods = lax.all_to_all(local_mods, CLIP, 0, 0, tiled=True)
    every_mod = lax.all_gather(own_mods, "seq", axis=0, tiled=False)
    modulation = every_mod.transpose(2, 1, 0, 3).reshape(layers, 6, d)
    modulation = jnp.pad(modulation, ((0, 0), (0, 2), (0, 0)))

    def far(block):
        return hop(block, 4, clips)

    def near(block):
        return hop(block, 2, clips)

    def side(block, distance):
        return lax.ppermute(block, "seq", [(i, i ^ distance) for i in range(seq)])

    def put(*parts):
        return jnp.concatenate(parts, axis=1)

    def pack_rows(layer):
        tall = down_weight[layer].reshape(-1, rows, d // seq)
        return (
            jnp.concatenate([qkv_weight[layer], out_weight[layer]], axis=1),
            up_weight[layer],
            tall.transpose(1, 0, 2).reshape(rows, d),
        )

    def along_seq(blocks):
        return lax.all_gather(blocks, "seq", axis=0, tiled=False)

    def across(upper, lower):
        upper_x, lower_y = side(upper, 1), side(lower, 2)
        upper_y, lower_x = side(upper, 2), side(lower, 1)
        blocks = (
            (upper, lower),
            (upper_x, lower_x),
            (upper_y, lower_y),
            (side(upper_x, 2), side(lower_y, 1)),
        )
        return jnp.stack([put(*pair) for pair in blocks])

    def both_cores(own, deps):
        own = gate(own, deps)
        return own, hop(own, 1, clips)

    def fetch_natural(layer):
        return tuple(
            lax.all_gather(
                lax.all_gather(item[layer], CLIP, axis=0, tiled=True), "seq", axis=1, tiled=True
            )
            for item in (qkv_weight, out_weight, up_weight, down_weight)
        )

    def reduce_seq(half):
        flat = lax.psum_scatter(half.reshape(-1, d), "seq", scatter_dimension=0, tiled=True)
        return flat.reshape(zs, rows, d)

    def first_half(part):
        return hop(part[2:], 2, clips)

    def add_first(part, got):
        return (part[:2].astype(F32) + got.astype(F32)).astype(BF16)

    def second_half(part):
        return hop(part[1], 4, clips)

    def add_second(part, got):
        return part[0].astype(F32) + got.astype(F32)

    def shed_natural(left, right):
        full = mm(left, right, TN).astype(BF16)
        part = lax.psum_scatter(full, "seq", scatter_dimension=1, tiled=True)
        return lax.psum_scatter(part, CLIP, scatter_dimension=0, tiled=True).astype(F32)

    def swap_tokens(x):
        block = x.reshape(seq, n // seq, d)
        return lax.all_to_all(block, "seq", 0, 0, tiled=True).reshape(n, d)

    def by_places(x):
        return x.reshape(frames, seq, places // seq, d).transpose(1, 0, 2, 3).reshape(n, d)

    def by_frames(x):
        return (
            x.reshape(seq, frames, places // seq, d)
            .transpose(1, 0, 2, 3)
            .reshape(1, frames, places, d)
        )

    shapes = (
        (seq, frames, places // seq),
        (seq * frames, places // seq // 16, 16),
    )

    def qkv_bias_of(layer):
        bias = attention_bias[layer]
        return jnp.concatenate([bias[0], jnp.zeros_like(bias[0]), bias[1]])[None]

    def forward_natural(layer, x):
        mods = modulation[layer]
        qkv_full, out_full, up_full, down_full = fetch_natural(layer)
        hidden, qkv = qkv_forward(x, mods, qkv_full, qkv_bias_of(layer))
        qkv = qkv.reshape(shapes[layer] + (3 * d,))
        attended, lse, peak = attention_forward(qkv, layer == 1)
        attended = attended.reshape(n, d)
        out_bias = attention_bias[layer, 2:3]
        branch, middle, hidden_two = out_forward(attended, x, mods, out_full, out_bias)
        active, slope = up_forward(hidden_two, up_full, up_bias[layer : layer + 1])
        update, result = down_forward(
            active, middle, mods, down_full, down_bias[layer : layer + 1]
        )
        kept = (x, hidden, qkv, lse, attended, branch, middle, hidden_two, active, slope, update)
        weights = (qkv_full, out_full, up_full, down_full)
        return result, kept, weights, jnp.max(peak, axis=(0, 1))

    def backward_natural(layer, grad_out, kept, weights):
        x, hidden, qkv, lse, attended, branch, middle, hidden_two, active, slope, update = kept
        qkv_full, out_full, up_full, down_full = weights
        mods = modulation[layer]
        grad_update, update_sums = update_back(grad_out, mods)
        inner_grad, up_sums, hidden_grad = feed_back(grad_update, slope, down_full, up_full)
        middle_grad, branch_grad, _, attended_grad, middle_sums = middle_back(
            hidden_grad, middle, branch, grad_out, update, mods, out_full, 1
        )
        qkv_grad, _, qkv_sums = attention_back(
            qkv, attended_grad.reshape(shapes[layer] + (d,)), lse, layer == 1, 1
        )
        qkv_grad = qkv_grad.reshape(n, 3 * d)
        stream_grad, stream_sums = stream_back(
            qkv_grad, qkv_full, x, middle_grad, mods, BF16 if layer == 1 else F32
        )
        parts = (
            shed_natural(hidden, qkv_grad),
            shed_natural(attended, branch_grad),
            shed_natural(hidden_two, inner_grad),
            shed_natural(active, grad_update),
        )
        if layer == 0:
            stream_grad = by_frames(stream_grad)
        return stream_grad, (stream_sums, middle_sums, update_sums, qkv_sums, up_sums), parts

    def unpack(parts):
        down_g, up_g, both = parts
        down_g = down_g.reshape(rows, -1, d // seq).transpose(1, 0, 2).reshape(-1, d // seq)
        return both[:, :own_columns], both[:, own_columns:], up_g, down_g

    def run_natural():
        first_in = by_places(video_latents)
        second_go = swap_tokens(by_places(cotangent))
        first_out, first_kept, first_weights, first_peak = forward_natural(0, first_in)
        second_in = swap_tokens(first_out)
        second_out, second_kept, second_weights, second_peak = forward_natural(1, second_in)
        second_grad, second_sums, second_parts = backward_natural(
            1, second_go, second_kept, second_weights
        )
        first_grad, first_sums, first_parts = backward_natural(
            0, swap_tokens(second_grad), first_kept, first_weights
        )
        peaks = (first_peak, second_peak)
        sums = (first_sums, second_sums)
        second_out = swap_tokens(second_out)

        def finish(small, own_mod_grad):
            return total(small, (CLIP, clips), ("seq", seq)), first_parts

        return second_out, first_grad, peaks, collect(sums), finish, second_parts

    def run_packed():
        first_pack, second_pack = pack_rows(0), pack_rows(1)
        first_in = by_places(video_latents)
        second_go = swap_tokens(by_places(cotangent))

        block = first_pack[0][None, None]
        pair = put(block, far(block))
        rest = gate(near(pair), (second_go,))
        whole_q0 = across(pair, rest)
        block = gate(first_pack[1][None, None], (rest,))
        pair = put(block, far(block))
        line_u0 = put(pair, near(pair))
        block = gate(first_pack[2][None, None], (line_u0,))
        pair_d0 = put(block, gate(far(block), (modulation,)))
        whole_u0 = along_seq(line_u0)

        def attention_part(layer, x, qkv, out_full):
            qkv = qkv.reshape(shapes[layer] + (3 * d,))
            attended, lse, peak = attention_forward(qkv, layer == 1)
            return qkv, attended.reshape(n, d), lse, jnp.max(peak, axis=(0, 1))

        mods = modulation[0]
        qkv_full, out_full = join_qkv_out(turned, *both_cores(whole_q0, (pair_d0,)), 0)
        hidden, qkv = qkv_forward(first_in, mods, qkv_full, qkv_bias_of(0))
        hidden, qkv, got = joint(hidden, qkv, near(pair_d0))
        line_d0 = put(pair_d0, got)
        whole_d0 = along_seq(line_d0)
        block_q1 = gate(second_pack[0][None, None], (got,))
        qkv, attended, lse, peak0 = attention_part(0, first_in, qkv, out_full)
        attended, lse, got = joint(attended, lse, far(block_q1))
        pair_q1 = put(block_q1, got)
        branch, middle, hidden_two = out_forward(
            attended, first_in, mods, out_full, attention_bias[0, 2:3]
        )
        branch, middle, hidden_two, got = joint(branch, middle, hidden_two, near(pair_q1))
        line_q1 = put(pair_q1, got)
        whole_q1 = along_seq(line_q1)
        block_f1 = gate(jnp.stack(second_pack[1:])[:, None], (got,))
        up_full = join_up(place, *both_cores(whole_u0, (branch,)), 0, deps=(line_q1, line_d0))
        active, slope = up_forward(hidden_two, up_full, up_bias[:1])
        active, slope, got = joint(active, slope, far(block_f1))
        pair_f1 = put(block_f1, got)
        down_full = join_down(place, *both_cores(whole_d0, (active,)), 0, deps=(pair_f1,))
        update, result = down_forward(active, middle, mods, down_full, down_bias[:1])
        update, result, got = joint(update, result, near(pair_f1))
        line_f1 = put(pair_f1, got)
        whole_u1, whole_d1 = along_seq(line_f1[:1]), along_seq(line_f1[1:])
        kept0 = (
            first_in, hidden, qkv, lse, attended, branch, middle, hidden_two, active, slope, update
        )
        weights0 = (qkv_full, out_full, up_full, down_full)
        second_in = swap_tokens(result)

        mods = modulation[1]
        own, got = both_cores(whole_q1, (second_in, line_f1))
        qkv_full, out_full = join_qkv_out(place, own, got, 0)
        hidden, qkv = qkv_forward(second_in, mods, qkv_full, qkv_bias_of(1))
        qkv, attended, lse, peak1 = attention_part(1, second_in, qkv, out_full)
        branch, middle, hidden_two = out_forward(
            attended, second_in, mods, out_full, attention_bias[1, 2:3]
        )
        own, got = both_cores(whole_u1, (attended,))
        branch, middle, hidden_two, got = joint(branch, middle, hidden_two, got)
        up_full = join_up(place, own, got, 0)
        active, slope = up_forward(hidden_two, up_full, up_bias[1:2])
        grad_update, update_sums1 = update_back(second_go, mods, deps=(active,))
        down_m, down_o = down_grad(place, active, grad_update, seq, zs)
        own, got = both_cores(whole_d1, (down_m,))
        half_d1 = add_pieces(down_m, hop(down_o, 1, clips), deps=(own,))
        half_d1, got = joint(half_d1, got)
        part_d1 = reduce_seq(half_d1)
        down_full = join_down(place, own, got, 0)
        update, result = down_forward(
            active, middle, mods, down_full, down_bias[1:2], deps=(half_d1,)
        )
        kept1 = (
            second_in, hidden, qkv, lse, attended, branch, middle, hidden_two, active, slope, update
        )
        weights1 = (qkv_full, out_full, up_full, down_full)
        kept, weights = (kept0, kept1), (weights0, weights1)

        def up_stage(layer, hidden_grad, inner_grad, grad_out, deps):
            _, _, _, _, _, branch, middle, hidden_two, _, _, update = kept[layer]
            up_m, up_o = up_grad(place, hidden_two, inner_grad, seq, zs, deps=deps)
            middle_grad, _, branch_cut, attended_grad, middle_sums = middle_back(
                hidden_grad, middle, branch, grad_out, update, modulation[layer],
                weights[layer][1], cuts, deps=(up_m,),
            )
            half_u = add_pieces(up_m, hop(up_o, 1, clips), deps=(middle_grad,))
            return half_u, reduce_seq(half_u), middle_grad, branch_cut, attended_grad, middle_sums

        def attention_stage(layer, attended_grad, deps):
            _, _, qkv, lse = kept[layer][:4]
            grad = attended_grad.reshape(shapes[layer] + (d,))
            qkv_grad, qkv_cut, qkv_sums = attention_back(
                qkv, grad, lse, layer == 1, cuts, deps=deps
            )
            return qkv_grad.reshape(n, 3 * d), qkv_cut.reshape(seq, n, -1), qkv_sums

        def last_grad(layer, qkv_cut, branch_cut, deps):
            hidden, attended = kept[layer][1], kept[layer][4]
            return qkv_out_grad(place, hidden, attended, qkv_cut, branch_cut, zs, deps=deps)

        inner_grad, up_sums, hidden_grad = feed_back(
            grad_update, kept1[9], weights1[3], weights1[2], deps=(result,)
        )
        inner_grad, hidden_grad, second_out = joint(inner_grad, hidden_grad, swap_tokens(result))
        half_u, part_u1, middle_grad, branch_cut, attended_grad, middle_sums = up_stage(
            1, hidden_grad, inner_grad, second_go, ()
        )
        qkv_grad, qkv_cut, qkv_sums = attention_stage(1, attended_grad, (half_u, part_d1))
        qkv_grad, qkv_cut, got = joint(qkv_grad, qkv_cut, first_half(part_d1))
        sum_d1 = add_first(part_d1, got)
        stream_grad, stream_sums = stream_back(
            qkv_grad, weights1[0], kept1[0], middle_grad, modulation[1], BF16
        )
        stream_grad, stream_sums, got = joint(stream_grad, stream_sums, second_half(sum_d1))
        down_g1 = add_second(sum_d1, got)
        second_sums = (stream_sums, middle_sums, update_sums1, qkv_sums, up_sums)
        last_m, last_o = last_grad(1, qkv_cut, branch_cut, (stream_grad,))
        last_m, last_o, first_go = joint(last_m, last_o, swap_tokens(stream_grad))

        grad_update, update_sums = update_back(first_go, modulation[0])
        half_q1 = add_pieces(last_m, hop(last_o, 1, clips), deps=(grad_update,))
        part_q1 = reduce_seq(half_q1)
        down_m, down_o = down_grad(place, kept0[8], grad_update, seq, zs, deps=(half_q1,))
        inner_grad, up_sums, hidden_grad = feed_back(
            grad_update, kept0[9], weights0[3], weights0[2], deps=(down_m, part_u1)
        )
        inner_grad, hidden_grad, got = joint(inner_grad, hidden_grad, first_half(part_u1))
        sum_u1 = add_first(part_u1, got)
        half_d0 = add_pieces(down_m, hop(down_o, 1, clips), deps=(hidden_grad, part_q1))
        part_d0 = reduce_seq(half_d0)
        half_u, part_u0, middle_grad, branch_cut, attended_grad, middle_sums = up_stage(
            0, hidden_grad, inner_grad, first_go, (half_d0, sum_u1)
        )
        qkv_grad, qkv_cut, qkv_sums = attention_stage(0, attended_grad, (half_u,))
        qkv_grad, qkv_cut, got, got2 = joint(
            qkv_grad, qkv_cut, first_half(part_q1), second_half(sum_u1)
        )
        sum_q1 = add_first(part_q1, got)
        up_g1 = add_second(sum_u1, got2)
        last_m, last_o = last_grad(0, qkv_cut, branch_cut, (part_d0, sum_q1))
        last_m, last_o, got, got2 = joint(last_m, last_o, first_half(part_d0), second_half(sum_q1))
        sum_d0 = add_first(part_d0, got)
        both_g1 = add_second(sum_q1, got2)
        first_grad, stream_sums = stream_back(
            qkv_grad, weights0[0], kept0[0], middle_grad, modulation[0], F32, shape=shapes[0],
            deps=(last_m, sum_d0),
        )
        first_grad, stream_sums, got = joint(first_grad, stream_sums, second_half(sum_d0))
        down_g0 = add_second(sum_d0, got)
        first_sums = (stream_sums, middle_sums, update_sums, qkv_sums, up_sums)
        half = add_pieces(last_m, hop(last_o, 1, clips), deps=(first_grad,))
        part_q0 = reduce_seq(half)
        got = first_half(part_u0)
        rows_of = collect((first_sums, second_sums), deps=(half, got))
        sum_u0 = add_first(part_u0, got)
        second_parts = unpack((down_g1, up_g1, both_g1))

        def finish(small, own_mod_grad):
            up_g0 = add_second(sum_u0, gate(second_half(sum_u0), (own_mod_grad,)))
            part = gate(part_q0, (up_g0,))
            sum_q0 = add_first(part, first_half(part))
            both_g0 = add_second(sum_q0, second_half(sum_q0))
            return total(small, (CLIP, clips), ("seq", seq)), unpack((down_g0, up_g0, both_g0))

        return second_out, first_grad, (peak0, peak1), rows_of, finish, second_parts

    run = run_packed if packed else run_natural
    second_out, latents_grad, peaks, (mod_grads, bias_rows), finish, second_shed = run()
    output_latents = by_frames(second_out)

    mod_grads = total(mod_grads, ("seq", seq)).reshape(layers, clips, seq, -1)
    of_columns = lax.dynamic_index_in_dim(mod_grads, lax.axis_index("seq"), 2, keepdims=False)
    own_mod_grad = lax.all_to_all(of_columns.transpose(1, 0, 2), CLIP, 0, 0, tiled=True)
    ada_bias_grad = jnp.sum(own_mod_grad, axis=0)
    rounded_mod = own_mod_grad.astype(BF16)
    ada_weight_grad = jnp.einsum("kd,klc->ldc", squashed, rounded_mod, preferred_element_type=F32)
    squash_part = jnp.einsum("klc,ldc->kd", rounded_mod, ada_weight, preferred_element_type=F32)
    bias_count = bias_rows.shape[0]
    devices = clips * seq
    device = clip_index * seq + lax.axis_index("seq")
    peak_rows = -(-devices * layers * HEADS // d)
    own_peaks = jnp.concatenate(peaks)[None]
    placed = lax.dynamic_update_slice(
        jnp.zeros((devices, layers * HEADS), F32), own_peaks, (device, 0)
    ).reshape(-1)
    placed = jnp.pad(placed, (0, peak_rows * d - placed.shape[0])).reshape(peak_rows, d)
    summed, first_shed = finish(
        jnp.concatenate([bias_rows, squash_part, placed], axis=0), own_mod_grad
    )
    bias_sums = summed[:bias_count].reshape(layers, -1, d)
    own_squash = lax.dynamic_slice_in_dim(summed, bias_count + clip_index, 1, axis=0)
    peaks = summed[bias_count + clips :].reshape(-1)[: devices * layers * HEADS]
    logit_peak = jnp.max(peaks.reshape(devices, layers, HEADS), axis=0)
    column_index = lax.axis_index("seq") * own_columns + jnp.arange(own_columns, dtype=jnp.int32)
    head_of = column_index % d // (d // HEADS)
    head_match = (head_of[:, None] == jnp.arange(HEADS, dtype=jnp.int32)[None, :]).astype(F32)
    roots = jnp.sqrt(clip_limit / jnp.maximum(logit_peak, clip_limit))
    column_roots = jnp.sum(roots[:, None, :] * head_match[None, :, :], axis=-1)
    column_scale = jnp.where(column_index[None, :] < 2 * d, column_roots, 1.0)
    clipped_qkv = qkv_weight.astype(F32) * column_scale[:, None, :]
    silu_value, silu_pull = jax.vjp(jax.nn.silu, conditioning)
    conditioning_grad = silu_pull(own_squash)[0]
    return (
        output_latents,
        latents_grad.reshape(1, frames, places, d),
        conditioning_grad,
        ada_weight_grad,
        ada_bias_grad,
        jnp.stack([first_shed[0], second_shed[0]]),
        jnp.stack([first_shed[1], second_shed[1]]),
        jnp.stack([first_shed[2], second_shed[2]]),
        jnp.stack([first_shed[3], second_shed[3]]),
        bias_sums[:, :3],
        bias_sums[:, 4:].reshape(layers, ff),
        bias_sums[:, 3],
        clipped_qkv,
        logit_peak,
    )


def solution(mesh):
    clips, seq = mesh.shape["clip"], mesh.shape["seq"]
    finer = jax.sharding.Mesh(
        mesh.devices.reshape(clips // 2, 2, seq), ("z", "core", "seq")
    )
    every = (*CLIP, "seq")
    tokens = P(CLIP, "seq", None, None)
    matrix = P(None, CLIP, "seq")
    return jax.shard_map(
        partial(on_device, clips=clips, seq=seq),
        mesh=finer,
        in_specs=(
            tokens,
            P(CLIP, None),
            P(None, None, every),
            P(None, every),
            matrix,
            matrix,
            matrix,
            matrix,
            P(),
            P(),
            P(),
            tokens,
        ),
        out_specs=(
            tokens,
            tokens,
            P(CLIP, None),
            P(None, None, every),
            P(None, every),
            matrix,
            matrix,
            matrix,
            matrix,
            P(),
            P(),
            P(),
            matrix,
            P(),
        ),
        check_vma=False,
    )
```

```python
from functools import partial

import jax
import jax.numpy as jnp
from jax import lax
from jax.experimental import pallas as pl
from jax.experimental.pallas import tpu as pltpu
from jax.sharding import PartitionSpec as P

HEADS = 16
F32 = jnp.float32
BF16 = jnp.bfloat16
NN = (((1,), (0,)), ((), ()))
NT = (((1,), (1,)), ((), ()))
TN = (((0,), (0,)), ((), ()))
VMEM_BYTES = 56 * 1024 * 1024
FEED_ROWS = 1024
UP_ROWS, UP_CUTS = 1024, 1
QKV_ROWS = 512


def mm(a, b, dims=NN):
    return lax.dot_general(a, b, dims, preferred_element_type=F32)


def call(
    body, grid, in_specs, out_specs, out_shape, scratch=(), scalars=0, flops=0, nbytes=0, deps=()
):
    first = scalars + len(in_specs)

    def run(*refs):
        body(*refs[:first], *refs[first + len(deps) :])

    kernel = pl.pallas_call(
        run,
        grid_spec=pltpu.PrefetchScalarGridSpec(
            num_scalar_prefetch=scalars,
            grid=grid,
            in_specs=[*in_specs, *[pl.BlockSpec(memory_space=pl.ANY)] * len(deps)],
            out_specs=out_specs,
            scratch_shapes=list(scratch),
        ),
        out_shape=out_shape,
        compiler_params=pltpu.CompilerParams(
            dimension_semantics=("arbitrary",) * len(grid), vmem_limit_bytes=VMEM_BYTES
        ),
        cost_estimate=pl.CostEstimate(flops=flops, bytes_accessed=nbytes, transcendentals=0),
    )
    return lambda *args: kernel(*args, *deps)


def gate(x, deps):
    def body(*refs):
        pass

    anywhere = pl.BlockSpec(memory_space=pl.ANY)
    return pl.pallas_call(
        body,
        in_specs=[anywhere] * (1 + len(deps)),
        out_specs=anywhere,
        out_shape=sds(x.shape, x.dtype),
        input_output_aliases={0: 0},
    )(x, *deps)


def joint(*arrays):
    def body(*refs):
        pass

    anywhere = pl.BlockSpec(memory_space=pl.ANY)
    return pl.pallas_call(
        body,
        in_specs=[anywhere] * len(arrays),
        out_specs=[anywhere] * len(arrays),
        out_shape=[sds(x.shape, x.dtype) for x in arrays],
        input_output_aliases={k: k for k in range(len(arrays))},
    )(*arrays)


def whole(shape):
    return pl.BlockSpec(shape, lambda *_: (0,) * len(shape))


def sds(shape, dtype):
    return jax.ShapeDtypeStruct(shape, dtype)


def standard(x):
    centred = x - jnp.mean(x, axis=-1, keepdims=True)
    r = lax.rsqrt(jnp.mean(centred * centred, axis=-1, keepdims=True) + 1e-06)
    return centred * r, r


def fold(n, limit=512):
    return min(n, limit)


def qkv_forward(x, mods, w, bias, deps=()):
    n, d = x.shape
    wide = w.shape[1]
    mt = fold(n, QKV_ROWS)

    def body(x_ref, mod_ref, w_ref, b_ref, hid_ref, out_ref):
        m = pl.program_id(1)
        rows = pl.ds(pl.multiple_of(m * mt, mt), mt)

        @pl.when(pl.program_id(0) == 0)
        def _():
            v, _ = standard(x_ref[...].astype(F32))
            hid_ref[rows, :] = (v * (1.0 + mod_ref[1:2, :]) + mod_ref[0:1, :]).astype(BF16)

        out_ref[...] = (mm(hid_ref[rows, :], w_ref[...]) + b_ref[...]).astype(BF16)

    return call(
        body,
        (wide // d, n // mt),
        [
            pl.BlockSpec((mt, d), lambda j, m: (jnp.where(j == 0, m, n // mt - 1), 0)),
            whole((8, d)),
            pl.BlockSpec((d, d), lambda j, m: (0, j)),
            pl.BlockSpec((1, d), lambda j, m: (0, j)),
        ],
        [whole((n, d)), pl.BlockSpec((mt, d), lambda j, m: (m, j))],
        [sds((n, d), BF16), sds((n, wide), BF16)],
        flops=2 * n * d * wide,
        nbytes=2 * (d * wide + n * wide + 2 * n * d),
        deps=deps,
    )(x, mods, w, bias)


def window(h, size, d):
    lo = h * size
    start = lo // 128 * 128
    stop = min(-(-(lo + size) // 128) * 128, d)
    return start, stop, lo - start


def head_mask(start, stop, off, size, rows):
    lane = lax.broadcasted_iota(jnp.int32, (rows, stop - start), 1)
    return (lane >= off) & (lane < off + size)


def attention_forward(qkv, temporal, deps=()):
    a, g, p, wide = qkv.shape
    d = wide // 3
    size = d // HEADS
    t = a * p
    scale = size ** (-0.5)

    def body(qkv_ref, att_ref, lse_ref, peak_ref, acc):
        acc[...] = jnp.zeros_like(acc)
        if temporal:
            qi = lax.broadcasted_iota(jnp.int32, (t, t), 0)
            ki = lax.broadcasted_iota(jnp.int32, (t, t), 1)
            same = lax.rem(qi, p) == lax.rem(ki, p)
        tops, totals = [], []
        for h in range(HEADS):
            lo, hi, off = window(h, size, d)
            keep = head_mask(lo, hi, off, size, t)
            q = qkv_ref[:, 0, :, lo:hi].reshape(t, hi - lo)
            k = qkv_ref[:, 0, :, d + lo : d + hi].reshape(t, hi - lo)
            v = qkv_ref[:, 0, :, 2 * d + lo : 2 * d + hi].reshape(t, hi - lo)
            zero = jnp.zeros_like(q)
            s = mm(jnp.where(keep, q, zero), k, NT) * scale
            if temporal:
                s = jnp.where(same, s, -1e30)
            top = jnp.max(s, axis=-1, keepdims=True)
            e = jnp.exp(s - top)
            total = jnp.sum(e, axis=-1, keepdims=True)
            probs = (e / total).astype(BF16)
            acc[:, lo:hi] += mm(probs, jnp.where(keep, v, zero))
            tops.append(top)
            totals.append(total)
        top = jnp.concatenate(tops, axis=1)
        lse_ref[0] = (top + jnp.log(jnp.concatenate(totals, axis=1))).T
        peak_ref[...] = jnp.max(top, axis=0, keepdims=True)[None]
        att_ref[...] = acc[...].astype(BF16).reshape(a, 1, p, d)

    return call(
        body,
        (g,),
        [pl.BlockSpec((a, 1, p, wide), lambda i: (0, i, 0, 0))],
        [
            pl.BlockSpec((a, 1, p, d), lambda i: (0, i, 0, 0)),
            pl.BlockSpec((1, HEADS, t), lambda i: (i, 0, 0)),
            pl.BlockSpec((1, 1, HEADS), lambda i: (i, 0, 0)),
        ],
        [sds((a, g, p, d), BF16), sds((g, HEADS, t), F32), sds((g, 1, HEADS), F32)],
        [pltpu.VMEM((t, d), F32)],
        flops=4 * g * HEADS * t * t * 256,
        nbytes=2 * a * g * p * (wide + d),
        deps=deps,
    )(qkv)


def out_forward(att, x, mods, w, bias, deps=()):
    n, d = att.shape
    mt = fold(n, 256)

    def body(att_ref, x_ref, mod_ref, w_ref, b_ref, branch_ref, mid_ref, hid_ref):
        branch = mm(att_ref[...], w_ref[...]) + b_ref[...]
        branch_ref[...] = branch.astype(BF16)
        mid = x_ref[...].astype(F32) + mod_ref[2:3, :] * branch
        mid_ref[...] = mid
        v, _ = standard(mid)
        hid_ref[...] = (v * (1.0 + mod_ref[4:5, :]) + mod_ref[3:4, :]).astype(BF16)

    tile = pl.BlockSpec((mt, d), lambda m: (m, 0))
    return call(
        body,
        (n // mt,),
        [tile, tile, whole((8, d)), whole((d, d)), whole((1, d))],
        [tile, tile, tile],
        [sds((n, d), BF16), sds((n, d), F32), sds((n, d), BF16)],
        flops=2 * n * d * d,
        nbytes=2 * (d * d + 6 * n * d),
        deps=deps,
    )(att, x, mods, w, bias)


GELU_A = 0.7978845608028654
GELU_B = 0.044715


def up_forward(hid, w, bias, deps=()):
    n, d = hid.shape
    ff = w.shape[1]
    mt = fold(n, UP_ROWS)
    ft = d
    cuts = UP_CUTS

    def body(hid_ref, w_ref, b_ref, act_ref, slope_ref):
        for c in range(cuts):
            cols = slice(c * ft // cuts, (c + 1) * ft // cuts)
            u = mm(hid_ref[...], w_ref[:, cols]) + b_ref[:, cols]
            square = u * u
            tanh = jnp.tanh(u * (GELU_A + (GELU_A * GELU_B) * square))
            half = 0.5 + 0.5 * tanh
            act_ref[:, cols] = (u * half).astype(BF16)
            bend = GELU_A + (3.0 * GELU_A * GELU_B) * square
            slope_ref[:, cols] = (half + (u * half) * ((1.0 - tanh) * bend)).astype(BF16)

    tile = pl.BlockSpec((mt, ft), lambda f, m: (m, f))
    return call(
        body,
        (ff // ft, n // mt),
        [
            pl.BlockSpec((mt, d), lambda f, m: (m, 0)),
            pl.BlockSpec((d, ft), lambda f, m: (0, f)),
            pl.BlockSpec((1, ft), lambda f, m: (0, f)),
        ],
        [tile, tile],
        [sds((n, ff), BF16), sds((n, ff), BF16)],
        flops=2 * n * d * ff,
        nbytes=2 * (d * ff + 2 * n * ff + n * d),
        deps=deps,
    )(hid, w, bias)


def down_forward(act, mid, mods, w, bias, deps=()):
    n, ff = act.shape
    d = w.shape[1]
    mt = fold(n, 256)

    def body(act_ref, mid_ref, mod_ref, w_ref, b_ref, upd_ref, out_ref):
        upd = mm(act_ref[...], w_ref[...]) + b_ref[...]
        upd_ref[...] = upd.astype(BF16)
        out_ref[...] = (mid_ref[...] + mod_ref[5:6, :] * upd).astype(BF16)

    tile = pl.BlockSpec((mt, d), lambda m: (m, 0))
    return call(
        body,
        (n // mt,),
        [
            pl.BlockSpec((mt, ff), lambda m: (m, 0)),
            tile,
            whole((8, d)),
            whole((ff, d)),
            whole((1, d)),
        ],
        [tile, tile],
        [sds((n, d), BF16), sds((n, d), BF16)],
        flops=2 * n * d * ff,
        nbytes=2 * (d * ff + n * ff + 4 * n * d),
        deps=deps,
    )(act, mid, mods, w, bias)


def column_sum(v):
    return jnp.sum(v, axis=0, keepdims=True)


def update_back(go, mods, deps=()):
    n, d = go.shape
    mt = fold(n, 256)

    def body(go_ref, mod_ref, gu_ref, sum_ref):
        @pl.when(pl.program_id(0) == 0)
        def _():
            sum_ref[...] = jnp.zeros_like(sum_ref)

        low = (mod_ref[5:6, :] * go_ref[...].astype(F32)).astype(BF16)
        gu_ref[...] = low
        sum_ref[0:1, :] += column_sum(low.astype(F32))

    tile = pl.BlockSpec((mt, d), lambda m: (m, 0))
    return call(
        body,
        (n // mt,),
        [tile, whole((8, d))],
        [tile, whole((8, d))],
        [sds((n, d), BF16), sds((8, d), F32)],
        flops=n * d,
        nbytes=4 * n * d,
        deps=deps,
    )(go, mods)


def slot(k):
    return k % 2 * 2 + k // 2


def shed_specs(seq, zs, rows, d):
    return sds((seq, zs, rows, d), BF16)


def shares(start, stop, rows):
    found = []
    while start < stop:
        block = start // rows
        end = min(stop, (block + 1) * rows)
        found.append((block, start - block * rows, start, end))
        start = end
    return found


def down_grad(place, act, gu, seq, zs, deps=()):
    n, ff = act.shape
    d = gu.shape[1]
    rows, quarter = d // (2 * zs), d // seq
    parts = ff // (2 * zs) // rows
    cuts = 3

    def body(place_ref, act_ref, gu_ref, mine_ref, other_ref):
        def fill(targets):
            for c in range(cuts):
                first, stop = c * (ff // zs) // cuts, (c + 1) * (ff // zs) // cuts
                full = mm(act_ref[:, first:stop], gu_ref[...], TN).astype(BF16)
                for block, at, lo, hi in shares(first, stop, rows):
                    target, q = targets[block // parts], block % parts
                    for s in range(seq):
                        target[s, 0, at : at + hi - lo, q * quarter : (q + 1) * quarter] = full[
                            lo - first : hi - first, s * quarter : (s + 1) * quarter
                        ]

        @pl.when(place_ref[0] == 0)
        def _():
            fill((mine_ref, other_ref))

        @pl.when(place_ref[0] == 1)
        def _():
            fill((other_ref, mine_ref))

    piece = pl.BlockSpec((seq, 1, rows, d), lambda i, place_ref: (0, i, 0, 0))
    return call(
        body,
        (zs,),
        [
            pl.BlockSpec((n, ff // zs), lambda i, place_ref: (0, slot(i) ^ place_ref[1])),
            whole((n, d)),
        ],
        [piece, piece],
        [shed_specs(seq, zs, rows, d)] * 2,
        scalars=1,
        flops=2 * n * d * ff,
        nbytes=2 * (d * ff + n * ff + n * d),
        deps=deps,
    )(place, act, gu)


def up_grad(place, hid, gi, seq, zs, deps=()):
    n, d = hid.shape
    ff = gi.shape[1]
    rows, wide = d // (2 * zs), ff // seq
    cuts = 3

    def body(place_ref, hid_ref, gi_ref, mine_ref, other_ref):
        z = place_ref[1]

        def fill(targets):
            for c in range(cuts):
                first, stop = c * d // cuts, (c + 1) * d // cuts
                full = mm(hid_ref[:, first:stop], gi_ref[...], TN).astype(BF16)
                for block, at, lo, hi in shares(first, stop, rows):
                    targets[block % 2][0, slot((block // 2) ^ z), at : at + hi - lo, :] = full[
                        lo - first : hi - first
                    ]

        @pl.when(place_ref[0] == 0)
        def _():
            fill((mine_ref, other_ref))

        @pl.when(place_ref[0] == 1)
        def _():
            fill((other_ref, mine_ref))

    piece = pl.BlockSpec((1, zs, rows, wide), lambda i, place_ref: (i, 0, 0, 0))
    return call(
        body,
        (seq,),
        [whole((n, d)), pl.BlockSpec((n, wide), lambda i, place_ref: (0, i))],
        [piece, piece],
        [shed_specs(seq, zs, rows, wide)] * 2,
        scalars=1,
        flops=2 * n * d * ff,
        nbytes=2 * (d * ff + n * ff + n * d),
        deps=deps,
    )(place, hid, gi)


def qkv_out_grad(place, hid, att, gqkv, gb, zs, deps=()):
    n, d = hid.shape
    seq, _, wa = gqkv.shape
    wb = gb.shape[2]
    rows = d // (2 * zs)
    cuts = 3

    def body(place_ref, hid_ref, att_ref, gqkv_ref, gb_ref, mine_ref, other_ref):
        z = place_ref[1]

        def fill(targets):
            for c in range(cuts):
                first, stop = c * d // cuts, (c + 1) * d // cuts
                left = mm(hid_ref[:, first:stop], gqkv_ref[0], TN).astype(BF16)
                right = mm(att_ref[:, first:stop], gb_ref[0], TN).astype(BF16)
                full = jnp.concatenate([left, right], axis=1)
                for block, at, lo, hi in shares(first, stop, rows):
                    targets[block % 2][0, slot((block // 2) ^ z), at : at + hi - lo, :] = full[
                        lo - first : hi - first
                    ]

        @pl.when(place_ref[0] == 0)
        def _():
            fill((mine_ref, other_ref))

        @pl.when(place_ref[0] == 1)
        def _():
            fill((other_ref, mine_ref))

    piece = pl.BlockSpec((1, zs, rows, wa + wb), lambda i, place_ref: (i, 0, 0, 0))
    return call(
        body,
        (seq,),
        [
            whole((n, d)),
            whole((n, d)),
            pl.BlockSpec((1, n, wa), lambda i, place_ref: (i, 0, 0)),
            pl.BlockSpec((1, n, wb), lambda i, place_ref: (i, 0, 0)),
        ],
        [piece, piece],
        [shed_specs(seq, zs, rows, wa + wb)] * 2,
        scalars=1,
        flops=2 * n * d * seq * (wa + wb),
        nbytes=2 * seq * (d + n) * (wa + wb),
        deps=deps,
    )(place, hid, att, gqkv, gb)


def feed_back(gu, slope, w_down, w_up, deps=()):
    n, d = gu.shape
    ff = slope.shape[1]
    mt = fold(n, FEED_ROWS)
    last = ff // d - 1

    def body(gu_ref, slope_ref, wd_ref, wu_ref, gi_ref, bias_ref, out_ref, acc):
        f = pl.program_id(0)
        m = pl.program_id(1)
        rows = pl.ds(pl.multiple_of(m * mt, mt), mt)
        gi = (mm(gu_ref[...], wd_ref[...], NT) * slope_ref[...].astype(F32)).astype(BF16)
        gi_ref[...] = gi
        total = column_sum(gi.astype(F32))

        @pl.when(m == 0)
        def _():
            bias_ref[...] = total

        @pl.when(m > 0)
        def _():
            bias_ref[...] += total

        part = mm(gi, wu_ref[...], NT)

        @pl.when(f == 0)
        def _():
            acc[rows, :] = part

        @pl.when((f > 0) & (f < last))
        def _():
            acc[rows, :] += part

        @pl.when(f == last)
        def _():
            out_ref[...] = acc[rows, :] + part

    return call(
        body,
        (ff // d, n // mt),
        [
            pl.BlockSpec((mt, d), lambda f, m: (m, 0)),
            pl.BlockSpec((mt, d), lambda f, m: (m, f)),
            pl.BlockSpec((d, d), lambda f, m: (f, 0)),
            pl.BlockSpec((d, d), lambda f, m: (0, f)),
        ],
        [
            pl.BlockSpec((mt, d), lambda f, m: (m, f)),
            pl.BlockSpec((1, d), lambda f, m: (0, f)),
            pl.BlockSpec((mt, d), lambda f, m: (jnp.where(f == last, m, 0), 0)),
        ],
        [sds((n, ff), BF16), sds((1, ff), F32), sds((n, d), F32)],
        [pltpu.VMEM((n, d), F32)],
        flops=4 * n * d * ff,
        nbytes=2 * (2 * d * ff + 2 * n * ff + 3 * n * d),
        deps=deps,
    )(gu, slope, w_down, w_up)


def norm_back(grad, v, r, stretch):
    dn = grad * stretch
    return r * (
        dn - jnp.mean(dn, axis=-1, keepdims=True) - v * jnp.mean(dn * v, axis=-1, keepdims=True)
    )


def middle_back(gh, mid, branch, go, upd, mods, w, seq, deps=()):
    n, d = gh.shape
    mt = fold(n, 256)
    wide = d // seq

    def body(
        gh_ref, mid_ref, branch_ref, go_ref, upd_ref, mod_ref, w_ref,
        gmid_ref, gb_ref, cut_ref, ga_ref, sum_ref,
    ):
        @pl.when(pl.program_id(0) == 0)
        def _():
            sum_ref[...] = jnp.zeros_like(sum_ref)

        g = gh_ref[...]
        v, r = standard(mid_ref[...])
        sum_ref[0:1, :] += column_sum(g * v)
        sum_ref[1:2, :] += column_sum(g)
        go = go_ref[...].astype(F32)
        sum_ref[4:5, :] += column_sum(go * upd_ref[...].astype(F32))
        gmid = go + norm_back(g, v, r, 1.0 + mod_ref[4:5, :])
        gmid_ref[...] = gmid
        sum_ref[2:3, :] += column_sum(gmid * branch_ref[...].astype(F32))
        low = (mod_ref[2:3, :] * gmid).astype(BF16)
        gb_ref[...] = low
        for s in range(seq):
            cut_ref[s] = low[:, s * wide : (s + 1) * wide]
        sum_ref[3:4, :] += column_sum(low.astype(F32))
        ga_ref[...] = mm(low, w_ref[...], NT).astype(BF16)

    tile = pl.BlockSpec((mt, d), lambda m: (m, 0))
    return call(
        body,
        (n // mt,),
        [tile, tile, tile, tile, tile, whole((8, d)), whole((d, d))],
        [tile, tile, pl.BlockSpec((seq, mt, wide), lambda m: (0, m, 0)), tile, whole((8, d))],
        [
            sds((n, d), F32),
            sds((n, d), BF16),
            sds((seq, n, wide), BF16),
            sds((n, d), BF16),
            sds((8, d), F32),
        ],
        flops=2 * n * d * d,
        nbytes=2 * (d * d + 11 * n * d),
        deps=deps,
    )(gh, mid, branch, go, upd, mods, w)


def attention_back(qkv, ga, lse, temporal, seq, deps=()):
    a, g, p, wide = qkv.shape
    d = wide // 3
    size = d // HEADS
    t = a * p
    scale = size ** (-0.5)
    cut = wide // seq

    def body(qkv_ref, ga_ref, lse_ref, out_ref, cut_ref, sum_ref, acc):
        acc[...] = jnp.zeros_like(acc)
        if temporal:
            ki = lax.broadcasted_iota(jnp.int32, (t, t), 0)
            qi = lax.broadcasted_iota(jnp.int32, (t, t), 1)
            same = lax.rem(qi, p) == lax.rem(ki, p)
        for h in range(HEADS):
            lo, hi, off = window(h, size, d)
            keep = head_mask(lo, hi, off, size, t)
            q = qkv_ref[:, 0, :, lo:hi].reshape(t, hi - lo)
            k = qkv_ref[:, 0, :, d + lo : d + hi].reshape(t, hi - lo)
            v = qkv_ref[:, 0, :, 2 * d + lo : 2 * d + hi].reshape(t, hi - lo)
            o = ga_ref[:, 0, :, lo:hi].reshape(t, hi - lo)
            zero = jnp.zeros_like(q)
            q, o = jnp.where(keep, q, zero), jnp.where(keep, o, zero)
            s = mm(k, q, NT) * scale
            probs = jnp.exp(s - lse_ref[0, h : h + 1, :])
            if temporal:
                probs = jnp.where(same, probs, 0.0)
            dp = mm(v, o, NT)
            acc[:, 2 * d + lo : 2 * d + hi] += mm(probs.astype(BF16), o)
            ds = (probs * (dp - column_sum(probs * dp))).astype(BF16)
            acc[:, d + lo : d + hi] += mm(ds, q) * scale
            acc[:, lo:hi] += mm(ds, jnp.where(keep, k, zero), TN) * scale
        low = acc[...].astype(BF16)
        out_ref[...] = low.reshape(a, 1, p, wide)
        for s in range(seq):
            cut_ref[s] = low[:, s * cut : (s + 1) * cut].reshape(a, 1, p, cut)
        total = column_sum(low.astype(F32))

        @pl.when(pl.program_id(0) == 0)
        def _():
            sum_ref[...] = total

        @pl.when(pl.program_id(0) > 0)
        def _():
            sum_ref[...] += total

    return call(
        body,
        (g,),
        [
            pl.BlockSpec((a, 1, p, wide), lambda i: (0, i, 0, 0)),
            pl.BlockSpec((a, 1, p, d), lambda i: (0, i, 0, 0)),
            pl.BlockSpec((1, HEADS, t), lambda i: (i, 0, 0)),
        ],
        [
            pl.BlockSpec((a, 1, p, wide), lambda i: (0, i, 0, 0)),
            pl.BlockSpec((seq, a, 1, p, cut), lambda i: (0, 0, i, 0, 0)),
            whole((1, wide)),
        ],
        [sds((a, g, p, wide), BF16), sds((seq, a, g, p, cut), BF16), sds((1, wide), F32)],
        [pltpu.VMEM((t, wide), F32)],
        flops=12 * g * HEADS * t * t * 256,
        nbytes=2 * a * g * p * (3 * wide + d),
        deps=deps,
    )(qkv, ga, lse)


def stream_back(gqkv, w, x, gmid, mods, out_dtype, shape=None, deps=()):
    n, wide = gqkv.shape
    d = w.shape[0]
    mt = fold(n, 256) if shape is None else n // shape[0]

    def body(g_ref, w_ref, x_ref, gmid_ref, mod_ref, out_ref, sum_ref):
        @pl.when(pl.program_id(0) == 0)
        def _():
            sum_ref[...] = jnp.zeros_like(sum_ref)

        grad = mm(g_ref[...], w_ref[...], NT)
        v, r = standard(x_ref[...].astype(F32))
        sum_ref[0:1, :] += column_sum(grad * v)
        sum_ref[1:2, :] += column_sum(grad)
        out = gmid_ref[...] + norm_back(grad, v, r, 1.0 + mod_ref[1:2, :])
        out_ref[...] = out.astype(out_dtype).reshape(out_ref.shape)

    tile = pl.BlockSpec((mt, d), lambda m: (m, 0))
    result, block = sds((n, d), out_dtype), tile
    if shape is not None:
        parts, frames, places = shape
        result = sds((frames, parts, places, d), out_dtype)
        block = pl.BlockSpec((frames, 1, places, d), lambda m: (0, m, 0, 0))
    return call(
        body,
        (n // mt,),
        [
            pl.BlockSpec((mt, wide), lambda m: (m, 0)),
            whole((d, wide)),
            tile,
            tile,
            whole((8, d)),
        ],
        [block, whole((8, d))],
        [result, sds((8, d), F32)],
        flops=2 * n * d * wide,
        nbytes=2 * (d * wide + n * wide + 5 * n * d),
        deps=deps,
    )(gqkv, w, x, gmid, mods)


def collect(sums, deps=()):
    flat = [item for layer in sums for item in layer]
    d = flat[0].shape[1]
    ups = flat[4].shape[1] // d
    each = 4 + ups

    def body(*refs):
        mod_ref, bias_ref = refs[len(flat) :]
        for k in range(len(sums)):
            stream, middle, update, qkv, up = refs[5 * k : 5 * k + 5]
            rows = (
                (stream, 1), (stream, 0), (middle, 2), (middle, 1), (middle, 0), (middle, 4)
            )
            for r, (ref, at) in enumerate(rows):
                mod_ref[6 * k + r : 6 * k + r + 1, :] = ref[at : at + 1, :]
            base = each * k
            bias_ref[base : base + 1, :] = qkv[:, :d]
            bias_ref[base + 1 : base + 2, :] = qkv[:, 2 * d :]
            bias_ref[base + 2 : base + 3, :] = middle[3:4, :]
            bias_ref[base + 3 : base + 4, :] = update[0:1, :]
            for u in range(ups):
                bias_ref[base + 4 + u : base + 5 + u, :] = up[:, u * d : (u + 1) * d]

    shapes = [(6 * len(sums), d), (each * len(sums), d)]
    return call(
        body,
        (1,),
        [whole(item.shape) for item in flat],
        [whole(shape) for shape in shapes],
        [sds(shape, F32) for shape in shapes],
        deps=deps,
    )(*flat)


def laid_out(pairs):
    count = len(pairs)
    flat = [item for pair in pairs for item in pair]
    _, half, rows, d = flat[0].shape

    def body(*refs):
        for k in range(count):
            refs[-1][k, 0, :half] = refs[2 * k][0]
            refs[-1][k, 0, half:] = refs[2 * k + 1][0]

    return call(
        body,
        (1,),
        [whole(item.shape) for item in flat],
        whole((count, 1, 2 * half, rows, d)),
        sds((count, 1, 2 * half, rows, d), BF16),
        nbytes=8 * count * half * rows * d,
    )(*flat)


def add_pieces(left, right, deps=()):
    seq, zs, rows, d = left.shape

    def body(left_ref, right_ref, out_ref):
        out_ref[...] = (left_ref[...].astype(F32) + right_ref[...].astype(F32)).astype(BF16)

    piece = pl.BlockSpec((1, zs, rows, d), lambda i: (i, 0, 0, 0))
    return call(
        body,
        (seq,),
        [piece, piece],
        piece,
        sds(left.shape, BF16),
        nbytes=6 * seq * zs * rows * d,
        deps=deps,
    )(left, right)


def join_qkv_out(place, own, got, which, deps=()):
    seq, _, zs, rows, d = own.shape
    wide = d * 3 // 4

    def body(place_ref, own_ref, got_ref, qkv_ref, out_ref):
        def put(c, src):
            span = slice(c * rows, (c + 1) * rows)
            qkv_ref[span, :] = jnp.concatenate([src[s ^ place_ref[2], 0, 0, :, :wide] for s in range(seq)], axis=1)
            out_ref[span, :] = jnp.concatenate([src[s ^ place_ref[2], 0, 0, :, wide:] for s in range(seq)], axis=1)

        for c in range(2):

            @pl.when(place_ref[0] == c)
            def _(c=c):
                put(c, own_ref)
                put(1 - c, got_ref)

    piece = pl.BlockSpec(
        (seq, 1, 1, rows, d), lambda i, place_ref: (0, which, slot(i ^ place_ref[1]), 0, 0)
    )
    return call(
        body,
        (zs,),
        [piece, piece],
        [
            pl.BlockSpec((2 * rows, seq * wide), lambda i, place_ref: (i, 0)),
            pl.BlockSpec((2 * rows, d), lambda i, place_ref: (i, 0)),
        ],
        [sds((2 * rows * zs, seq * wide), BF16), sds((2 * rows * zs, d), BF16)],
        scalars=1,
        nbytes=8 * seq * zs * rows * d,
        deps=deps,
    )(place, own, got)


def join_up(place, own, got, which, deps=()):
    seq, _, zs, rows, d = own.shape

    def body(place_ref, own_ref, got_ref, up_ref):
        for c in range(2):

            @pl.when(place_ref[0] == c)
            def _(c=c):
                for s in range(seq):
                    cols = slice(s * d, (s + 1) * d)
                    up_ref[c * rows : (c + 1) * rows, cols] = own_ref[s ^ place_ref[2], 0, 0]
                    up_ref[(1 - c) * rows : (2 - c) * rows, cols] = got_ref[s ^ place_ref[2], 0, 0]

    piece = pl.BlockSpec(
        (seq, 1, 1, rows, d), lambda i, place_ref: (0, which, slot(i ^ place_ref[1]), 0, 0)
    )
    return call(
        body,
        (zs,),
        [piece, piece],
        pl.BlockSpec((2 * rows, seq * d), lambda i, place_ref: (i, 0)),
        sds((2 * rows * zs, seq * d), BF16),
        scalars=1,
        nbytes=8 * seq * zs * rows * d,
        deps=deps,
    )(place, own, got)


def join_down(place, own, got, which, deps=()):
    seq, _, zs, rows, d = own.shape
    quarter = d // seq
    parts = d // quarter

    def body(place_ref, own_ref, got_ref, down_ref):
        def put(c, src):
            for q in range(parts):
                base = (c * parts + q) * rows
                cols = slice(q * quarter, (q + 1) * quarter)
                down_ref[base : base + rows, :] = jnp.concatenate(
                    [src[s ^ place_ref[2], 0, 0, :, cols] for s in range(seq)], axis=1
                )

        for c in range(2):

            @pl.when(place_ref[0] == c)
            def _(c=c):
                put(c, own_ref)
                put(1 - c, got_ref)

    piece = pl.BlockSpec(
        (seq, 1, 1, rows, d), lambda i, place_ref: (0, which, slot(i ^ place_ref[1]), 0, 0)
    )
    return call(
        body,
        (zs,),
        [piece, piece],
        pl.BlockSpec((2 * parts * rows, d), lambda i, place_ref: (i, 0)),
        sds((2 * parts * rows * zs, d), BF16),
        scalars=1,
        nbytes=8 * seq * zs * rows * d,
        deps=deps,
    )(place, own, got)


clip_limit = 8.0
CLIP = ("z", "core")


def hop(x, distance, count):
    return lax.ppermute(x, CLIP, [(i, i ^ distance) for i in range(count)])


def on_device(
    video_latents,
    conditioning,
    ada_weight,
    ada_bias,
    qkv_weight,
    out_weight,
    up_weight,
    down_weight,
    attention_bias,
    up_bias,
    down_bias,
    cotangent,
    *,
    clips,
    seq,
):
    zs = clips // 2
    layers, rows, own_columns = qkv_weight.shape
    d = video_latents.shape[-1]
    frames, places = video_latents.shape[1:3]
    n = frames * places
    ff = up_bias.shape[1]
    clip_index = lax.axis_index(CLIP)
    seq_index = lax.axis_index("seq")
    place = jnp.stack([clip_index % 2, clip_index // 2, 0 * seq_index]).astype(jnp.int32)
    packed = zs == 4 and seq == 4 and rows % 16 == 0 and down_weight.shape[1] % rows == 0 and d % seq == 0
    cuts = seq if packed else 1

    def total(v, *axes):
        for axis, count in axes:
            step = 1
            while step < count:
                v = v + lax.ppermute(v, axis, [(i, i ^ step) for i in range(count)])
                step *= 2
        return v

    def modulate(first, second):
        own_place = (clip_index, jnp.zeros_like(clip_index))
        placed = lax.dynamic_update_slice(jnp.zeros((clips, d), F32), conditioning, own_place)
        if first:
            placed = gate(placed, first)
        squashed = jax.nn.silu(total(placed, (CLIP, clips))).astype(BF16)
        local_mods = (
            jnp.einsum("kd,ldc->klc", squashed, ada_weight, preferred_element_type=F32)
            + ada_bias[None, :, :]
        )
        if second:
            local_mods = gate(local_mods, second)
        own_mods = lax.all_to_all(local_mods, CLIP, 0, 0, tiled=True)
        every_mod = lax.all_gather(own_mods, "seq", axis=0, tiled=False)
        modulation = every_mod.transpose(2, 1, 0, 3).reshape(layers, 6, d)
        return squashed, jnp.pad(modulation, ((0, 0), (0, 2), (0, 0)))

    def far(block):
        return hop(block, 4, clips)

    def near(block):
        return hop(block, 2, clips)

    def put(*parts):
        return jnp.concatenate(parts, axis=1)

    def pack_rows(layer):
        tall = down_weight[layer].reshape(-1, rows, d // seq)
        return (
            jnp.concatenate([qkv_weight[layer], out_weight[layer]], axis=1),
            up_weight[layer],
            tall.transpose(1, 0, 2).reshape(rows, d),
        )

    def along_seq(blocks):
        return lax.all_gather(blocks, "seq", axis=0, tiled=False)

    def both_cores(own, deps):
        own = gate(own, deps)
        return own, hop(own, 1, clips)

    def fetch_natural(layer):
        return tuple(
            lax.all_gather(
                lax.all_gather(item[layer], CLIP, axis=0, tiled=True), "seq", axis=1, tiled=True
            )
            for item in (qkv_weight, out_weight, up_weight, down_weight)
        )

    def reduce_seq(half):
        flat = lax.psum_scatter(half.reshape(-1, d), "seq", scatter_dimension=0, tiled=True)
        return flat.reshape(zs, rows, d)

    def first_half(part):
        return hop(part[2:], 2, clips)

    def add_first(part, got):
        return (part[:2].astype(F32) + got.astype(F32)).astype(BF16)

    def second_half(part):
        return hop(part[1], 4, clips)

    def add_second(part, got):
        return part[0].astype(F32) + got.astype(F32)

    def shed_natural(left, right):
        full = mm(left, right, TN).astype(BF16)
        part = lax.psum_scatter(full, "seq", scatter_dimension=1, tiled=True)
        return lax.psum_scatter(part, CLIP, scatter_dimension=0, tiled=True).astype(F32)

    def swap_tokens(x):
        block = x.reshape(seq, n // seq, d)
        return lax.all_to_all(block, "seq", 0, 0, tiled=True).reshape(n, d)

    def by_places(x):
        return x.reshape(frames, seq, places // seq, d).transpose(1, 0, 2, 3).reshape(n, d)

    def by_frames(x):
        return (
            x.reshape(seq, frames, places // seq, d)
            .transpose(1, 0, 2, 3)
            .reshape(1, frames, places, d)
        )

    shapes = (
        (seq, frames, places // seq),
        (seq * frames, places // seq // 16, 16),
    )

    def qkv_bias_of(layer):
        bias = attention_bias[layer]
        return jnp.concatenate([bias[0], jnp.zeros_like(bias[0]), bias[1]])[None]

    def forward_natural(layer, x, modulation):
        mods = modulation[layer]
        qkv_full, out_full, up_full, down_full = fetch_natural(layer)
        hidden, qkv = qkv_forward(x, mods, qkv_full, qkv_bias_of(layer))
        qkv = qkv.reshape(shapes[layer] + (3 * d,))
        attended, lse, peak = attention_forward(qkv, layer == 1)
        attended = attended.reshape(n, d)
        out_bias = attention_bias[layer, 2:3]
        branch, middle, hidden_two = out_forward(attended, x, mods, out_full, out_bias)
        active, slope = up_forward(hidden_two, up_full, up_bias[layer : layer + 1])
        update, result = down_forward(
            active, middle, mods, down_full, down_bias[layer : layer + 1]
        )
        kept = (x, hidden, qkv, lse, attended, branch, middle, hidden_two, active, slope, update)
        weights = (qkv_full, out_full, up_full, down_full)
        return result, kept, weights, jnp.max(peak, axis=(0, 1))

    def backward_natural(layer, grad_out, kept, weights, modulation):
        x, hidden, qkv, lse, attended, branch, middle, hidden_two, active, slope, update = kept
        qkv_full, out_full, up_full, down_full = weights
        mods = modulation[layer]
        grad_update, update_sums = update_back(grad_out, mods)
        inner_grad, up_sums, hidden_grad = feed_back(grad_update, slope, down_full, up_full)
        middle_grad, branch_grad, _, attended_grad, middle_sums = middle_back(
            hidden_grad, middle, branch, grad_out, update, mods, out_full, 1
        )
        qkv_grad, _, qkv_sums = attention_back(
            qkv, attended_grad.reshape(shapes[layer] + (d,)), lse, layer == 1, 1
        )
        qkv_grad = qkv_grad.reshape(n, 3 * d)
        stream_grad, stream_sums = stream_back(
            qkv_grad, qkv_full, x, middle_grad, mods, BF16 if layer == 1 else F32
        )
        parts = (
            shed_natural(hidden, qkv_grad),
            shed_natural(attended, branch_grad),
            shed_natural(hidden_two, inner_grad),
            shed_natural(active, grad_update),
        )
        if layer == 0:
            stream_grad = by_frames(stream_grad)
        return stream_grad, (stream_sums, middle_sums, update_sums, qkv_sums, up_sums), parts

    def unpack(parts):
        down_g, up_g, both = parts
        down_g = down_g.reshape(rows, -1, d // seq).transpose(1, 0, 2).reshape(-1, d // seq)
        return both[:, :own_columns], both[:, own_columns:], up_g, down_g

    def run_natural():
        squashed, modulation = modulate((), ())
        first_in = by_places(video_latents)
        second_go = swap_tokens(by_places(cotangent))
        first_out, first_kept, first_weights, first_peak = forward_natural(0, first_in, modulation)
        second_in = swap_tokens(first_out)
        second_out, second_kept, second_weights, second_peak = forward_natural(1, second_in, modulation)
        second_grad, second_sums, second_parts = backward_natural(
            1, second_go, second_kept, second_weights, modulation
        )
        first_grad, first_sums, first_parts = backward_natural(
            0, swap_tokens(second_grad), first_kept, first_weights, modulation
        )
        peaks = (first_peak, second_peak)
        sums = (first_sums, second_sums)
        second_out = swap_tokens(second_out)

        def finish(small, own_mod_grad, exchanged):
            return total(small, (CLIP, clips), ("seq", seq)), first_parts, second_parts

        return squashed, second_out, first_grad, peaks, collect(sums), finish

    def run_packed():
        first_pack, second_pack = pack_rows(0), pack_rows(1)
        first_in = by_places(video_latents)
        second_go = swap_tokens(by_places(cotangent))

        block = first_pack[0][None, None]
        pair = put(block, far(block))
        squashed, modulation = modulate((), ())
        line_q0 = put(pair, gate(near(pair), (second_go,)))
        block = gate(first_pack[1][None, None], (line_q0,))
        pair = put(block, far(block))
        line_u0 = put(pair, gate(near(pair), (modulation,)))
        block = gate(first_pack[2][None, None], (line_u0,))
        pair_d0 = put(block, far(block))
        whole_q0 = along_seq(line_q0)
        whole_u0 = along_seq(line_u0)

        def attention_part(layer, x, qkv, out_full):
            qkv = qkv.reshape(shapes[layer] + (3 * d,))
            attended, lse, peak = attention_forward(qkv, layer == 1)
            return qkv, attended.reshape(n, d), lse, jnp.max(peak, axis=(0, 1))

        mods = modulation[0]
        qkv_full, out_full = join_qkv_out(place, *both_cores(whole_q0, (pair_d0,)), 0)
        hidden, qkv = qkv_forward(first_in, mods, qkv_full, qkv_bias_of(0))
        hidden, qkv, got = joint(hidden, qkv, near(pair_d0))
        line_d0 = put(pair_d0, got)
        whole_d0 = along_seq(line_d0)
        block_q1 = gate(second_pack[0][None, None], (got,))
        qkv, attended, lse, peak0 = attention_part(0, first_in, qkv, out_full)
        attended, lse, got = joint(attended, lse, far(block_q1))
        pair_q1 = put(block_q1, got)
        branch, middle, hidden_two = out_forward(
            attended, first_in, mods, out_full, attention_bias[0, 2:3]
        )
        branch, middle, hidden_two, got = joint(branch, middle, hidden_two, near(pair_q1))
        line_q1 = put(pair_q1, got)
        whole_q1 = along_seq(line_q1)
        block_f1 = gate(jnp.stack(second_pack[1:])[:, None], (got,))
        up_full = join_up(place, *both_cores(whole_u0, (branch,)), 0, deps=(line_q1, line_d0))
        active, slope = up_forward(hidden_two, up_full, up_bias[:1])
        active, slope, got = joint(active, slope, far(block_f1))
        pair_f1 = put(block_f1, got)
        down_full = join_down(place, *both_cores(whole_d0, (active,)), 0, deps=(pair_f1,))
        update, result = down_forward(active, middle, mods, down_full, down_bias[:1])
        update, result, got = joint(update, result, near(pair_f1))
        line_f1 = put(pair_f1, got)
        whole_u1, whole_d1 = along_seq(line_f1[:1]), along_seq(line_f1[1:])
        kept0 = (
            first_in, hidden, qkv, lse, attended, branch, middle, hidden_two, active, slope, update
        )
        weights0 = (qkv_full, out_full, up_full, down_full)
        second_in = swap_tokens(result)

        mods = modulation[1]
        own, got = both_cores(whole_q1, (second_in, line_f1))
        qkv_full, out_full = join_qkv_out(place, own, got, 0)
        hidden, qkv = qkv_forward(second_in, mods, qkv_full, qkv_bias_of(1))
        qkv, attended, lse, peak1 = attention_part(1, second_in, qkv, out_full)
        branch, middle, hidden_two = out_forward(
            attended, second_in, mods, out_full, attention_bias[1, 2:3]
        )
        own, got = both_cores(whole_u1, (attended,))
        branch, middle, hidden_two, got = joint(branch, middle, hidden_two, got)
        up_full = join_up(place, own, got, 0)
        active, slope = up_forward(hidden_two, up_full, up_bias[1:2])
        grad_update, update_sums1 = update_back(second_go, mods, deps=(active,))
        down_m, down_o = down_grad(place, active, grad_update, seq, zs)
        own, got = both_cores(whole_d1, (down_m,))
        half_d1 = add_pieces(down_m, hop(down_o, 1, clips), deps=(own,))
        half_d1, got = joint(half_d1, got)
        part_d1 = reduce_seq(half_d1)
        down_full = join_down(place, own, got, 0)
        update, result = down_forward(
            active, middle, mods, down_full, down_bias[1:2], deps=(half_d1,)
        )
        kept1 = (
            second_in, hidden, qkv, lse, attended, branch, middle, hidden_two, active, slope, update
        )
        weights1 = (qkv_full, out_full, up_full, down_full)
        kept, weights = (kept0, kept1), (weights0, weights1)

        def up_stage(layer, hidden_grad, inner_grad, grad_out, deps):
            _, _, _, _, _, branch, middle, hidden_two, _, _, update = kept[layer]
            up_m, up_o = up_grad(place, hidden_two, inner_grad, seq, zs, deps=deps)
            middle_grad, _, branch_cut, attended_grad, middle_sums = middle_back(
                hidden_grad, middle, branch, grad_out, update, modulation[layer],
                weights[layer][1], cuts, deps=(up_m,),
            )
            half_u = add_pieces(up_m, hop(up_o, 1, clips), deps=(middle_grad,))
            return half_u, reduce_seq(half_u), middle_grad, branch_cut, attended_grad, middle_sums

        def attention_stage(layer, attended_grad, deps):
            _, _, qkv, lse = kept[layer][:4]
            grad = attended_grad.reshape(shapes[layer] + (d,))
            qkv_grad, qkv_cut, qkv_sums = attention_back(
                qkv, grad, lse, layer == 1, cuts, deps=deps
            )
            return qkv_grad.reshape(n, 3 * d), qkv_cut.reshape(seq, n, -1), qkv_sums

        def last_grad(layer, qkv_cut, branch_cut, deps):
            hidden, attended = kept[layer][1], kept[layer][4]
            return qkv_out_grad(place, hidden, attended, qkv_cut, branch_cut, zs, deps=deps)

        inner_grad, up_sums, hidden_grad = feed_back(
            grad_update, kept1[9], weights1[3], weights1[2], deps=(result,)
        )
        inner_grad, hidden_grad, second_out = joint(inner_grad, hidden_grad, swap_tokens(result))
        half_u, part_u1, middle_grad, branch_cut, attended_grad, middle_sums = up_stage(
            1, hidden_grad, inner_grad, second_go, ()
        )
        qkv_grad, qkv_cut, qkv_sums = attention_stage(1, attended_grad, (half_u, part_d1))
        qkv_grad, qkv_cut, got = joint(qkv_grad, qkv_cut, first_half(part_d1))
        sum_d1 = add_first(part_d1, got)
        stream_grad, stream_sums = stream_back(
            qkv_grad, weights1[0], kept1[0], middle_grad, modulation[1], BF16
        )
        stream_grad, stream_sums, got = joint(stream_grad, stream_sums, second_half(sum_d1))
        down_g1 = add_second(sum_d1, got)
        second_sums = (stream_sums, middle_sums, update_sums1, qkv_sums, up_sums)
        last_m, last_o = last_grad(1, qkv_cut, branch_cut, (stream_grad,))
        last_m, last_o, first_go = joint(last_m, last_o, swap_tokens(stream_grad))

        grad_update, update_sums = update_back(first_go, modulation[0])
        half_q1 = add_pieces(last_m, hop(last_o, 1, clips), deps=(grad_update,))
        part_q1 = reduce_seq(half_q1)
        down_m, down_o = down_grad(place, kept0[8], grad_update, seq, zs, deps=(half_q1,))
        inner_grad, up_sums, hidden_grad = feed_back(
            grad_update, kept0[9], weights0[3], weights0[2], deps=(down_m, part_u1)
        )
        inner_grad, hidden_grad, got = joint(inner_grad, hidden_grad, first_half(part_u1))
        sum_u1 = add_first(part_u1, got)
        half_d0 = add_pieces(down_m, hop(down_o, 1, clips), deps=(hidden_grad, part_q1))
        part_d0 = reduce_seq(half_d0)
        half_u, part_u0, middle_grad, branch_cut, attended_grad, middle_sums = up_stage(
            0, hidden_grad, inner_grad, first_go, (half_d0, sum_u1)
        )
        qkv_grad, qkv_cut, qkv_sums = attention_stage(0, attended_grad, (half_u,))
        qkv_grad, qkv_cut, got, got2 = joint(
            qkv_grad, qkv_cut, first_half(part_q1), second_half(sum_u1)
        )
        sum_q1 = add_first(part_q1, got)
        up_g1 = add_second(sum_u1, got2)
        last_m, last_o = last_grad(0, qkv_cut, branch_cut, (part_d0, sum_q1))
        last_m, last_o, got, got2 = joint(last_m, last_o, first_half(part_d0), second_half(sum_q1))
        sum_d0 = add_first(part_d0, got)
        both_g1 = add_second(sum_q1, got2)
        first_grad, stream_sums = stream_back(
            qkv_grad, weights0[0], kept0[0], middle_grad, modulation[0], F32, shape=shapes[0],
            deps=(last_m, sum_d0),
        )
        first_grad, stream_sums, got = joint(first_grad, stream_sums, second_half(sum_d0))
        down_g0 = add_second(sum_d0, got)
        first_sums = (stream_sums, middle_sums, update_sums, qkv_sums, up_sums)
        half = add_pieces(last_m, hop(last_o, 1, clips), deps=(first_grad,))
        part_q0 = reduce_seq(half)
        rows_of = collect((first_sums, second_sums), deps=(half,))

        def finish(small, own_mod_grad, exchanged):
            sum_u0 = add_first(part_u0, exchanged)
            up_g0 = add_second(sum_u0, second_half(sum_u0))
            part = gate(part_q0, (up_g0,))
            sum_q0 = add_first(part, first_half(part))
            both_g0 = add_second(sum_q0, second_half(sum_q0))
            early = [gate(item, (own_mod_grad,)) for item in (down_g1, up_g1, both_g1, down_g0)]
            small = total(small, (CLIP, clips), ("seq", seq))
            return small, unpack((early[3], up_g0, both_g0)), unpack(early[:3])

        finish.exchange = lambda: first_half(part_u0)
        return squashed, second_out, first_grad, (peak0, peak1), rows_of, finish

    run = run_packed if packed else run_natural
    squashed, second_out, latents_grad, peaks, (mod_grads, bias_rows), finish = run()
    output_latents = by_frames(second_out)

    mod_grads = total(mod_grads, ("seq", seq)).reshape(layers, clips, seq, -1)
    of_columns = lax.dynamic_index_in_dim(mod_grads, lax.axis_index("seq"), 2, keepdims=False)
    own_mod_grad = lax.all_to_all(of_columns.transpose(1, 0, 2), CLIP, 0, 0, tiled=True)
    exchanged = None
    if packed:
        own_mod_grad, exchanged = joint(own_mod_grad, finish.exchange())
    ada_bias_grad = jnp.sum(own_mod_grad, axis=0)
    rounded_mod = own_mod_grad.astype(BF16)
    ada_weight_grad = jnp.einsum("kd,klc->ldc", squashed, rounded_mod, preferred_element_type=F32)
    squash_part = jnp.einsum("klc,ldc->kd", rounded_mod, ada_weight, preferred_element_type=F32)
    bias_count = bias_rows.shape[0]
    devices = clips * seq
    device = clip_index * seq + lax.axis_index("seq")
    peak_rows = -(-devices * layers * HEADS // d)
    own_peaks = jnp.concatenate(peaks)[None]
    placed = lax.dynamic_update_slice(
        jnp.zeros((devices, layers * HEADS), F32), own_peaks, (device, 0)
    ).reshape(-1)
    placed = jnp.pad(placed, (0, peak_rows * d - placed.shape[0])).reshape(peak_rows, d)
    summed, first_shed, second_shed = finish(
        jnp.concatenate([bias_rows, squash_part, placed], axis=0), own_mod_grad, exchanged
    )
    bias_sums = summed[:bias_count].reshape(layers, -1, d)
    own_squash = lax.dynamic_slice_in_dim(summed, bias_count + clip_index, 1, axis=0)
    peaks = summed[bias_count + clips :].reshape(-1)[: devices * layers * HEADS]
    logit_peak = jnp.max(peaks.reshape(devices, layers, HEADS), axis=0)
    column_index = lax.axis_index("seq") * own_columns + jnp.arange(own_columns, dtype=jnp.int32)
    head_of = column_index % d // (d // HEADS)
    head_match = (head_of[:, None] == jnp.arange(HEADS, dtype=jnp.int32)[None, :]).astype(F32)
    roots = jnp.sqrt(clip_limit / jnp.maximum(logit_peak, clip_limit))
    column_roots = jnp.sum(roots[:, None, :] * head_match[None, :, :], axis=-1)
    column_scale = jnp.where(column_index[None, :] < 2 * d, column_roots, 1.0)
    clipped_qkv = qkv_weight.astype(F32) * column_scale[:, None, :]
    silu_value, silu_pull = jax.vjp(jax.nn.silu, conditioning)
    conditioning_grad = silu_pull(own_squash)[0]
    return (
        output_latents,
        latents_grad.reshape(1, frames, places, d),
        conditioning_grad,
        ada_weight_grad,
        ada_bias_grad,
        jnp.stack([first_shed[0], second_shed[0]]),
        jnp.stack([first_shed[1], second_shed[1]]),
        jnp.stack([first_shed[2], second_shed[2]]),
        jnp.stack([first_shed[3], second_shed[3]]),
        bias_sums[:, :3],
        bias_sums[:, 4:].reshape(layers, ff),
        bias_sums[:, 3],
        clipped_qkv,
        logit_peak,
    )


def solution(mesh):
    clips, seq = mesh.shape["clip"], mesh.shape["seq"]
    finer = jax.sharding.Mesh(
        mesh.devices.reshape(clips // 2, 2, seq), ("z", "core", "seq")
    )
    every = (*CLIP, "seq")
    tokens = P(CLIP, "seq", None, None)
    matrix = P(None, CLIP, "seq")
    return jax.shard_map(
        partial(on_device, clips=clips, seq=seq),
        mesh=finer,
        in_specs=(
            tokens,
            P(CLIP, None),
            P(None, None, every),
            P(None, every),
            matrix,
            matrix,
            matrix,
            matrix,
            P(),
            P(),
            P(),
            tokens,
        ),
        out_specs=(
            tokens,
            tokens,
            P(CLIP, None),
            P(None, None, every),
            P(None, every),
            matrix,
            matrix,
            matrix,
            matrix,
            P(),
            P(),
            P(),
            matrix,
            P(),
        ),
        check_vma=False,
    )
```

```python
from functools import partial

import jax
import jax.numpy as jnp
from jax import lax
from jax.experimental import pallas as pl
from jax.experimental.pallas import tpu as pltpu
from jax.sharding import PartitionSpec as P

HEADS = 16
F32 = jnp.float32
BF16 = jnp.bfloat16
NN = (((1,), (0,)), ((), ()))
NT = (((1,), (1,)), ((), ()))
TN = (((0,), (0,)), ((), ()))
VMEM_BYTES = 56 * 1024 * 1024
FEED_ROWS = 1024
UP_ROWS, UP_CUTS = 1024, 1
QKV_ROWS = 512


def mm(a, b, dims=NN):
    return lax.dot_general(a, b, dims, preferred_element_type=F32)


def call(
    body, grid, in_specs, out_specs, out_shape, scratch=(), scalars=0, flops=0, nbytes=0, deps=()
):
    first = scalars + len(in_specs)

    def run(*refs):
        body(*refs[:first], *refs[first + len(deps) :])

    kernel = pl.pallas_call(
        run,
        grid_spec=pltpu.PrefetchScalarGridSpec(
            num_scalar_prefetch=scalars,
            grid=grid,
            in_specs=[*in_specs, *[pl.BlockSpec(memory_space=pl.ANY)] * len(deps)],
            out_specs=out_specs,
            scratch_shapes=list(scratch),
        ),
        out_shape=out_shape,
        compiler_params=pltpu.CompilerParams(
            dimension_semantics=("arbitrary",) * len(grid), vmem_limit_bytes=VMEM_BYTES
        ),
        cost_estimate=pl.CostEstimate(flops=flops, bytes_accessed=nbytes, transcendentals=0),
    )
    return lambda *args: kernel(*args, *deps)


def gate(x, deps):
    def body(*refs):
        pass

    anywhere = pl.BlockSpec(memory_space=pl.ANY)
    return pl.pallas_call(
        body,
        in_specs=[anywhere] * (1 + len(deps)),
        out_specs=anywhere,
        out_shape=sds(x.shape, x.dtype),
        input_output_aliases={0: 0},
    )(x, *deps)


def joint(*arrays):
    def body(*refs):
        pass

    anywhere = pl.BlockSpec(memory_space=pl.ANY)
    return pl.pallas_call(
        body,
        in_specs=[anywhere] * len(arrays),
        out_specs=[anywhere] * len(arrays),
        out_shape=[sds(x.shape, x.dtype) for x in arrays],
        input_output_aliases={k: k for k in range(len(arrays))},
    )(*arrays)


def whole(shape):
    return pl.BlockSpec(shape, lambda *_: (0,) * len(shape))


def sds(shape, dtype):
    return jax.ShapeDtypeStruct(shape, dtype)


def standard(x):
    centred = x - jnp.mean(x, axis=-1, keepdims=True)
    r = lax.rsqrt(jnp.mean(centred * centred, axis=-1, keepdims=True) + 1e-06)
    return centred * r, r


def fold(n, limit=512):
    return min(n, limit)


def qkv_forward(x, mods, w, bias, deps=()):
    n, d = x.shape
    wide = w.shape[1]
    mt = fold(n, QKV_ROWS)

    def body(x_ref, mod_ref, w_ref, b_ref, hid_ref, out_ref):
        m = pl.program_id(1)
        rows = pl.ds(pl.multiple_of(m * mt, mt), mt)

        @pl.when(pl.program_id(0) == 0)
        def _():
            v, _ = standard(x_ref[...].astype(F32))
            hid_ref[rows, :] = (v * (1.0 + mod_ref[1:2, :]) + mod_ref[0:1, :]).astype(BF16)

        out_ref[...] = (mm(hid_ref[rows, :], w_ref[...]) + b_ref[...]).astype(BF16)

    return call(
        body,
        (wide // d, n // mt),
        [
            pl.BlockSpec((mt, d), lambda j, m: (jnp.where(j == 0, m, n // mt - 1), 0)),
            whole((8, d)),
            pl.BlockSpec((d, d), lambda j, m: (0, j)),
            pl.BlockSpec((1, d), lambda j, m: (0, j)),
        ],
        [whole((n, d)), pl.BlockSpec((mt, d), lambda j, m: (m, j))],
        [sds((n, d), BF16), sds((n, wide), BF16)],
        flops=2 * n * d * wide,
        nbytes=2 * (d * wide + n * wide + 2 * n * d),
        deps=deps,
    )(x, mods, w, bias)


def window(h, size, d):
    lo = h * size
    start = lo // 128 * 128
    stop = min(-(-(lo + size) // 128) * 128, d)
    return start, stop, lo - start


def head_mask(start, stop, off, size, rows):
    lane = lax.broadcasted_iota(jnp.int32, (rows, stop - start), 1)
    return (lane >= off) & (lane < off + size)


def attention_forward(qkv, temporal, deps=()):
    a, g, p, wide = qkv.shape
    d = wide // 3
    size = d // HEADS
    t = a * p
    scale = size ** (-0.5)

    def body(qkv_ref, att_ref, lse_ref, peak_ref, acc):
        acc[...] = jnp.zeros_like(acc)
        if temporal:
            qi = lax.broadcasted_iota(jnp.int32, (t, t), 0)
            ki = lax.broadcasted_iota(jnp.int32, (t, t), 1)
            same = lax.rem(qi, p) == lax.rem(ki, p)
        tops, totals = [], []
        for h in range(HEADS):
            lo, hi, off = window(h, size, d)
            keep = head_mask(lo, hi, off, size, t)
            q = qkv_ref[:, 0, :, lo:hi].reshape(t, hi - lo)
            k = qkv_ref[:, 0, :, d + lo : d + hi].reshape(t, hi - lo)
            v = qkv_ref[:, 0, :, 2 * d + lo : 2 * d + hi].reshape(t, hi - lo)
            zero = jnp.zeros_like(q)
            s = mm(jnp.where(keep, q, zero), k, NT) * scale
            if temporal:
                s = jnp.where(same, s, -1e30)
            top = jnp.max(s, axis=-1, keepdims=True)
            e = jnp.exp(s - top)
            total = jnp.sum(e, axis=-1, keepdims=True)
            probs = (e / total).astype(BF16)
            acc[:, lo:hi] += mm(probs, jnp.where(keep, v, zero))
            tops.append(top)
            totals.append(total)
        top = jnp.concatenate(tops, axis=1)
        lse_ref[0] = (top + jnp.log(jnp.concatenate(totals, axis=1))).T
        peak_ref[...] = jnp.max(top, axis=0, keepdims=True)[None]
        att_ref[...] = acc[...].astype(BF16).reshape(a, 1, p, d)

    return call(
        body,
        (g,),
        [pl.BlockSpec((a, 1, p, wide), lambda i: (0, i, 0, 0))],
        [
            pl.BlockSpec((a, 1, p, d), lambda i: (0, i, 0, 0)),
            pl.BlockSpec((1, HEADS, t), lambda i: (i, 0, 0)),
            pl.BlockSpec((1, 1, HEADS), lambda i: (i, 0, 0)),
        ],
        [sds((a, g, p, d), BF16), sds((g, HEADS, t), F32), sds((g, 1, HEADS), F32)],
        [pltpu.VMEM((t, d), F32)],
        flops=4 * g * HEADS * t * t * 256,
        nbytes=2 * a * g * p * (wide + d),
        deps=deps,
    )(qkv)


def out_forward(att, x, mods, w, bias, deps=()):
    n, d = att.shape
    mt = fold(n, 256)

    def body(att_ref, x_ref, mod_ref, w_ref, b_ref, branch_ref, mid_ref, hid_ref):
        branch = mm(att_ref[...], w_ref[...]) + b_ref[...]
        branch_ref[...] = branch.astype(BF16)
        mid = x_ref[...].astype(F32) + mod_ref[2:3, :] * branch
        mid_ref[...] = mid
        v, _ = standard(mid)
        hid_ref[...] = (v * (1.0 + mod_ref[4:5, :]) + mod_ref[3:4, :]).astype(BF16)

    tile = pl.BlockSpec((mt, d), lambda m: (m, 0))
    return call(
        body,
        (n // mt,),
        [tile, tile, whole((8, d)), whole((d, d)), whole((1, d))],
        [tile, tile, tile],
        [sds((n, d), BF16), sds((n, d), F32), sds((n, d), BF16)],
        flops=2 * n * d * d,
        nbytes=2 * (d * d + 6 * n * d),
        deps=deps,
    )(att, x, mods, w, bias)


GELU_A = 0.7978845608028654
GELU_B = 0.044715


def up_forward(hid, w, bias, deps=()):
    n, d = hid.shape
    ff = w.shape[1]
    mt = fold(n, UP_ROWS)
    ft = d
    cuts = UP_CUTS

    def body(hid_ref, w_ref, b_ref, act_ref, slope_ref):
        for c in range(cuts):
            cols = slice(c * ft // cuts, (c + 1) * ft // cuts)
            u = mm(hid_ref[...], w_ref[:, cols]) + b_ref[:, cols]
            square = u * u
            tanh = jnp.tanh(u * (GELU_A + (GELU_A * GELU_B) * square))
            half = 0.5 + 0.5 * tanh
            act_ref[:, cols] = (u * half).astype(BF16)
            bend = GELU_A + (3.0 * GELU_A * GELU_B) * square
            slope_ref[:, cols] = (half + (u * half) * ((1.0 - tanh) * bend)).astype(BF16)

    tile = pl.BlockSpec((mt, ft), lambda f, m: (m, f))
    return call(
        body,
        (ff // ft, n // mt),
        [
            pl.BlockSpec((mt, d), lambda f, m: (m, 0)),
            pl.BlockSpec((d, ft), lambda f, m: (0, f)),
            pl.BlockSpec((1, ft), lambda f, m: (0, f)),
        ],
        [tile, tile],
        [sds((n, ff), BF16), sds((n, ff), BF16)],
        flops=2 * n * d * ff,
        nbytes=2 * (d * ff + 2 * n * ff + n * d),
        deps=deps,
    )(hid, w, bias)


def down_forward(act, mid, mods, w, bias, deps=()):
    n, ff = act.shape
    d = w.shape[1]
    mt = fold(n, 256)

    def body(act_ref, mid_ref, mod_ref, w_ref, b_ref, upd_ref, out_ref):
        upd = mm(act_ref[...], w_ref[...]) + b_ref[...]
        upd_ref[...] = upd.astype(BF16)
        out_ref[...] = (mid_ref[...] + mod_ref[5:6, :] * upd).astype(BF16)

    tile = pl.BlockSpec((mt, d), lambda m: (m, 0))
    return call(
        body,
        (n // mt,),
        [
            pl.BlockSpec((mt, ff), lambda m: (m, 0)),
            tile,
            whole((8, d)),
            whole((ff, d)),
            whole((1, d)),
        ],
        [tile, tile],
        [sds((n, d), BF16), sds((n, d), BF16)],
        flops=2 * n * d * ff,
        nbytes=2 * (d * ff + n * ff + 4 * n * d),
        deps=deps,
    )(act, mid, mods, w, bias)


def column_sum(v):
    return jnp.sum(v, axis=0, keepdims=True)


def update_back(go, mods, deps=()):
    n, d = go.shape
    mt = fold(n, 256)

    def body(go_ref, mod_ref, gu_ref, sum_ref):
        @pl.when(pl.program_id(0) == 0)
        def _():
            sum_ref[...] = jnp.zeros_like(sum_ref)

        low = (mod_ref[5:6, :] * go_ref[...].astype(F32)).astype(BF16)
        gu_ref[...] = low
        sum_ref[0:1, :] += column_sum(low.astype(F32))

    tile = pl.BlockSpec((mt, d), lambda m: (m, 0))
    return call(
        body,
        (n // mt,),
        [tile, whole((8, d))],
        [tile, whole((8, d))],
        [sds((n, d), BF16), sds((8, d), F32)],
        flops=n * d,
        nbytes=4 * n * d,
        deps=deps,
    )(go, mods)


def slot(k):
    return k % 2 * 2 + k // 2


def shed_specs(seq, zs, rows, d):
    return sds((seq, zs, rows, d), BF16)


def shares(start, stop, rows):
    found = []
    while start < stop:
        block = start // rows
        end = min(stop, (block + 1) * rows)
        found.append((block, start - block * rows, start, end))
        start = end
    return found


def down_grad(place, act, gu, seq, zs, deps=()):
    n, ff = act.shape
    d = gu.shape[1]
    rows, quarter = d // (2 * zs), d // seq
    parts = ff // (2 * zs) // rows
    cuts = 3

    def body(place_ref, act_ref, gu_ref, mine_ref, other_ref):
        def fill(targets):
            for c in range(cuts):
                first, stop = c * (ff // zs) // cuts, (c + 1) * (ff // zs) // cuts
                full = mm(act_ref[:, first:stop], gu_ref[...], TN).astype(BF16)
                for block, at, lo, hi in shares(first, stop, rows):
                    target, q = targets[block // parts], block % parts
                    for s in range(seq):
                        target[s, 0, at : at + hi - lo, q * quarter : (q + 1) * quarter] = full[
                            lo - first : hi - first, s * quarter : (s + 1) * quarter
                        ]

        @pl.when(place_ref[0] == 0)
        def _():
            fill((mine_ref, other_ref))

        @pl.when(place_ref[0] == 1)
        def _():
            fill((other_ref, mine_ref))

    piece = pl.BlockSpec((seq, 1, rows, d), lambda i, place_ref: (0, i, 0, 0))
    return call(
        body,
        (zs,),
        [
            pl.BlockSpec((n, ff // zs), lambda i, place_ref: (0, slot(i) ^ place_ref[1])),
            whole((n, d)),
        ],
        [piece, piece],
        [shed_specs(seq, zs, rows, d)] * 2,
        scalars=1,
        flops=2 * n * d * ff,
        nbytes=2 * (d * ff + n * ff + n * d),
        deps=deps,
    )(place, act, gu)


def up_grad(place, hid, gi, seq, zs, deps=()):
    n, d = hid.shape
    ff = gi.shape[1]
    rows, wide = d // (2 * zs), ff // seq
    cuts = 3

    def body(place_ref, hid_ref, gi_ref, mine_ref, other_ref):
        z = place_ref[1]

        def fill(targets):
            for c in range(cuts):
                first, stop = c * d // cuts, (c + 1) * d // cuts
                full = mm(hid_ref[:, first:stop], gi_ref[...], TN).astype(BF16)
                for block, at, lo, hi in shares(first, stop, rows):
                    targets[block % 2][0, slot((block // 2) ^ z), at : at + hi - lo, :] = full[
                        lo - first : hi - first
                    ]

        @pl.when(place_ref[0] == 0)
        def _():
            fill((mine_ref, other_ref))

        @pl.when(place_ref[0] == 1)
        def _():
            fill((other_ref, mine_ref))

    piece = pl.BlockSpec((1, zs, rows, wide), lambda i, place_ref: (i, 0, 0, 0))
    return call(
        body,
        (seq,),
        [whole((n, d)), pl.BlockSpec((n, wide), lambda i, place_ref: (0, i))],
        [piece, piece],
        [shed_specs(seq, zs, rows, wide)] * 2,
        scalars=1,
        flops=2 * n * d * ff,
        nbytes=2 * (d * ff + n * ff + n * d),
        deps=deps,
    )(place, hid, gi)


def qkv_out_grad(place, hid, att, gqkv, gb, zs, deps=()):
    n, d = hid.shape
    seq, _, wa = gqkv.shape
    wb = gb.shape[2]
    rows = d // (2 * zs)
    cuts = 3

    def body(place_ref, hid_ref, att_ref, gqkv_ref, gb_ref, mine_ref, other_ref):
        z = place_ref[1]

        def fill(targets):
            for c in range(cuts):
                first, stop = c * d // cuts, (c + 1) * d // cuts
                left = mm(hid_ref[:, first:stop], gqkv_ref[0], TN).astype(BF16)
                right = mm(att_ref[:, first:stop], gb_ref[0], TN).astype(BF16)
                full = jnp.concatenate([left, right], axis=1)
                for block, at, lo, hi in shares(first, stop, rows):
                    targets[block % 2][0, slot((block // 2) ^ z), at : at + hi - lo, :] = full[
                        lo - first : hi - first
                    ]

        @pl.when(place_ref[0] == 0)
        def _():
            fill((mine_ref, other_ref))

        @pl.when(place_ref[0] == 1)
        def _():
            fill((other_ref, mine_ref))

    piece = pl.BlockSpec((1, zs, rows, wa + wb), lambda i, place_ref: (i, 0, 0, 0))
    return call(
        body,
        (seq,),
        [
            whole((n, d)),
            whole((n, d)),
            pl.BlockSpec((1, n, wa), lambda i, place_ref: (i, 0, 0)),
            pl.BlockSpec((1, n, wb), lambda i, place_ref: (i, 0, 0)),
        ],
        [piece, piece],
        [shed_specs(seq, zs, rows, wa + wb)] * 2,
        scalars=1,
        flops=2 * n * d * seq * (wa + wb),
        nbytes=2 * seq * (d + n) * (wa + wb),
        deps=deps,
    )(place, hid, att, gqkv, gb)


def feed_back(gu, slope, w_down, w_up, deps=()):
    n, d = gu.shape
    ff = slope.shape[1]
    mt = fold(n, FEED_ROWS)
    last = ff // d - 1

    def body(gu_ref, slope_ref, wd_ref, wu_ref, gi_ref, bias_ref, out_ref, acc):
        f = pl.program_id(0)
        m = pl.program_id(1)
        rows = pl.ds(pl.multiple_of(m * mt, mt), mt)
        gi = (mm(gu_ref[...], wd_ref[...], NT) * slope_ref[...].astype(F32)).astype(BF16)
        gi_ref[...] = gi
        total = column_sum(gi.astype(F32))

        @pl.when(m == 0)
        def _():
            bias_ref[...] = total

        @pl.when(m > 0)
        def _():
            bias_ref[...] += total

        part = mm(gi, wu_ref[...], NT)

        @pl.when(f == 0)
        def _():
            acc[rows, :] = part

        @pl.when((f > 0) & (f < last))
        def _():
            acc[rows, :] += part

        @pl.when(f == last)
        def _():
            out_ref[...] = acc[rows, :] + part

    return call(
        body,
        (ff // d, n // mt),
        [
            pl.BlockSpec((mt, d), lambda f, m: (m, 0)),
            pl.BlockSpec((mt, d), lambda f, m: (m, f)),
            pl.BlockSpec((d, d), lambda f, m: (f, 0)),
            pl.BlockSpec((d, d), lambda f, m: (0, f)),
        ],
        [
            pl.BlockSpec((mt, d), lambda f, m: (m, f)),
            pl.BlockSpec((1, d), lambda f, m: (0, f)),
            pl.BlockSpec((mt, d), lambda f, m: (jnp.where(f == last, m, 0), 0)),
        ],
        [sds((n, ff), BF16), sds((1, ff), F32), sds((n, d), F32)],
        [pltpu.VMEM((n, d), F32)],
        flops=4 * n * d * ff,
        nbytes=2 * (2 * d * ff + 2 * n * ff + 3 * n * d),
        deps=deps,
    )(gu, slope, w_down, w_up)


def norm_back(grad, v, r, stretch):
    dn = grad * stretch
    return r * (
        dn - jnp.mean(dn, axis=-1, keepdims=True) - v * jnp.mean(dn * v, axis=-1, keepdims=True)
    )


def middle_back(gh, mid, branch, go, upd, mods, w, seq, deps=()):
    n, d = gh.shape
    mt = fold(n, 256)
    wide = d // seq

    def body(
        gh_ref, mid_ref, branch_ref, go_ref, upd_ref, mod_ref, w_ref,
        gmid_ref, gb_ref, cut_ref, ga_ref, sum_ref,
    ):
        @pl.when(pl.program_id(0) == 0)
        def _():
            sum_ref[...] = jnp.zeros_like(sum_ref)

        g = gh_ref[...]
        v, r = standard(mid_ref[...])
        sum_ref[0:1, :] += column_sum(g * v)
        sum_ref[1:2, :] += column_sum(g)
        go = go_ref[...].astype(F32)
        sum_ref[4:5, :] += column_sum(go * upd_ref[...].astype(F32))
        gmid = go + norm_back(g, v, r, 1.0 + mod_ref[4:5, :])
        gmid_ref[...] = gmid
        sum_ref[2:3, :] += column_sum(gmid * branch_ref[...].astype(F32))
        low = (mod_ref[2:3, :] * gmid).astype(BF16)
        gb_ref[...] = low
        for s in range(seq):
            cut_ref[s] = low[:, s * wide : (s + 1) * wide]
        sum_ref[3:4, :] += column_sum(low.astype(F32))
        ga_ref[...] = mm(low, w_ref[...], NT).astype(BF16)

    tile = pl.BlockSpec((mt, d), lambda m: (m, 0))
    return call(
        body,
        (n // mt,),
        [tile, tile, tile, tile, tile, whole((8, d)), whole((d, d))],
        [tile, tile, pl.BlockSpec((seq, mt, wide), lambda m: (0, m, 0)), tile, whole((8, d))],
        [
            sds((n, d), F32),
            sds((n, d), BF16),
            sds((seq, n, wide), BF16),
            sds((n, d), BF16),
            sds((8, d), F32),
        ],
        flops=2 * n * d * d,
        nbytes=2 * (d * d + 11 * n * d),
        deps=deps,
    )(gh, mid, branch, go, upd, mods, w)


def attention_back(qkv, ga, lse, temporal, seq, deps=()):
    a, g, p, wide = qkv.shape
    d = wide // 3
    size = d // HEADS
    t = a * p
    scale = size ** (-0.5)
    cut = wide // seq

    def body(qkv_ref, ga_ref, lse_ref, out_ref, cut_ref, sum_ref, acc):
        acc[...] = jnp.zeros_like(acc)
        if temporal:
            ki = lax.broadcasted_iota(jnp.int32, (t, t), 0)
            qi = lax.broadcasted_iota(jnp.int32, (t, t), 1)
            same = lax.rem(qi, p) == lax.rem(ki, p)
        for h in range(HEADS):
            lo, hi, off = window(h, size, d)
            keep = head_mask(lo, hi, off, size, t)
            q = qkv_ref[:, 0, :, lo:hi].reshape(t, hi - lo)
            k = qkv_ref[:, 0, :, d + lo : d + hi].reshape(t, hi - lo)
            v = qkv_ref[:, 0, :, 2 * d + lo : 2 * d + hi].reshape(t, hi - lo)
            o = ga_ref[:, 0, :, lo:hi].reshape(t, hi - lo)
            zero = jnp.zeros_like(q)
            q, o = jnp.where(keep, q, zero), jnp.where(keep, o, zero)
            s = mm(k, q, NT) * scale
            probs = jnp.exp(s - lse_ref[0, h : h + 1, :])
            if temporal:
                probs = jnp.where(same, probs, 0.0)
            dp = mm(v, o, NT)
            acc[:, 2 * d + lo : 2 * d + hi] += mm(probs.astype(BF16), o)
            ds = (probs * (dp - column_sum(probs * dp))).astype(BF16)
            acc[:, d + lo : d + hi] += mm(ds, q) * scale
            acc[:, lo:hi] += mm(ds, jnp.where(keep, k, zero), TN) * scale
        low = acc[...].astype(BF16)
        out_ref[...] = low.reshape(a, 1, p, wide)
        for s in range(seq):
            cut_ref[s] = low[:, s * cut : (s + 1) * cut].reshape(a, 1, p, cut)
        total = column_sum(low.astype(F32))

        @pl.when(pl.program_id(0) == 0)
        def _():
            sum_ref[...] = total

        @pl.when(pl.program_id(0) > 0)
        def _():
            sum_ref[...] += total

    return call(
        body,
        (g,),
        [
            pl.BlockSpec((a, 1, p, wide), lambda i: (0, i, 0, 0)),
            pl.BlockSpec((a, 1, p, d), lambda i: (0, i, 0, 0)),
            pl.BlockSpec((1, HEADS, t), lambda i: (i, 0, 0)),
        ],
        [
            pl.BlockSpec((a, 1, p, wide), lambda i: (0, i, 0, 0)),
            pl.BlockSpec((seq, a, 1, p, cut), lambda i: (0, 0, i, 0, 0)),
            whole((1, wide)),
        ],
        [sds((a, g, p, wide), BF16), sds((seq, a, g, p, cut), BF16), sds((1, wide), F32)],
        [pltpu.VMEM((t, wide), F32)],
        flops=12 * g * HEADS * t * t * 256,
        nbytes=2 * a * g * p * (3 * wide + d),
        deps=deps,
    )(qkv, ga, lse)


def stream_back(gqkv, w, x, gmid, mods, out_dtype, shape=None, deps=()):
    n, wide = gqkv.shape
    d = w.shape[0]
    mt = fold(n, 256) if shape is None else n // shape[0]

    def body(g_ref, w_ref, x_ref, gmid_ref, mod_ref, out_ref, sum_ref):
        @pl.when(pl.program_id(0) == 0)
        def _():
            sum_ref[...] = jnp.zeros_like(sum_ref)

        grad = mm(g_ref[...], w_ref[...], NT)
        v, r = standard(x_ref[...].astype(F32))
        sum_ref[0:1, :] += column_sum(grad * v)
        sum_ref[1:2, :] += column_sum(grad)
        out = gmid_ref[...] + norm_back(grad, v, r, 1.0 + mod_ref[1:2, :])
        out_ref[...] = out.astype(out_dtype).reshape(out_ref.shape)

    tile = pl.BlockSpec((mt, d), lambda m: (m, 0))
    result, block = sds((n, d), out_dtype), tile
    if shape is not None:
        parts, frames, places = shape
        result = sds((frames, parts, places, d), out_dtype)
        block = pl.BlockSpec((frames, 1, places, d), lambda m: (0, m, 0, 0))
    return call(
        body,
        (n // mt,),
        [
            pl.BlockSpec((mt, wide), lambda m: (m, 0)),
            whole((d, wide)),
            tile,
            tile,
            whole((8, d)),
        ],
        [block, whole((8, d))],
        [result, sds((8, d), F32)],
        flops=2 * n * d * wide,
        nbytes=2 * (d * wide + n * wide + 5 * n * d),
        deps=deps,
    )(gqkv, w, x, gmid, mods)


def collect(sums, deps=()):
    flat = [item for layer in sums for item in layer]
    d = flat[0].shape[1]
    ups = flat[4].shape[1] // d
    each = 4 + ups

    def body(*refs):
        mod_ref, bias_ref = refs[len(flat) :]
        for k in range(len(sums)):
            stream, middle, update, qkv, up = refs[5 * k : 5 * k + 5]
            rows = (
                (stream, 1), (stream, 0), (middle, 2), (middle, 1), (middle, 0), (middle, 4)
            )
            for r, (ref, at) in enumerate(rows):
                mod_ref[6 * k + r : 6 * k + r + 1, :] = ref[at : at + 1, :]
            base = each * k
            bias_ref[base : base + 1, :] = qkv[:, :d]
            bias_ref[base + 1 : base + 2, :] = qkv[:, 2 * d :]
            bias_ref[base + 2 : base + 3, :] = middle[3:4, :]
            bias_ref[base + 3 : base + 4, :] = update[0:1, :]
            for u in range(ups):
                bias_ref[base + 4 + u : base + 5 + u, :] = up[:, u * d : (u + 1) * d]

    shapes = [(6 * len(sums), d), (each * len(sums), d)]
    return call(
        body,
        (1,),
        [whole(item.shape) for item in flat],
        [whole(shape) for shape in shapes],
        [sds(shape, F32) for shape in shapes],
        deps=deps,
    )(*flat)


def laid_out(pairs):
    count = len(pairs)
    flat = [item for pair in pairs for item in pair]
    _, half, rows, d = flat[0].shape

    def body(*refs):
        for k in range(count):
            refs[-1][k, 0, :half] = refs[2 * k][0]
            refs[-1][k, 0, half:] = refs[2 * k + 1][0]

    return call(
        body,
        (1,),
        [whole(item.shape) for item in flat],
        whole((count, 1, 2 * half, rows, d)),
        sds((count, 1, 2 * half, rows, d), BF16),
        nbytes=8 * count * half * rows * d,
    )(*flat)


def add_pieces(left, right, deps=()):
    seq, zs, rows, d = left.shape

    def body(left_ref, right_ref, out_ref):
        out_ref[...] = (left_ref[...].astype(F32) + right_ref[...].astype(F32)).astype(BF16)

    piece = pl.BlockSpec((1, zs, rows, d), lambda i: (i, 0, 0, 0))
    return call(
        body,
        (seq,),
        [piece, piece],
        piece,
        sds(left.shape, BF16),
        nbytes=6 * seq * zs * rows * d,
        deps=deps,
    )(left, right)


def join_qkv_out(place, own, got, which, deps=()):
    seq, _, zs, rows, d = own.shape
    wide = d * 3 // 4

    def body(place_ref, own_ref, got_ref, qkv_ref, out_ref):
        def put(c, src):
            span = slice(c * rows, (c + 1) * rows)
            qkv_ref[span, :] = jnp.concatenate([src[s ^ place_ref[2], 0, 0, :, :wide] for s in range(seq)], axis=1)
            out_ref[span, :] = jnp.concatenate([src[s ^ place_ref[2], 0, 0, :, wide:] for s in range(seq)], axis=1)

        for c in range(2):

            @pl.when(place_ref[0] == c)
            def _(c=c):
                put(c, own_ref)
                put(1 - c, got_ref)

    piece = pl.BlockSpec(
        (seq, 1, 1, rows, d), lambda i, place_ref: (0, which, slot(i ^ place_ref[1]), 0, 0)
    )
    return call(
        body,
        (zs,),
        [piece, piece],
        [
            pl.BlockSpec((2 * rows, seq * wide), lambda i, place_ref: (i, 0)),
            pl.BlockSpec((2 * rows, d), lambda i, place_ref: (i, 0)),
        ],
        [sds((2 * rows * zs, seq * wide), BF16), sds((2 * rows * zs, d), BF16)],
        scalars=1,
        nbytes=8 * seq * zs * rows * d,
        deps=deps,
    )(place, own, got)


def join_up(place, own, got, which, deps=()):
    seq, _, zs, rows, d = own.shape

    def body(place_ref, own_ref, got_ref, up_ref):
        for c in range(2):

            @pl.when(place_ref[0] == c)
            def _(c=c):
                for s in range(seq):
                    cols = slice(s * d, (s + 1) * d)
                    up_ref[c * rows : (c + 1) * rows, cols] = own_ref[s ^ place_ref[2], 0, 0]
                    up_ref[(1 - c) * rows : (2 - c) * rows, cols] = got_ref[s ^ place_ref[2], 0, 0]

    piece = pl.BlockSpec(
        (seq, 1, 1, rows, d), lambda i, place_ref: (0, which, slot(i ^ place_ref[1]), 0, 0)
    )
    return call(
        body,
        (zs,),
        [piece, piece],
        pl.BlockSpec((2 * rows, seq * d), lambda i, place_ref: (i, 0)),
        sds((2 * rows * zs, seq * d), BF16),
        scalars=1,
        nbytes=8 * seq * zs * rows * d,
        deps=deps,
    )(place, own, got)


def join_down(place, own, got, which, deps=()):
    seq, _, zs, rows, d = own.shape
    quarter = d // seq
    parts = d // quarter

    def body(place_ref, own_ref, got_ref, down_ref):
        def put(c, src):
            for q in range(parts):
                base = (c * parts + q) * rows
                cols = slice(q * quarter, (q + 1) * quarter)
                down_ref[base : base + rows, :] = jnp.concatenate(
                    [src[s ^ place_ref[2], 0, 0, :, cols] for s in range(seq)], axis=1
                )

        for c in range(2):

            @pl.when(place_ref[0] == c)
            def _(c=c):
                put(c, own_ref)
                put(1 - c, got_ref)

    piece = pl.BlockSpec(
        (seq, 1, 1, rows, d), lambda i, place_ref: (0, which, slot(i ^ place_ref[1]), 0, 0)
    )
    return call(
        body,
        (zs,),
        [piece, piece],
        pl.BlockSpec((2 * parts * rows, d), lambda i, place_ref: (i, 0)),
        sds((2 * parts * rows * zs, d), BF16),
        scalars=1,
        nbytes=8 * seq * zs * rows * d,
        deps=deps,
    )(place, own, got)


clip_limit = 8.0
CLIP = ("z", "core")


def hop(x, distance, count):
    return lax.ppermute(x, CLIP, [(i, i ^ distance) for i in range(count)])


def on_device(
    video_latents,
    conditioning,
    ada_weight,
    ada_bias,
    qkv_weight,
    out_weight,
    up_weight,
    down_weight,
    attention_bias,
    up_bias,
    down_bias,
    cotangent,
    *,
    clips,
    seq,
):
    zs = clips // 2
    layers, rows, own_columns = qkv_weight.shape
    d = video_latents.shape[-1]
    frames, places = video_latents.shape[1:3]
    n = frames * places
    ff = up_bias.shape[1]
    clip_index = lax.axis_index(CLIP)
    seq_index = lax.axis_index("seq")
    place = jnp.stack([clip_index % 2, clip_index // 2, 0 * seq_index]).astype(jnp.int32)
    packed = zs == 4 and seq == 4 and rows % 16 == 0 and down_weight.shape[1] % rows == 0 and d % seq == 0
    cuts = seq if packed else 1

    def total(v, *axes):
        for axis, count in axes:
            step = 1
            while step < count:
                v = v + lax.ppermute(v, axis, [(i, i ^ step) for i in range(count)])
                step *= 2
        return v

    def modulate(first, second):
        own_place = (clip_index, jnp.zeros_like(clip_index))
        placed = lax.dynamic_update_slice(jnp.zeros((clips, d), F32), conditioning, own_place)
        if first:
            placed = gate(placed, first)
        squashed = jax.nn.silu(total(placed, (CLIP, clips))).astype(BF16)
        local_mods = (
            jnp.einsum("kd,ldc->klc", squashed, ada_weight, preferred_element_type=F32)
            + ada_bias[None, :, :]
        )
        if second:
            local_mods = gate(local_mods, second)
        own_mods = lax.all_to_all(local_mods, CLIP, 0, 0, tiled=True)
        every_mod = lax.all_gather(own_mods, "seq", axis=0, tiled=False)
        modulation = every_mod.transpose(2, 1, 0, 3).reshape(layers, 6, d)
        return squashed, jnp.pad(modulation, ((0, 0), (0, 2), (0, 0)))

    def far(block):
        return hop(block, 4, clips)

    def near(block):
        return hop(block, 2, clips)

    def put(*parts):
        return jnp.concatenate(parts, axis=1)

    def pack_rows(layer):
        tall = down_weight[layer].reshape(-1, rows, d // seq)
        return (
            jnp.concatenate([qkv_weight[layer], out_weight[layer]], axis=1),
            up_weight[layer],
            tall.transpose(1, 0, 2).reshape(rows, d),
        )

    def along_seq(blocks):
        return lax.all_gather(blocks, "seq", axis=0, tiled=False)

    def both_cores(own, deps):
        own = gate(own, deps)
        return own, hop(own, 1, clips)

    def fetch_natural(layer):
        return tuple(
            lax.all_gather(
                lax.all_gather(item[layer], CLIP, axis=0, tiled=True), "seq", axis=1, tiled=True
            )
            for item in (qkv_weight, out_weight, up_weight, down_weight)
        )

    def reduce_seq(half):
        flat = lax.psum_scatter(half.reshape(-1, d), "seq", scatter_dimension=0, tiled=True)
        return flat.reshape(zs, rows, d)

    def first_half(part):
        return hop(part[2:], 2, clips)

    def add_first(part, got):
        return (part[:2].astype(F32) + got.astype(F32)).astype(BF16)

    def second_half(part):
        return hop(part[1], 4, clips)

    def add_second(part, got):
        return part[0].astype(F32) + got.astype(F32)

    def shed_natural(left, right):
        full = mm(left, right, TN).astype(BF16)
        part = lax.psum_scatter(full, "seq", scatter_dimension=1, tiled=True)
        return lax.psum_scatter(part, CLIP, scatter_dimension=0, tiled=True).astype(F32)

    def swap_tokens(x):
        block = x.reshape(seq, n // seq, d)
        return lax.all_to_all(block, "seq", 0, 0, tiled=True).reshape(n, d)

    def by_places(x):
        return x.reshape(frames, seq, places // seq, d).transpose(1, 0, 2, 3).reshape(n, d)

    def by_frames(x):
        return (
            x.reshape(seq, frames, places // seq, d)
            .transpose(1, 0, 2, 3)
            .reshape(1, frames, places, d)
        )

    shapes = (
        (seq, frames, places // seq),
        (seq * frames, places // seq // 16, 16),
    )

    def qkv_bias_of(layer):
        bias = attention_bias[layer]
        return jnp.concatenate([bias[0], jnp.zeros_like(bias[0]), bias[1]])[None]

    def forward_natural(layer, x, modulation):
        mods = modulation[layer]
        qkv_full, out_full, up_full, down_full = fetch_natural(layer)
        hidden, qkv = qkv_forward(x, mods, qkv_full, qkv_bias_of(layer))
        qkv = qkv.reshape(shapes[layer] + (3 * d,))
        attended, lse, peak = attention_forward(qkv, layer == 1)
        attended = attended.reshape(n, d)
        out_bias = attention_bias[layer, 2:3]
        branch, middle, hidden_two = out_forward(attended, x, mods, out_full, out_bias)
        active, slope = up_forward(hidden_two, up_full, up_bias[layer : layer + 1])
        update, result = down_forward(
            active, middle, mods, down_full, down_bias[layer : layer + 1]
        )
        kept = (x, hidden, qkv, lse, attended, branch, middle, hidden_two, active, slope, update)
        weights = (qkv_full, out_full, up_full, down_full)
        return result, kept, weights, jnp.max(peak, axis=(0, 1))

    def backward_natural(layer, grad_out, kept, weights, modulation):
        x, hidden, qkv, lse, attended, branch, middle, hidden_two, active, slope, update = kept
        qkv_full, out_full, up_full, down_full = weights
        mods = modulation[layer]
        grad_update, update_sums = update_back(grad_out, mods)
        inner_grad, up_sums, hidden_grad = feed_back(grad_update, slope, down_full, up_full)
        middle_grad, branch_grad, _, attended_grad, middle_sums = middle_back(
            hidden_grad, middle, branch, grad_out, update, mods, out_full, 1
        )
        qkv_grad, _, qkv_sums = attention_back(
            qkv, attended_grad.reshape(shapes[layer] + (d,)), lse, layer == 1, 1
        )
        qkv_grad = qkv_grad.reshape(n, 3 * d)
        stream_grad, stream_sums = stream_back(
            qkv_grad, qkv_full, x, middle_grad, mods, BF16 if layer == 1 else F32
        )
        parts = (
            shed_natural(hidden, qkv_grad),
            shed_natural(attended, branch_grad),
            shed_natural(hidden_two, inner_grad),
            shed_natural(active, grad_update),
        )
        if layer == 0:
            stream_grad = by_frames(stream_grad)
        return stream_grad, (stream_sums, middle_sums, update_sums, qkv_sums, up_sums), parts

    def unpack(parts):
        down_g, up_g, both = parts
        down_g = down_g.reshape(rows, -1, d // seq).transpose(1, 0, 2).reshape(-1, d // seq)
        return both[:, :own_columns], both[:, own_columns:], up_g, down_g

    def run_natural():
        squashed, modulation = modulate((), ())
        first_in = by_places(video_latents)
        second_go = swap_tokens(by_places(cotangent))
        first_out, first_kept, first_weights, first_peak = forward_natural(0, first_in, modulation)
        second_in = swap_tokens(first_out)
        second_out, second_kept, second_weights, second_peak = forward_natural(1, second_in, modulation)
        second_grad, second_sums, second_parts = backward_natural(
            1, second_go, second_kept, second_weights, modulation
        )
        first_grad, first_sums, first_parts = backward_natural(
            0, swap_tokens(second_grad), first_kept, first_weights, modulation
        )
        peaks = (first_peak, second_peak)
        sums = (first_sums, second_sums)
        second_out = swap_tokens(second_out)

        def finish(small, own_mod_grad, exchanged):
            return total(small, (CLIP, clips), ("seq", seq)), first_parts, second_parts

        return squashed, second_out, first_grad, peaks, collect(sums), finish

    def run_packed():
        first_pack, second_pack = pack_rows(0), pack_rows(1)
        first_in = by_places(video_latents)
        second_go = swap_tokens(by_places(cotangent))

        block = first_pack[0][None, None]
        pair = put(block, far(block))
        squashed, modulation = modulate((), ())
        line_q0 = put(pair, gate(near(pair), (second_go,)))
        block = gate(first_pack[1][None, None], (line_q0,))
        pair = put(block, far(block))
        line_u0 = put(pair, gate(near(pair), (modulation,)))
        block = gate(first_pack[2][None, None], (line_u0,))
        pair_d0 = put(block, far(block))
        whole_q0 = along_seq(line_q0)
        whole_u0 = along_seq(line_u0)

        def attention_part(layer, x, qkv, out_full):
            qkv = qkv.reshape(shapes[layer] + (3 * d,))
            attended, lse, peak = attention_forward(qkv, layer == 1)
            return qkv, attended.reshape(n, d), lse, jnp.max(peak, axis=(0, 1))

        mods = modulation[0]
        qkv_full, out_full = join_qkv_out(place, *both_cores(whole_q0, (pair_d0,)), 0)
        hidden, qkv = qkv_forward(first_in, mods, qkv_full, qkv_bias_of(0))
        hidden, qkv, got = joint(hidden, qkv, near(pair_d0))
        line_d0 = put(pair_d0, got)
        block_q1 = gate(second_pack[0][None, None], (got,))
        qkv, attended, lse, peak0 = attention_part(0, first_in, qkv, out_full)
        attended, lse, got = joint(attended, lse, far(block_q1))
        pair_q1 = put(block_q1, got)
        branch, middle, hidden_two = out_forward(
            attended, first_in, mods, out_full, attention_bias[0, 2:3]
        )
        branch, middle, hidden_two, got = joint(branch, middle, hidden_two, near(pair_q1))
        line_q1 = put(pair_q1, got)
        whole_dq = along_seq(jnp.concatenate([line_d0, line_q1], axis=0))
        block_f1 = gate(jnp.stack(second_pack[1:])[:, None], (got,))
        up_full = join_up(place, *both_cores(whole_u0, (branch,)), 0, deps=(line_q1, line_d0))
        active, slope = up_forward(hidden_two, up_full, up_bias[:1])
        active, slope, got = joint(active, slope, far(block_f1))
        pair_f1 = put(block_f1, got)
        own_dq, got_dq = both_cores(whole_dq, (active,))
        down_full = join_down(place, own_dq, got_dq, 0, deps=(pair_f1,))
        update, result = down_forward(active, middle, mods, down_full, down_bias[:1])
        update, result, got = joint(update, result, near(pair_f1))
        line_f1 = put(pair_f1, got)
        whole_u1, whole_d1 = along_seq(line_f1[:1]), along_seq(line_f1[1:])
        kept0 = (
            first_in, hidden, qkv, lse, attended, branch, middle, hidden_two, active, slope, update
        )
        weights0 = (qkv_full, out_full, up_full, down_full)
        second_in = swap_tokens(result)

        mods = modulation[1]
        qkv_full, out_full = join_qkv_out(place, own_dq, got_dq, 1, deps=(result, line_f1))
        hidden, qkv = qkv_forward(second_in, mods, qkv_full, qkv_bias_of(1))
        qkv, attended, lse, peak1 = attention_part(1, second_in, qkv, out_full)
        branch, middle, hidden_two = out_forward(
            attended, second_in, mods, out_full, attention_bias[1, 2:3]
        )
        own, got = both_cores(whole_u1, (attended,))
        branch, middle, hidden_two, got = joint(branch, middle, hidden_two, got)
        up_full = join_up(place, own, got, 0)
        active, slope = up_forward(hidden_two, up_full, up_bias[1:2])
        grad_update, update_sums1 = update_back(second_go, mods, deps=(active,))
        down_m, down_o = down_grad(place, active, grad_update, seq, zs)
        own, got = both_cores(whole_d1, (down_m,))
        half_d1 = add_pieces(down_m, hop(down_o, 1, clips), deps=(own,))
        half_d1, got = joint(half_d1, got)
        part_d1 = reduce_seq(half_d1)
        down_full = join_down(place, own, got, 0)
        update, result = down_forward(
            active, middle, mods, down_full, down_bias[1:2], deps=(half_d1,)
        )
        kept1 = (
            second_in, hidden, qkv, lse, attended, branch, middle, hidden_two, active, slope, update
        )
        weights1 = (qkv_full, out_full, up_full, down_full)
        kept, weights = (kept0, kept1), (weights0, weights1)

        def up_stage(layer, hidden_grad, inner_grad, grad_out, deps):
            _, _, _, _, _, branch, middle, hidden_two, _, _, update = kept[layer]
            up_m, up_o = up_grad(place, hidden_two, inner_grad, seq, zs, deps=deps)
            middle_grad, _, branch_cut, attended_grad, middle_sums = middle_back(
                hidden_grad, middle, branch, grad_out, update, modulation[layer],
                weights[layer][1], cuts, deps=(up_m,),
            )
            half_u = add_pieces(up_m, hop(up_o, 1, clips), deps=(middle_grad,))
            return half_u, reduce_seq(half_u), middle_grad, branch_cut, attended_grad, middle_sums

        def attention_stage(layer, attended_grad, deps):
            _, _, qkv, lse = kept[layer][:4]
            grad = attended_grad.reshape(shapes[layer] + (d,))
            qkv_grad, qkv_cut, qkv_sums = attention_back(
                qkv, grad, lse, layer == 1, cuts, deps=deps
            )
            return qkv_grad.reshape(n, 3 * d), qkv_cut.reshape(seq, n, -1), qkv_sums

        def last_grad(layer, qkv_cut, branch_cut, deps):
            hidden, attended = kept[layer][1], kept[layer][4]
            return qkv_out_grad(place, hidden, attended, qkv_cut, branch_cut, zs, deps=deps)

        inner_grad, up_sums, hidden_grad = feed_back(
            grad_update, kept1[9], weights1[3], weights1[2], deps=(result,)
        )
        inner_grad, hidden_grad, second_out = joint(inner_grad, hidden_grad, swap_tokens(result))
        half_u, part_u1, middle_grad, branch_cut, attended_grad, middle_sums = up_stage(
            1, hidden_grad, inner_grad, second_go, ()
        )
        qkv_grad, qkv_cut, qkv_sums = attention_stage(1, attended_grad, (half_u, part_d1))
        qkv_grad, qkv_cut, got = joint(qkv_grad, qkv_cut, first_half(part_d1))
        sum_d1 = add_first(part_d1, got)
        stream_grad, stream_sums = stream_back(
            qkv_grad, weights1[0], kept1[0], middle_grad, modulation[1], BF16
        )
        stream_grad, stream_sums, got = joint(stream_grad, stream_sums, second_half(sum_d1))
        down_g1 = add_second(sum_d1, got)
        second_sums = (stream_sums, middle_sums, update_sums1, qkv_sums, up_sums)
        last_m, last_o = last_grad(1, qkv_cut, branch_cut, (stream_grad,))
        last_m, last_o, first_go = joint(last_m, last_o, swap_tokens(stream_grad))

        grad_update, update_sums = update_back(first_go, modulation[0])
        half_q1 = add_pieces(last_m, hop(last_o, 1, clips), deps=(grad_update,))
        part_q1 = reduce_seq(half_q1)
        down_m, down_o = down_grad(place, kept0[8], grad_update, seq, zs, deps=(half_q1,))
        inner_grad, up_sums, hidden_grad = feed_back(
            grad_update, kept0[9], weights0[3], weights0[2], deps=(down_m, part_u1)
        )
        inner_grad, hidden_grad, got = joint(inner_grad, hidden_grad, first_half(part_u1))
        sum_u1 = add_first(part_u1, got)
        half_d0 = add_pieces(down_m, hop(down_o, 1, clips), deps=(hidden_grad, part_q1))
        part_d0 = reduce_seq(half_d0)
        half_u, part_u0, middle_grad, branch_cut, attended_grad, middle_sums = up_stage(
            0, hidden_grad, inner_grad, first_go, (half_d0, sum_u1)
        )
        qkv_grad, qkv_cut, qkv_sums = attention_stage(0, attended_grad, (half_u,))
        qkv_grad, qkv_cut, got, got2 = joint(
            qkv_grad, qkv_cut, first_half(part_q1), second_half(sum_u1)
        )
        sum_q1 = add_first(part_q1, got)
        up_g1 = add_second(sum_u1, got2)
        last_m, last_o = last_grad(0, qkv_cut, branch_cut, (part_d0, sum_q1))
        last_m, last_o, got, got2 = joint(last_m, last_o, first_half(part_d0), second_half(sum_q1))
        sum_d0 = add_first(part_d0, got)
        both_g1 = add_second(sum_q1, got2)
        first_grad, stream_sums = stream_back(
            qkv_grad, weights0[0], kept0[0], middle_grad, modulation[0], F32, shape=shapes[0],
            deps=(last_m, sum_d0),
        )
        first_grad, stream_sums, got = joint(first_grad, stream_sums, second_half(sum_d0))
        down_g0 = add_second(sum_d0, got)
        first_sums = (stream_sums, middle_sums, update_sums, qkv_sums, up_sums)
        half = add_pieces(last_m, hop(last_o, 1, clips), deps=(first_grad,))
        part_q0 = reduce_seq(half)
        rows_of = collect((first_sums, second_sums), deps=(half,))

        def finish(small, own_mod_grad, exchanged):
            sum_u0 = add_first(part_u0, exchanged)
            up_g0 = add_second(sum_u0, second_half(sum_u0))
            sum_q0 = add_first(part_q0, first_half(part_q0))
            both_g0 = add_second(sum_q0, second_half(sum_q0))
            early = [gate(item, (own_mod_grad,)) for item in (down_g1, up_g1, both_g1, down_g0)]
            small = total(small, (CLIP, clips), ("seq", seq))
            return small, unpack((early[3], up_g0, both_g0)), unpack(early[:3])

        finish.exchange = lambda: first_half(part_u0)
        return squashed, second_out, first_grad, (peak0, peak1), rows_of, finish

    run = run_packed if packed else run_natural
    squashed, second_out, latents_grad, peaks, (mod_grads, bias_rows), finish = run()
    output_latents = by_frames(second_out)

    mod_grads = total(mod_grads, ("seq", seq)).reshape(layers, clips, seq, -1)
    of_columns = lax.dynamic_index_in_dim(mod_grads, lax.axis_index("seq"), 2, keepdims=False)
    own_mod_grad = lax.all_to_all(of_columns.transpose(1, 0, 2), CLIP, 0, 0, tiled=True)
    exchanged = None
    if packed:
        own_mod_grad, exchanged = joint(own_mod_grad, finish.exchange())
    ada_bias_grad = jnp.sum(own_mod_grad, axis=0)
    rounded_mod = own_mod_grad.astype(BF16)
    ada_weight_grad = jnp.einsum("kd,klc->ldc", squashed, rounded_mod, preferred_element_type=F32)
    squash_part = jnp.einsum("klc,ldc->kd", rounded_mod, ada_weight, preferred_element_type=F32)
    bias_count = bias_rows.shape[0]
    devices = clips * seq
    device = clip_index * seq + lax.axis_index("seq")
    peak_rows = -(-devices * layers * HEADS // d)
    own_peaks = jnp.concatenate(peaks)[None]
    placed = lax.dynamic_update_slice(
        jnp.zeros((devices, layers * HEADS), F32), own_peaks, (device, 0)
    ).reshape(-1)
    placed = jnp.pad(placed, (0, peak_rows * d - placed.shape[0])).reshape(peak_rows, d)
    summed, first_shed, second_shed = finish(
        jnp.concatenate([bias_rows, squash_part, placed], axis=0), own_mod_grad, exchanged
    )
    bias_sums = summed[:bias_count].reshape(layers, -1, d)
    own_squash = lax.dynamic_slice_in_dim(summed, bias_count + clip_index, 1, axis=0)
    peaks = summed[bias_count + clips :].reshape(-1)[: devices * layers * HEADS]
    logit_peak = jnp.max(peaks.reshape(devices, layers, HEADS), axis=0)
    column_index = lax.axis_index("seq") * own_columns + jnp.arange(own_columns, dtype=jnp.int32)
    head_of = column_index % d // (d // HEADS)
    head_match = (head_of[:, None] == jnp.arange(HEADS, dtype=jnp.int32)[None, :]).astype(F32)
    roots = jnp.sqrt(clip_limit / jnp.maximum(logit_peak, clip_limit))
    column_roots = jnp.sum(roots[:, None, :] * head_match[None, :, :], axis=-1)
    column_scale = jnp.where(column_index[None, :] < 2 * d, column_roots, 1.0)
    clipped_qkv = qkv_weight.astype(F32) * column_scale[:, None, :]
    silu_value, silu_pull = jax.vjp(jax.nn.silu, conditioning)
    conditioning_grad = silu_pull(own_squash)[0]
    return (
        output_latents,
        latents_grad.reshape(1, frames, places, d),
        conditioning_grad,
        ada_weight_grad,
        ada_bias_grad,
        jnp.stack([first_shed[0], second_shed[0]]),
        jnp.stack([first_shed[1], second_shed[1]]),
        jnp.stack([first_shed[2], second_shed[2]]),
        jnp.stack([first_shed[3], second_shed[3]]),
        bias_sums[:, :3],
        bias_sums[:, 4:].reshape(layers, ff),
        bias_sums[:, 3],
        clipped_qkv,
        logit_peak,
    )


def solution(mesh):
    clips, seq = mesh.shape["clip"], mesh.shape["seq"]
    finer = jax.sharding.Mesh(
        mesh.devices.reshape(clips // 2, 2, seq), ("z", "core", "seq")
    )
    every = (*CLIP, "seq")
    tokens = P(CLIP, "seq", None, None)
    matrix = P(None, CLIP, "seq")
    return jax.shard_map(
        partial(on_device, clips=clips, seq=seq),
        mesh=finer,
        in_specs=(
            tokens,
            P(CLIP, None),
            P(None, None, every),
            P(None, every),
            matrix,
            matrix,
            matrix,
            matrix,
            P(),
            P(),
            P(),
            tokens,
        ),
        out_specs=(
            tokens,
            tokens,
            P(CLIP, None),
            P(None, None, every),
            P(None, every),
            matrix,
            matrix,
            matrix,
            matrix,
            P(),
            P(),
            P(),
            matrix,
            P(),
        ),
        check_vma=False,
    )
```
